128 devices in a mesh: grp: 4 (over y_lo, core), dev: 32 (over z, y_hi, x).
Axes of the slice: x: 4, y: 4 (y_hi: 2, y_lo: 2; y = y_hi * 2 + y_lo), z: 4, core: 2. Of those that a mesh axis runs over, the one named last changes fastest.
Arguments:
- tokens: bfloat16 [1536, 4096], P(None, 'dev'), may hold values from -30 to 30
- in_weight: bfloat16 [4096, 16384], P(None, 'dev'), may hold values from -0.09375 to 0.09375
- upstream: bfloat16 [1536, 16384], P(None, 'dev'), may hold values from -30 to 30
- slot_block: int32 [256], P('dev'), may hold values from 0 to 255, as said below
- refreshed: int32 [32], replicated, may hold values from 0 to 255, as said below
- statistics: bfloat16 [256, 2, 512, 512], P('dev'), may hold values from -60 to 90, as said below
- roots: bfloat16 [256, 2, 512, 512], P('dev'), may hold values from 0 to 8, as said below
Outputs:
- update: bfloat16 [256, 512, 512], P('dev', 'grp')
The draws below stay inside these ranges and needn't reach their ends.
Inputs may be any that keep to these rules, and one draw needn't show every extreme that they name: `slot_block`: a permutation of the 256 block ids; slot s belongs to owner s // 8. `refreshed`: 32 distinct block ids; at most 2 of them are held in the slots of one owner, and some owner holds exactly 2. `statistics`: each [512, 512] matrix is symmetric. `roots`: each [512, 512] matrix is symmetric.
All inputs are finite; a program needn't handle non-finite values.
Results may differ from the reference program's by a relative error of at most 0.02.
Values may be sent and summed in bfloat16 or wider, within the bound.
No kernel may reach another device: no remote copies, remote signals or barrier semaphores. Data moves between devices by JAX's collectives and lax.ppermute only.
A program may use at most 128 MiB of HBM per device.

```python
import math
import jax
import jax.numpy as jnp
from jax import lax

D = 4096
BLOCK = 512
TG = 512
ITERS = 3
MOSTR = 2
RB = 8
COLS = 32
F = 16384
NB = 256
NR = 32
TRAIN = 3
TOKENS = 1536


def column_field(noise, scale_key, columns, low, high):
    scales = jnp.exp(jax.random.uniform(scale_key, (columns,), jnp.float32, math.log(low), math.log(high)))
    return noise * scales[None, :]


def kernel_blocks(key, count, order, spread, low, high, kernel_weight, width_scale):
    place_key, scale_key, extra_key = jax.random.split(key, 3)
    places = jax.random.uniform(place_key, (count, order), jnp.float32, 0.0, spread)
    scales = jnp.exp(jax.random.uniform(scale_key, (count, order), jnp.float32, math.log(low), math.log(high)))
    extra = jax.random.uniform(extra_key, (count, order), jnp.float32, 0.5, 1.5)
    distance = jnp.abs(places[:, :, None] - places[:, None, :])
    kernel = kernel_weight * jnp.exp(-distance * width_scale)
    kernel = kernel + jnp.eye(order, dtype=jnp.float32)[None, :, :] * extra[:, :, None]
    return jnp.sqrt(scales[:, :, None] * scales[:, None, :]) * kernel


def shared_directions(key):
    base = jax.random.fold_in(key, 105)
    loading_key, feature_key, unit_key = jax.random.split(base, 3)
    loading = jnp.clip(jax.random.normal(loading_key, (TOKENS,), jnp.float32), -3.0, 3.0)
    feature_trend = jnp.clip(jax.random.normal(feature_key, (D,), jnp.float32), -3.0, 3.0)
    unit_trend = jnp.clip(jax.random.normal(unit_key, (F,), jnp.float32), -3.0, 3.0)
    return (loading, feature_trend, unit_trend)


def place_value(table, slot, value):
    where_now = jnp.sum(jnp.where(table == value, jnp.arange(NB, dtype=jnp.int32), 0)).astype(jnp.int32)
    table = table.at[where_now].set(table[slot])
    return table.at[slot].set(value).astype(jnp.int32)


def ownership(key):
    table = jax.random.permutation(jax.random.fold_in(key, 101), NB).astype(jnp.int32)
    owners = NB // RB
    order = jax.random.permutation(jax.random.fold_in(key, 102), owners)
    heavy = NR // 4
    light = NR - MOSTR * heavy
    ranking = jnp.arange(owners, dtype=jnp.int32)
    by_rank = jnp.where(ranking < heavy, MOSTR, jnp.where(ranking < heavy + light, 1, 0)).astype(jnp.int32)
    counts = jnp.zeros((owners,), jnp.int32).at[order].set(by_rank)
    owner_keys = jax.random.split(jax.random.fold_in(key, 103), owners)
    positions = jax.vmap(lambda owner_key: jax.random.permutation(owner_key, RB))(owner_keys).astype(jnp.int32)
    slots = jnp.arange(owners, dtype=jnp.int32)[:, None] * RB + positions
    valid = jnp.arange(RB, dtype=jnp.int32)[None, :] < counts[:, None]
    flat_slots = slots.reshape(-1)
    scores = (1 - valid.reshape(-1).astype(jnp.int32)) * (owners * RB) + jnp.arange(owners * RB, dtype=jnp.int32)
    chosen = flat_slots[jnp.argsort(scores, stable=True)[:NR]]
    chosen = chosen[jax.random.permutation(jax.random.fold_in(key, 104), NR)]
    table = place_value(table, chosen[0], NB - 1)
    table = place_value(table, chosen[1], 0)
    return (table, table[chosen].astype(jnp.int32))


def draw_slot_block(key, part):
    shared = ownership(key)
    return shared[0]


def draw_refreshed(key, part):
    shared = ownership(key)
    return shared[1]


def draw_tokens(key, part):
    loading, feature_trend, unit_trend = shared_directions(key)
    key = jax.random.fold_in(key, 11)
    noise_key, scale_key = jax.random.split(key, 2)
    common = 0.5 * loading[:, None] * feature_trend[None, :]
    noise = jnp.clip(jax.random.normal(noise_key, (TOKENS, D), jnp.float32), -6.0, 6.0)
    field = column_field(noise, scale_key, D, 0.5, 5.0)
    return jnp.clip(field + common, -30.0, 30.0).astype(jnp.bfloat16)


def draw_upstream(key, part):
    loading, feature_trend, unit_trend = shared_directions(key)
    key = jax.random.fold_in(key, 12)
    noise_key, scale_key = jax.random.split(key, 2)
    common = 0.5 * loading[:, None] * unit_trend[None, :]
    noise = jnp.clip(jax.random.normal(noise_key, (TOKENS, F), jnp.float32), -6.0, 6.0)
    field = column_field(noise, scale_key, F, 0.5, 5.0)
    return jnp.clip(field + common, -30.0, 30.0).astype(jnp.bfloat16)


def draw_statistics(key, part):
    loading, feature_trend, unit_trend = shared_directions(key)
    table = ownership(key)[0]
    key = jax.random.fold_in(key, 13)
    kernel_key, strength_key = jax.random.split(key)
    field = kernel_blocks(kernel_key, NB * 2, BLOCK, BLOCK / 8.0, 0.1, 10.0, 1.0, 1.0)
    strength = jnp.exp(jax.random.uniform(strength_key, (NB, 2), jnp.float32, 0.0, math.log(6.0)))
    left_trend = feature_trend.reshape(RB, BLOCK)[table // COLS]
    right_trend = unit_trend.reshape(COLS, BLOCK)[table % COLS]
    trend = jnp.stack([left_trend, right_trend], axis=1)
    outer = strength[:, :, None, None] * trend[:, :, :, None] * trend[:, :, None, :]
    return (field.reshape(NB, 2, BLOCK, BLOCK) + outer).astype(jnp.bfloat16)


def draw_roots(key, part):
    key = jax.random.fold_in(key, 14)
    field = kernel_blocks(key, NB * 2, BLOCK, BLOCK / 8.0, 0.3, 3.0, 0.5, 0.5)
    return field.reshape(NB, 2, BLOCK, BLOCK).astype(jnp.bfloat16)


def block_levels(own_key, shape, cuts, low, top_value):
    factor_of, own = 1.0, jax.random.fold_in(own_key, 6)
    for dim, blocks in cuts:
        draws = jnp.exp(jax.random.uniform(jax.random.fold_in(own, dim), (blocks,), jnp.float32, low / len(cuts), top_value / len(cuts)))
        factor_of = factor_of * jnp.repeat(draws, shape[dim] // blocks).reshape([-1 if axis == dim else 1 for axis in range(len(shape))])
    return factor_of


def centred(key, shape, scale, most, pieces=(), held_as=jnp.bfloat16):
    level = block_levels(key, shape, pieces, -0.22, 0.18) if pieces else 1.0
    entries = jax.random.normal(key, shape, jnp.float32) * scale * level
    return jnp.minimum(jnp.maximum(entries, -most), most).astype(held_as)


def setup_inputs(seed: int = 0) -> dict:
    splits = jax.random.split(jax.random.key(seed), 8)
    tokens = draw_tokens(jax.random.fold_in(splits[7], 71), 0)
    in_weight = centred(splits[1], (D, F), D ** -0.5, 0.09375, ((1, 32),))
    upstream = draw_upstream(jax.random.fold_in(splits[7], 71), 0)
    slot_block = draw_slot_block(jax.random.fold_in(splits[7], 71), 0)
    refreshed = draw_refreshed(jax.random.fold_in(splits[7], 71), 0)
    statistics = draw_statistics(jax.random.fold_in(splits[7], 71), 0)
    roots = draw_roots(jax.random.fold_in(splits[7], 71), 0)
    return {"tokens": tokens, "in_weight": in_weight, "upstream": upstream, "slot_block": slot_block, "refreshed": refreshed, "statistics": statistics, "roots": roots}


decay = 0.9
jitter = 1e-06
floor_eps = 1e-06

def gelu_slope(values):
    return 0.5 * (1.0 + lax.erf(values * 0.7071067811865476)) + values * jnp.exp(-0.5 * values * values) * 0.3989422804014327

def inverse_root(matrices):
    order = matrices.shape[-1]
    identity = jnp.eye(order, dtype=matrices.dtype)
    trace_value = jnp.trace(matrices, axis1=-2, axis2=-1)[..., None, None]
    power = matrices / trace_value
    result = None
    for sweep in range(ITERS):
        factor = (5.0 * identity - power) * 0.25
        if result is None:
            result = factor
        else:
            result = jnp.matmul(result, factor, precision=lax.Precision.HIGHEST)
        if sweep + 1 < ITERS:
            square = jnp.matmul(factor, factor, precision=lax.Precision.HIGHEST)
            fourth = jnp.matmul(square, square, precision=lax.Precision.HIGHEST)
            power = jnp.matmul(fourth, power, precision=lax.Precision.HIGHEST)
    return result

def kronecker_pair(stats_pair, grads):
    order = grads.shape[-1]
    identity = jnp.eye(order, dtype=jnp.float32)
    wide = grads.astype(jnp.float32)
    left_outer = jnp.einsum('kij,klj->kil', wide, wide)
    right_outer = jnp.einsum('kji,kjl->kil', wide, wide)
    outer = jnp.stack([left_outer, right_outer], axis=1)
    return decay * stats_pair.astype(jnp.float32) + outer + jitter * identity

def precondition(factors, grads):
    first = jnp.einsum('kab,kbc->kac', factors[:, 0].astype(jnp.float32), grads.astype(jnp.float32))
    first = lax.optimization_barrier(first.astype(jnp.bfloat16))
    second = jnp.einsum('kab,kbc->kac', first.astype(jnp.float32), factors[:, 1].astype(jnp.float32))
    mean_square = lax.optimization_barrier(jnp.mean(second * second, axis=(1, 2), keepdims=True))
    return (second * lax.rsqrt(mean_square + floor_eps)).astype(jnp.bfloat16)

def reference(tokens, in_weight, upstream, slot_block, refreshed, statistics, roots):
    total_tokens = tokens.shape[0]
    gradient = jnp.zeros((D, F), jnp.float32)
    for member in range(TRAIN):
        own_tokens = tokens[member * TG:(member + 1) * TG]
        own_upstream = upstream[member * TG:(member + 1) * TG]
        forward = jnp.dot(own_tokens, in_weight, preferred_element_type=jnp.float32)
        delta = (own_upstream.astype(jnp.float32) * gelu_slope(forward)).astype(jnp.bfloat16)
        partial_value = jnp.dot(own_tokens.T, delta, preferred_element_type=jnp.float32) / total_tokens
        partial_value = lax.optimization_barrier(partial_value.astype(jnp.bfloat16)).astype(jnp.float32)
        gradient = gradient + partial_value
    gradient = gradient.astype(jnp.bfloat16)
    blocks = gradient.reshape(RB, BLOCK, COLS, BLOCK).transpose(0, 2, 1, 3).reshape(NB, BLOCK, BLOCK)
    grads = blocks[slot_block]
    matches = (slot_block[None, :] == refreshed[:, None]).astype(jnp.int32)
    fresh_slots = lax.optimization_barrier(jnp.sum(matches * jnp.arange(NB, dtype=jnp.int32)[None, :], axis=1)).astype(jnp.int32)
    fresh = inverse_root(kronecker_pair(statistics[fresh_slots], grads[fresh_slots])).astype(jnp.bfloat16)
    factors = roots.at[fresh_slots].set(fresh)
    return precondition(factors, grads)
```

```python
import jax
import jax.numpy as jnp
from jax import lax
from jax.experimental import pallas as pl
from jax.experimental.pallas import tpu as pltpu
from jax.sharding import PartitionSpec as P

decay = 0.9
jitter = 1e-06
floor_eps = 1e-06

ROWS = 384
IDS = 16
BLOCK = 512
BF = jnp.bfloat16
F32 = jnp.float32
MIB = 1 << 20

CORE = [(0, 1), (1, 0), (2, 3), (3, 2)]
CHIP = [(0, 2), (2, 0), (1, 3), (3, 1)]
SAME_CORE = [[chip * 64 + core * 32 + d for chip in range(2) for d in range(32)] for core in range(2)]


def params(mib):
    return pltpu.CompilerParams(vmem_limit_bytes=mib * MIB)


def nt(a, b):
    return lax.dot_general(a, b, (((1,), (1,)), ((), ())), preferred_element_type=F32)


def nn(a, b):
    return jnp.dot(a, b, preferred_element_type=F32)


def unit(n, dtype):
    row = lax.broadcasted_iota(jnp.int32, (n, n), 0)
    col = lax.broadcasted_iota(jnp.int32, (n, n), 1)
    return jnp.where(row == col, 1.0, 0.0).astype(dtype)


def gelu_slope(values):
    return (
        0.5 * (1.0 + lax.erf(values * 0.7071067811865476))
        + values * jnp.exp(-0.5 * values * values) * 0.3989422804014327
    )


def spare_position(k):
    return jnp.where(k < 3, 7 - k, jnp.where(k < 6, 6 - k, jnp.where(k == 6, 4, 0)))


def place(is_fresh, fresh_seen, spare_seen):
    position = jnp.where(is_fresh, 4 * fresh_seen, spare_position(spare_seen))
    return jnp.minimum(position, 7)


def mark_fresh(refreshed, table):
    def clear(k, c):
        table[k] = 0
        return c

    def mark(k, c):
        table[refreshed[k]] = 1
        return c

    lax.fori_loop(0, 256, clear, 0, unroll=8)
    lax.fori_loop(0, 32, mark, 0, unroll=8)


def plan_kernel(slot_block, refreshed, slot_at, table):
    mark_fresh(refreshed, table)
    fresh_seen = jnp.int32(0)
    spare_seen = jnp.int32(0)
    for p in range(8):
        flag = table[slot_block[p]]
        slot_at[place(flag == 1, fresh_seen, spare_seen)] = p
        fresh_seen += flag
        spare_seen += 1 - flag
    slot_at[8] = fresh_seen


def plan(slot_block, refreshed):
    smem = pl.BlockSpec(memory_space=pltpu.SMEM)
    return pl.pallas_call(
        plan_kernel,
        out_shape=jax.ShapeDtypeStruct((16,), jnp.int32),
        in_specs=[smem, smem],
        out_specs=smem,
        scratch_shapes=[pltpu.SMEM((256,), jnp.int32)],
        name="plan",
    )(slot_block, refreshed)


def wide(ref):
    return jnp.concatenate([ref[j][:ROWS] for j in range(ref.shape[0])], axis=1)


def gradient_kernel(where, own, other, weight, up_own, up_other, out, acc, delta_t):
    step = pl.program_id(0)

    @pl.when(step == 0)
    def _():
        acc[...] = jnp.zeros_like(acc)

    @pl.when(step < 4)
    def _():
        acc[:ROWS] += nn(wide(own), weight[...])
        acc[ROWS:] += nn(wide(other), weight[...])

    @pl.when(step == 3)
    def _():
        eye = unit(256, BF)
        for half, up in ((0, up_own), (1, up_other)):
            rows = pl.ds(half * ROWS, ROWS)
            delta = (up[...].astype(F32) * gelu_slope(acc[rows])).astype(BF)
            delta_t[:, rows] = nt(eye, delta).astype(BF)

    @pl.when(step >= 4)
    def _():
        both = jnp.concatenate([wide(own), wide(other)], axis=0)
        part = (nn(delta_t[...], both) / 1536.0).astype(BF)
        for row in range(2):
            for quarter in range(4):
                start = row * BLOCK + quarter * 128
                out[quarter * 16 : (quarter + 1) * 16, row] = part[:, start : start + 128].reshape(16, 16, 128)


def gradient_pieces(where, own, other, in_weight, upstream):
    rows = ROWS + IDS
    return pl.pallas_call(
        gradient_kernel,
        out_shape=jax.ShapeDtypeStruct((64, 8, 16, 128), BF),
        grid_spec=pltpu.PrefetchScalarGridSpec(
            num_scalar_prefetch=1,
            grid=(8,),
            in_specs=[
                pl.BlockSpec((8, rows, 128), lambda i, w: (i % 4, 0, 0)),
                pl.BlockSpec((8, rows, 128), lambda i, w: (i % 4, 0, 0)),
                pl.BlockSpec((1024, 256), lambda i, w: (jnp.minimum(i, 3), w[1])),
                pl.BlockSpec((ROWS, 256), lambda i, w: (w[0], w[1])),
                pl.BlockSpec((ROWS, 256), lambda i, w: (w[2], w[1])),
            ],
            out_specs=pl.BlockSpec((64, 2, 16, 128), lambda i, w: (0, jnp.maximum(i - 4, 0), 0, 0)),
            scratch_shapes=[pltpu.VMEM((2 * ROWS, 256), F32), pltpu.VMEM((256, 2 * ROWS), BF)],
        ),
        compiler_params=params(40),
        name="gradient",
    )(where, own, other, in_weight, upstream, upstream)


def route_kernel(ids, refreshed, pieces, out, table):
    mark_fresh(refreshed, table)

    def owner(o, c):
        fresh_seen = jnp.int32(0)
        spare_seen = jnp.int32(0)
        for p in range(8):
            block = ids[o * 8 + p]
            flag = table[block]
            position = place(flag == 1, fresh_seen, spare_seen)
            fresh_seen += flag
            spare_seen += 1 - flag
            row, col = block // 32, block % 32
            total = pieces[col, row].astype(F32) + pieces[col + 32, row].astype(F32)
            out[(position // 4) * 32 + o, position % 4] = total.astype(BF)
        return c

    lax.fori_loop(0, 32, owner, 0)


def route(ids, refreshed, pieces):
    smem = pl.BlockSpec(memory_space=pltpu.SMEM)
    vmem = pl.BlockSpec(memory_space=pltpu.VMEM)
    return pl.pallas_call(
        route_kernel,
        out_shape=jax.ShapeDtypeStruct((64, 4, 16, 128), BF),
        in_specs=[smem, smem, vmem],
        out_specs=vmem,
        scratch_shapes=[pltpu.SMEM((256,), jnp.int32)],
        compiler_params=params(16),
        name="route",
    )(ids, refreshed, pieces)


def collect(core, mine, theirs, grad_t):
    for quarter in range(4):
        cols = slice(quarter * 128, (quarter + 1) * 128)
        part = slice(quarter * 16, (quarter + 1) * 16)
        grad_t[pl.ds(pl.multiple_of(core * 256, 256), 256), cols] = mine[part, 0].reshape(256, 128)
        grad_t[pl.ds(pl.multiple_of(256 - core * 256, 256), 256), cols] = theirs[part, 0].reshape(256, 128)


def precondition(left, right, grad_t):
    first = nt(left, grad_t).astype(BF)
    second = nn(first, right)
    mean_square = jnp.sum(second * second, keepdims=True) * (1.0 / (BLOCK * BLOCK))
    return second * lax.rsqrt(mean_square + floor_eps)


def hand_out(where, value, keep, send, full):
    full[...] = value
    keep[0] = full[pl.ds(pl.multiple_of(where[0] * 128, 128), 128)].astype(BF)
    send[0] = full[pl.ds(pl.multiple_of(where[3] * 128, 128), 128)].astype(BF)


def stored_kernel(where, slot_at, mine, theirs, roots, keep, send, grad_t, full):
    collect(where[1], mine, theirs, grad_t)
    hand_out(where, precondition(roots[0, 0], roots[0, 1], grad_t[...]), keep, send, full)


def stored_slots(where, slot_at, mine, theirs, roots):
    half = pl.BlockSpec((64, 1, 16, 128), lambda i, w, s: (0, i + 1, 0, 0))
    rows = pl.BlockSpec((1, 128, BLOCK), lambda i, w, s: (i, 0, 0))
    return pl.pallas_call(
        stored_kernel,
        out_shape=[jax.ShapeDtypeStruct((3, 128, BLOCK), BF)] * 2,
        grid_spec=pltpu.PrefetchScalarGridSpec(
            num_scalar_prefetch=2,
            grid=(3,),
            in_specs=[half, half, pl.BlockSpec((1, 2, BLOCK, BLOCK), lambda i, w, s: (s[w[4] + i + 1], 0, 0, 0))],
            out_specs=[rows, rows],
            scratch_shapes=[pltpu.VMEM((BLOCK, BLOCK), BF), pltpu.VMEM((BLOCK, BLOCK), F32)],
        ),
        compiler_params=params(32),
        name="stored",
    )(where, slot_at, mine, theirs, roots)


def split(a):
    high = a.astype(BF)
    return high, (a - high.astype(F32)).astype(BF)


def product(a, b):
    ah, al = a
    bh, bl = b
    return nn(ah, bh) + (nn(ah, bl) + nn(al, bh))


def inverse_root(matrix):
    eye = unit(BLOCK, F32)
    power = matrix / jnp.sum(matrix * eye, keepdims=True)
    factor0 = (5.0 * eye - power) * 0.25
    f0 = split(factor0)
    s = split(product(f0, f0))
    q = split(product(s, s))
    power = product(q, split(power))
    factor1 = (5.0 * eye - power) * 0.25
    f1 = split(factor1)
    result = split(product(f0, f1))
    s = split(product(f1, f1))
    q = split(product(s, s))
    power = product(q, split(power))
    factor2 = (5.0 * eye - power) * 0.25
    return product(result, split(factor2))


def newton_kernel(where, slot_at, mine, theirs, statistic, out, grad_t):
    core = where[1]
    collect(core, mine, theirs, grad_t)

    @pl.when(core == 0)
    def _():
        grad_t[...] = nt(unit(BLOCK, BF), grad_t[...]).astype(BF)

    g = grad_t[...]
    matrix = decay * statistic[0, 0].astype(F32) + nt(g, g) + jitter * unit(BLOCK, F32)
    out[...] = inverse_root(matrix).astype(BF)


def newton(where, slot_at, mine, theirs, statistics):
    half = pl.BlockSpec((64, 1, 16, 128), lambda i, w, s: (0, 0, 0, 0))
    return pl.pallas_call(
        newton_kernel,
        out_shape=jax.ShapeDtypeStruct((BLOCK, BLOCK), BF),
        grid_spec=pltpu.PrefetchScalarGridSpec(
            num_scalar_prefetch=2,
            grid=(1,),
            in_specs=[half, half, pl.BlockSpec((1, 1, BLOCK, BLOCK), lambda i, w, s: (s[w[4]], w[1], 0, 0))],
            out_specs=pl.BlockSpec((BLOCK, BLOCK), lambda i, w, s: (0, 0)),
            scratch_shapes=[pltpu.VMEM((BLOCK, BLOCK), BF)],
        ),
        compiler_params=params(48),
        name="newton",
    )(where, slot_at, mine, theirs, statistics)


def fresh_kernel(where, slot_at, mine, theirs, roots, root, other_root, keep, send, grad_t, full, pair):
    core = where[1]
    collect(core, mine, theirs, grad_t)
    pair[...] = roots[0]

    @pl.when(slot_at[8] > where[4] // 4)
    def _():
        pair[core] = root[...]
        pair[1 - core] = other_root[...]

    hand_out(where, precondition(pair[0], pair[1], grad_t[...]), keep, send, full)


def fresh_slot(where, slot_at, mine, theirs, roots, root, other_root):
    half = pl.BlockSpec((64, 1, 16, 128), lambda i, w, s: (0, 0, 0, 0))
    rows = pl.BlockSpec((1, 128, BLOCK), lambda i, w, s: (0, 0, 0))
    square = pl.BlockSpec((BLOCK, BLOCK), lambda i, w, s: (0, 0))
    return pl.pallas_call(
        fresh_kernel,
        out_shape=[jax.ShapeDtypeStruct((1, 128, BLOCK), BF)] * 2,
        grid_spec=pltpu.PrefetchScalarGridSpec(
            num_scalar_prefetch=2,
            grid=(1,),
            in_specs=[
                half,
                half,
                pl.BlockSpec((1, 2, BLOCK, BLOCK), lambda i, w, s: (s[w[4]], 0, 0, 0)),
                square,
                square,
            ],
            out_specs=[rows, rows],
            scratch_shapes=[
                pltpu.VMEM((BLOCK, BLOCK), BF),
                pltpu.VMEM((BLOCK, BLOCK), F32),
                pltpu.VMEM((2, BLOCK, BLOCK), BF),
            ],
        ),
        compiler_params=params(32),
        name="fresh",
    )(where, slot_at, mine, theirs, roots, root, other_root)


def assemble_kernel(where, slot_at, fresh_mine, fresh_theirs, mine, theirs, out):
    here = where[4]
    there = 4 - here
    out[slot_at[here]] = fresh_mine[0]
    out[slot_at[there]] = fresh_theirs[0]
    for k in range(3):
        out[slot_at[here + k + 1]] = mine[k]
        out[slot_at[there + k + 1]] = theirs[k]


def assemble(where, slot_at, *parts):
    smem = pl.BlockSpec(memory_space=pltpu.SMEM)
    vmem = pl.BlockSpec(memory_space=pltpu.VMEM)
    return pl.pallas_call(
        assemble_kernel,
        out_shape=jax.ShapeDtypeStruct((8, 128, BLOCK), BF),
        in_specs=[smem, smem] + [vmem] * 4,
        out_specs=vmem,
        compiler_params=params(16),
        name="assemble",
    )(where, slot_at, *parts)


def shards(tokens, in_weight, upstream, slot_block, refreshed, statistics, roots):
    group = lax.axis_index("grp")
    core = group % 2
    chip = group // 2
    both = ("grp", "dev")
    where = jnp.stack([group, core, group + 1 - 2 * core, group + 2 - 4 * chip, 4 * chip]).astype(jnp.int32)
    slot_at = plan(slot_block, refreshed)

    own = lax.dynamic_slice_in_dim(tokens, group * ROWS, ROWS, 0)
    ids = jnp.pad(slot_block.astype(BF).reshape(1, 8), ((0, IDS - 1), (0, 120)))
    sent = jnp.broadcast_to(jnp.concatenate([own, ids], axis=0)[None], (32, ROWS + IDS, 128))
    features = lax.all_to_all(sent, "dev", 0, 0, tiled=True)
    all_ids = features[:, ROWS, :8].astype(jnp.int32).reshape(256)
    other_features = lax.ppermute(features, "grp", CORE)

    pieces = gradient_pieces(where, features, other_features, in_weight, upstream)
    pieces = lax.all_to_all(pieces, both, 0, 0, tiled=True, axis_index_groups=SAME_CORE)
    pieces = route(all_ids, refreshed, pieces)
    mine = lax.all_to_all(pieces, both, 0, 0, tiled=True, axis_index_groups=SAME_CORE)
    theirs = lax.ppermute(mine, "grp", CORE)

    keep, send = stored_slots(where, slot_at, mine, theirs, roots)
    other_keep = lax.ppermute(send, "grp", CHIP)
    root = newton(where, slot_at, mine, theirs, statistics)
    other_root = lax.ppermute(root, "grp", CORE)
    fresh_keep, fresh_send = fresh_slot(where, slot_at, mine, theirs, roots, root, other_root)
    fresh_other = lax.ppermute(fresh_send, "grp", CHIP)
    return assemble(where, slot_at, fresh_keep, fresh_other, keep, other_keep)


def solution(mesh):
    return jax.shard_map(
        shards,
        mesh=mesh,
        in_specs=(
            P(None, "dev"),
            P(None, "dev"),
            P(None, "dev"),
            P("dev"),
            P(),
            P("dev", None, None, None),
            P("dev", None, None, None),
        ),
        out_specs=P("dev", "grp", None),
        check_vma=False,
    )
```

```python
import jax
import jax.numpy as jnp
from jax import lax
from jax.experimental import pallas as pl
from jax.experimental.pallas import tpu as pltpu
from jax.sharding import PartitionSpec as P

decay = 0.9
jitter = 1e-06
floor_eps = 1e-06

ROWS = 384
IDS = 16
BLOCK = 512
BF = jnp.bfloat16
F32 = jnp.float32
MIB = 1 << 20

CORE = [(0, 1), (1, 0), (2, 3), (3, 2)]
CHIP = [(0, 2), (2, 0), (1, 3), (3, 1)]
SAME_CORE = [[chip * 64 + core * 32 + d for chip in range(2) for d in range(32)] for core in range(2)]


def params(mib):
    return pltpu.CompilerParams(vmem_limit_bytes=mib * MIB)


def cost(flops, nbytes):
    return pl.CostEstimate(flops=flops, bytes_accessed=nbytes, transcendentals=0)


def nt(a, b):
    return lax.dot_general(a, b, (((1,), (1,)), ((), ())), preferred_element_type=F32)


def nn(a, b):
    return jnp.dot(a, b, preferred_element_type=F32)


def unit(n, dtype):
    row = lax.broadcasted_iota(jnp.int32, (n, n), 0)
    col = lax.broadcasted_iota(jnp.int32, (n, n), 1)
    return jnp.where(row == col, 1.0, 0.0).astype(dtype)


def gelu_slope(values):
    return (
        0.5 * (1.0 + lax.erf(values * 0.7071067811865476))
        + values * jnp.exp(-0.5 * values * values) * 0.3989422804014327
    )


def spare_position(k):
    return jnp.where(k < 3, 7 - k, jnp.where(k < 6, 6 - k, jnp.where(k == 6, 4, 0)))


def place(flag, fresh_seen, spare_seen):
    return jnp.minimum(jnp.where(flag == 1, 4 * fresh_seen, spare_position(spare_seen)), 7)


def order_kernel(ids, refreshed, slot_block, source, slot_at, table):
    def clear(k, c):
        table[k] = 0
        return c

    def mark(k, c):
        table[refreshed[k]] = 1
        return c

    lax.fori_loop(0, 256, clear, 0, unroll=8)
    lax.fori_loop(0, 32, mark, 0, unroll=8)

    def owner(o, c):
        fresh_seen = jnp.int32(0)
        spare_seen = jnp.int32(0)
        for p in range(8):
            block = ids[o * 8 + p]
            flag = table[block]
            position = place(flag, fresh_seen, spare_seen)
            fresh_seen += flag
            spare_seen += 1 - flag
            source[(position // 4) * 128 + o * 4 + position % 4] = (block % 32) * 8 + block // 32
        return c

    lax.fori_loop(0, 32, owner, 0)
    fresh_seen = jnp.int32(0)
    spare_seen = jnp.int32(0)
    for p in range(8):
        flag = table[slot_block[p]]
        slot_at[place(flag, fresh_seen, spare_seen)] = p
        fresh_seen += flag
        spare_seen += 1 - flag
    slot_at[8] = fresh_seen


def slot_order(ids, refreshed, slot_block):
    smem = pl.BlockSpec(memory_space=pltpu.SMEM)
    return pl.pallas_call(
        order_kernel,
        out_shape=[jax.ShapeDtypeStruct((256,), jnp.int32), jax.ShapeDtypeStruct((16,), jnp.int32)],
        in_specs=[smem] * 3,
        out_specs=[smem] * 2,
        scratch_shapes=[pltpu.SMEM((256,), jnp.int32)],
        cost_estimate=cost(0, 4096),
        name="order",
    )(ids, refreshed, slot_block)


def wide(ref, chunk):
    return jnp.concatenate([ref[8 * chunk + j] for j in range(8)], axis=1)


def weights_kernel(where, weight, upstream, w, up, sem):
    cols = pl.ds(pl.multiple_of(where[1] * 256, 256), 256)
    loads = [pltpu.make_async_copy(weight.at[:, cols], w, sem.at[2])]
    for k in range(2):
        rows = pl.ds(pl.multiple_of(where[2 * k] * ROWS, ROWS), ROWS)
        loads.append(pltpu.make_async_copy(upstream.at[rows, cols], up.at[k], sem.at[k]))
    for load in loads:
        load.start()
    for load in loads:
        load.wait()


def half_of_weights(where, in_weight, upstream):
    vmem = pl.BlockSpec(memory_space=pltpu.VMEM)
    hbm = pl.BlockSpec(memory_space=pl.ANY)
    return pl.pallas_call(
        weights_kernel,
        out_shape=[jax.ShapeDtypeStruct((4096, 256), BF), jax.ShapeDtypeStruct((2, ROWS, 256), BF)],
        in_specs=[pl.BlockSpec(memory_space=pltpu.SMEM), hbm, hbm],
        out_specs=[vmem, vmem],
        scratch_shapes=[pltpu.SemaphoreType.DMA((3,))],
        compiler_params=params(4),
        cost_estimate=cost(0, 5 * MIB),
        name="weights",
    )(where, in_weight, upstream)


def wide(ref, chunk):
    return jnp.concatenate([ref[8 * chunk + j, :ROWS] for j in range(8)], axis=1)


def gradient_kernel(own, other, w, up, out, acc, delta_t):
    for k in range(4):
        for half, ref in ((0, own), (1, other)):
            part = nn(wide(ref, k), w[1024 * k : 1024 * (k + 1)])
            rows = slice(half * ROWS, (half + 1) * ROWS)
            acc[rows] = part if k == 0 else acc[rows] + part
    eye = unit(256, BF)
    for half in range(2):
        rows = slice(half * ROWS, (half + 1) * ROWS)
        delta = (up[half].astype(F32) * gelu_slope(acc[rows])).astype(BF)
        delta_t[:, rows] = nt(eye, delta).astype(BF)
    for k in range(4):
        both = jnp.concatenate([wide(own, k), wide(other, k)], axis=0)
        part = (nn(delta_t[...], both) / 1536.0).astype(BF)
        for row in range(2):
            for quarter in range(4):
                start = row * BLOCK + quarter * 128
                out[quarter * 16 : (quarter + 1) * 16, 2 * k + row] = part[:, start : start + 128].reshape(16, 16, 128)


def gradient_pieces(own, other, w, up):
    vmem = pl.BlockSpec(memory_space=pltpu.VMEM)
    return pl.pallas_call(
        gradient_kernel,
        out_shape=jax.ShapeDtypeStruct((64, 8, 16, 128), BF),
        in_specs=[vmem] * 4,
        out_specs=vmem,
        scratch_shapes=[pltpu.VMEM((2 * ROWS, 256), F32), pltpu.VMEM((256, 2 * ROWS), BF)],
        compiler_params=params(10),
        cost_estimate=cost(4 * 768 * 4096 * 256, 12 * MIB),
        name="gradient",
    )(own, other, w, up)


def route_kernel(source, pieces, out):
    def some(n, c):
        for k in range(16):
            at = source[n * 16 + k]
            out[n * 16 + k] = (pieces[at].astype(F32) + pieces[at + 256].astype(F32)).astype(BF)
        return c

    lax.fori_loop(0, 16, some, 0)


def route(source, pieces):
    vmem = pl.BlockSpec(memory_space=pltpu.VMEM)
    out = pl.pallas_call(
        route_kernel,
        out_shape=jax.ShapeDtypeStruct((256, 16, 128), BF),
        in_specs=[pl.BlockSpec(memory_space=pltpu.SMEM), vmem],
        out_specs=vmem,
        compiler_params=params(16),
        cost_estimate=cost(0, 3 * MIB),
        name="route",
    )(source, pieces.reshape(512, 16, 128))
    return out.reshape(64, 4, 16, 128)


def collect(core, mine, theirs, slot, grad_t):
    for quarter in range(4):
        cols = slice(quarter * 128, (quarter + 1) * 128)
        part = slice(quarter * 16, (quarter + 1) * 16)
        grad_t[pl.ds(pl.multiple_of(core * 256, 256), 256), cols] = mine[part, slot].reshape(256, 128)
        grad_t[pl.ds(pl.multiple_of(256 - core * 256, 256), 256), cols] = theirs[part, slot].reshape(256, 128)


def hand_out(where, second, keep, send, slot, full):
    full[...] = second
    mean_square = jnp.sum(second * second, keepdims=True) * (1.0 / (BLOCK * BLOCK))
    scale = lax.rsqrt(mean_square + floor_eps)
    keep[slot] = (full[pl.ds(pl.multiple_of(where[0] * 128, 128), 128)] * scale).astype(BF)
    send[slot] = (full[pl.ds(pl.multiple_of(where[3] * 128, 128), 128)] * scale).astype(BF)


def fetch_kernel(where, slot_at, roots, statistics, pairs, statistic, sem):
    loads = [pltpu.make_async_copy(roots.at[slot_at[where[4] + k]], pairs.at[k], sem.at[k]) for k in range(4)]
    loads.append(pltpu.make_async_copy(statistics.at[slot_at[where[4]], where[1]], statistic, sem.at[4]))
    for load in loads:
        load.start()
    for load in loads:
        load.wait()


def fetch(where, slot_at, roots, statistics):
    smem = pl.BlockSpec(memory_space=pltpu.SMEM)
    vmem = pl.BlockSpec(memory_space=pltpu.VMEM)
    hbm = pl.BlockSpec(memory_space=pl.ANY)
    return pl.pallas_call(
        fetch_kernel,
        out_shape=[jax.ShapeDtypeStruct((4, 2, BLOCK, BLOCK), BF), jax.ShapeDtypeStruct((BLOCK, BLOCK), BF)],
        in_specs=[smem, smem, hbm, hbm],
        out_specs=[vmem, vmem],
        scratch_shapes=[pltpu.SemaphoreType.DMA((5,))],
        compiler_params=params(8),
        cost_estimate=cost(0, 9 * MIB),
        name="fetch",
    )(where, slot_at, roots, statistics)


def stored_kernel(where, mine, theirs, pairs, keep, send, grad_t, full):
    for k in range(3):
        collect(where[1], mine, theirs, k + 1, grad_t.at[k])
    firsts = [nt(pairs[k + 1, 0], grad_t[k]).astype(BF) for k in range(3)]
    seconds = [nn(firsts[k], pairs[k + 1, 1]) for k in range(3)]
    for k in range(3):
        hand_out(where, seconds[k], keep, send, k, full.at[k])


def stored_slots(where, mine, theirs, pairs):
    smem = pl.BlockSpec(memory_space=pltpu.SMEM)
    vmem = pl.BlockSpec(memory_space=pltpu.VMEM)
    return pl.pallas_call(
        stored_kernel,
        out_shape=[jax.ShapeDtypeStruct((3, 128, BLOCK), BF)] * 2,
        in_specs=[smem, vmem, vmem, vmem],
        out_specs=[vmem, vmem],
        scratch_shapes=[pltpu.VMEM((3, BLOCK, BLOCK), BF), pltpu.VMEM((3, BLOCK, BLOCK), F32)],
        compiler_params=params(20),
        cost_estimate=cost(12 * BLOCK**3, 4 * MIB),
        name="stored",
    )(where, mine, theirs, pairs)


def split(a):
    high = a.astype(BF)
    return high, (a - high.astype(F32)).astype(BF)


def product(a, b):
    ah, al = a
    bh, bl = b
    return nn(ah, bh) + (nn(ah, bl) + nn(al, bh))


def newton_kernel(where, mine, theirs, statistic, parts, grad_t):
    core = where[1]
    collect(core, mine, theirs, 0, grad_t)

    @pl.when(core == 0)
    def _():
        grad_t[...] = nt(unit(BLOCK, BF), grad_t[...]).astype(BF)

    g = grad_t[...]
    eye = unit(BLOCK, F32)
    matrix = decay * statistic[...].astype(F32) + nt(g, g) + jitter * eye
    power = matrix / jnp.sum(matrix * eye, keepdims=True)
    f0 = split((5.0 * eye - power) * 0.25)
    s = split(product(f0, f0))
    q = split(product(s, s))
    power = product(q, split(power))
    f1 = split((5.0 * eye - power) * 0.25)
    parts[0], parts[1] = split(product(f0, f1))
    s = split(product(f1, f1))
    q = split(product(s, s))
    power = product(q, split(power))
    parts[2], parts[3] = split((5.0 * eye - power) * 0.25)


def newton(where, mine, theirs, statistic):
    vmem = pl.BlockSpec(memory_space=pltpu.VMEM)
    return pl.pallas_call(
        newton_kernel,
        out_shape=jax.ShapeDtypeStruct((4, BLOCK, BLOCK), BF),
        in_specs=[pl.BlockSpec(memory_space=pltpu.SMEM), vmem, vmem, vmem],
        out_specs=vmem,
        scratch_shapes=[pltpu.VMEM((BLOCK, BLOCK), BF)],
        compiler_params=params(24),
        cost_estimate=cost(46 * BLOCK**3, 2 * MIB),
        name="newton",
    )(where, mine, theirs, statistic)


def root_kernel(parts, root):
    root[...] = product((parts[0], parts[1]), (parts[2], parts[3])).astype(BF)


def last_product(parts):
    vmem = pl.BlockSpec(memory_space=pltpu.VMEM)
    return pl.pallas_call(
        root_kernel,
        out_shape=jax.ShapeDtypeStruct((BLOCK, BLOCK), BF),
        in_specs=[vmem],
        out_specs=vmem,
        compiler_params=params(16),
        cost_estimate=cost(6 * BLOCK**3, 2 * MIB),
        name="root",
    )(parts)


def fresh_kernel(where, slot_at, mine, theirs, pairs, root, other_root, keep, send, grad_t, full, pair):
    core = where[1]
    pair[...] = pairs[0]

    @pl.when(slot_at[8] > where[4] // 4)
    def _():
        pair[core] = root[...]
        pair[1 - core] = other_root[...]

    collect(core, mine, theirs, 0, grad_t)
    first = nt(pair[0], grad_t[...]).astype(BF)
    hand_out(where, nn(first, pair[1]), keep, send, 0, full)


def fresh_slot(where, slot_at, mine, theirs, pairs, root, other_root):
    smem = pl.BlockSpec(memory_space=pltpu.SMEM)
    vmem = pl.BlockSpec(memory_space=pltpu.VMEM)
    return pl.pallas_call(
        fresh_kernel,
        out_shape=[jax.ShapeDtypeStruct((1, 128, BLOCK), BF)] * 2,
        in_specs=[smem, smem] + [vmem] * 5,
        out_specs=[vmem, vmem],
        scratch_shapes=[
            pltpu.VMEM((BLOCK, BLOCK), BF),
            pltpu.VMEM((BLOCK, BLOCK), F32),
            pltpu.VMEM((2, BLOCK, BLOCK), BF),
        ],
        compiler_params=params(16),
        cost_estimate=cost(4 * BLOCK**3, 2 * MIB),
        name="fresh",
    )(where, slot_at, mine, theirs, pairs, root, other_root)


def assemble_kernel(where, slot_at, fresh_mine, mine, theirs, out):
    here = where[4]
    there = 4 - here
    out[slot_at[here]] = fresh_mine[0]
    for k in range(3):
        out[slot_at[here + k + 1]] = mine[k]
        out[slot_at[there + k + 1]] = theirs[k]


def assemble(where, slot_at, *parts):
    smem = pl.BlockSpec(memory_space=pltpu.SMEM)
    vmem = pl.BlockSpec(memory_space=pltpu.VMEM)
    return pl.pallas_call(
        assemble_kernel,
        out_shape=jax.ShapeDtypeStruct((8, 128, BLOCK), BF),
        in_specs=[smem, smem] + [vmem] * 3,
        out_specs=vmem,
        compiler_params=params(16),
        cost_estimate=cost(0, 2 * MIB),
        name="assemble",
    )(where, slot_at, *parts)


def shards(tokens, in_weight, upstream, slot_block, refreshed, statistics, roots):
    group = lax.axis_index("grp")
    core = group % 2
    chip = group // 2
    both = ("grp", "dev")
    where = jnp.stack([group, core, group + 1 - 2 * core, group + 2 - 4 * chip, 4 * chip]).astype(jnp.int32)

    own = lax.dynamic_slice_in_dim(tokens, group * ROWS, ROWS, 0)
    ids = jnp.pad(slot_block.astype(BF).reshape(1, 8), ((0, IDS - 1), (0, 120)))
    sent = jnp.broadcast_to(jnp.concatenate([own, ids], axis=0)[None], (32, ROWS + IDS, 128))
    features = lax.all_to_all(sent, "dev", 0, 0, tiled=True)
    all_ids = features[:, ROWS, :8].astype(jnp.int32).reshape(256)
    other_features = lax.ppermute(features, "grp", CORE)

    w, up = half_of_weights(where, in_weight, upstream)
    pieces = gradient_pieces(features, other_features, w, up)
    pieces = lax.all_to_all(pieces, both, 0, 0, tiled=True, axis_index_groups=SAME_CORE)
    source, slot_at = slot_order(all_ids, refreshed, slot_block)
    pairs, statistic = fetch(where, slot_at, roots, statistics)
    source, pairs, statistic = lax.optimization_barrier((source, pairs, statistic))
    pieces = route(source, pieces)
    mine = lax.all_to_all(pieces, both, 0, 0, tiled=True, axis_index_groups=SAME_CORE)
    theirs = lax.ppermute(mine, "grp", CORE)

    keep, send = stored_slots(where, mine, theirs, pairs)
    other_keep = lax.ppermute(send, "grp", CHIP)
    mine, theirs, keep = lax.optimization_barrier((mine, theirs, keep))
    parts = newton(where, mine, theirs, statistic)
    parts, other_keep = lax.optimization_barrier((parts, other_keep))
    root = last_product(parts)
    other_root = lax.ppermute(root, "grp", CORE)
    fresh_keep, fresh_send = fresh_slot(where, slot_at, mine, theirs, pairs, root, other_root)
    fresh_other = lax.ppermute(fresh_send, "grp", CHIP)
    update = assemble(where, slot_at, fresh_keep, keep, other_keep)
    return lax.dynamic_update_slice_in_dim(update, fresh_other, slot_at[4 - 4 * chip], 0)


def solution(mesh):
    return jax.shard_map(
        shards,
        mesh=mesh,
        in_specs=(
            P(None, "dev"),
            P(None, "dev"),
            P(None, "dev"),
            P("dev"),
            P(),
            P("dev", None, None, None),
            P("dev", None, None, None),
        ),
        out_specs=P("dev", "grp", None),
        check_vma=False,
    )
```

```python
import functools

import jax
import jax.numpy as jnp
from jax import lax
from jax.experimental import pallas as pl
from jax.experimental.pallas import tpu as pltpu
from jax.sharding import PartitionSpec as P

decay = 0.9
jitter = 1e-06
floor_eps = 1e-06

ROWS = 384
IDS = 16
BLOCK = 512
BF = jnp.bfloat16
F32 = jnp.float32
MIB = 1 << 20

CORE = [(0, 1), (1, 0), (2, 3), (3, 2)]
CHIP = [(0, 2), (2, 0), (1, 3), (3, 1)]
def device(chip, core, z, y_hi, x):
    return (chip * 2 + core) * 32 + z * 8 + y_hi * 4 + x


def on_rings(chip, core, y_hi, first, second):
    return device(chip, core, second, y_hi, first) if core == 0 else device(chip, core, first, y_hi, second)


STAGE1 = [
    [on_rings(m, core, m ^ flip, i, a) for m in range(2) for i in range(4)]
    for core in range(2)
    for a in range(4)
    for flip in range(2)
]
EVERYWHERE = [
    (chip, core, z, y_hi, x)
    for chip in range(2)
    for core in range(2)
    for z in range(4)
    for y_hi in range(2)
    for x in range(4)
]


def along(step):
    return [
        (
            device(chip, core, z, y_hi, x),
            device(chip, core, z, y_hi, (x + step) % 4) if core else device(chip, core, (z + step) % 4, y_hi, x),
        )
        for chip, core, z, y_hi, x in EVERYWHERE
    ]


UP, DOWN = along(1), along(-1)
STEPS = (0, -1, 1, 2)
SAME_CORE = [[chip * 64 + core * 32 + d for chip in range(2) for d in range(32)] for core in range(2)]


def params(mib):
    return pltpu.CompilerParams(vmem_limit_bytes=mib * MIB)


def cost(flops, nbytes):
    return pl.CostEstimate(flops=flops, bytes_accessed=nbytes, transcendentals=0)


def nt(a, b):
    return lax.dot_general(a, b, (((1,), (1,)), ((), ())), preferred_element_type=F32)


def nn(a, b):
    return jnp.dot(a, b, preferred_element_type=F32)


def unit(n, dtype):
    row = lax.broadcasted_iota(jnp.int32, (n, n), 0)
    col = lax.broadcasted_iota(jnp.int32, (n, n), 1)
    return jnp.where(row == col, 1.0, 0.0).astype(dtype)


def gelu_slope(values):
    return (
        0.5 * (1.0 + lax.erf(values * 0.7071067811865476))
        + values * jnp.exp(-0.5 * values * values) * 0.3989422804014327
    )


def spare_position(k):
    return jnp.where(k < 3, 7 - k, jnp.where(k < 6, 6 - k, jnp.where(k == 6, 4, 0)))


def place(flag, fresh_seen, spare_seen):
    return jnp.minimum(jnp.where(flag == 1, 4 * fresh_seen, spare_position(spare_seen)), 7)


def order_kernel(where, ids, refreshed, slot_block, source, slot_at, table):
    def clear(k, c):
        table[k] = 0
        return c

    def mark(k, c):
        table[refreshed[k]] = 1
        return c

    lax.fori_loop(0, 256, clear, 0, unroll=8)
    lax.fori_loop(0, 32, mark, 0, unroll=8)

    def positions(blocks):
        flags = [table[block] for block in blocks]
        fresh_seen = jnp.int32(0)
        spare_seen = jnp.int32(0)
        found = []
        for flag in flags:
            found.append(place(flag, fresh_seen, spare_seen))
            fresh_seen += flag
            spare_seen += 1 - flag
        return found, fresh_seen

    def owner(o, c):
        z, y_hi, x = o >> 3, (o >> 2) & 1, o & 3
        across = jnp.where(where[1] == 0, z, x)
        inner = jnp.where(where[1] == 0, x, z)
        step = (across - where[6]) & 3
        group = jnp.where(step == 0, 0, jnp.where(step == 3, 1, step + 1))
        piece = group * 8 + (y_hi ^ where[5]) * 4 + inner
        blocks = [ids[piece * 8 + p] for p in range(8)]
        found, _ = positions(blocks)
        for block, position in zip(blocks, found):
            source[(position >> 2) * 128 + o * 4 + (position & 3)] = (block & 31) * 8 + (block >> 5)
        return c

    lax.fori_loop(0, 32, owner, 0)
    found, fresh_seen = positions([slot_block[p] for p in range(8)])
    for p in range(8):
        slot_at[found[p]] = p
    slot_at[8] = fresh_seen


def slot_order(where, ids, refreshed, slot_block):
    smem = pl.BlockSpec(memory_space=pltpu.SMEM)
    return pl.pallas_call(
        order_kernel,
        out_shape=[jax.ShapeDtypeStruct((256,), jnp.int32), jax.ShapeDtypeStruct((16,), jnp.int32)],
        in_specs=[smem] * 4,
        out_specs=[smem] * 2,
        scratch_shapes=[pltpu.SMEM((256,), jnp.int32)],
        cost_estimate=cost(0, 4096),
        name="order",
    )(where, ids, refreshed, slot_block)


def prepare_kernel(where, tokens, slot_block, out):
    row = lax.broadcasted_iota(jnp.int32, (IDS, 128), 0)
    lane = lax.broadcasted_iota(jnp.int32, (IDS, 128), 1)
    ids = jnp.zeros((IDS, 128), jnp.int32)
    for p in range(8):
        ids = jnp.where((row == 0) & (lane == p), slot_block[p], ids)
    ids = ids.astype(F32).astype(BF)
    for m in range(2):
        start = pl.multiple_of((2 * m + where[1]) * ROWS, ROWS)
        part = tokens[pl.ds(start, ROWS)]
        for i in range(4):
            out[4 * m + i, :ROWS] = part
            out[4 * m + i, ROWS:] = ids


def prepare(where, tokens, slot_block):
    smem = pl.BlockSpec(memory_space=pltpu.SMEM)
    vmem = pl.BlockSpec(memory_space=pltpu.VMEM)
    return pl.pallas_call(
        prepare_kernel,
        out_shape=jax.ShapeDtypeStruct((8, ROWS + IDS, 128), BF),
        in_specs=[smem, vmem, smem],
        out_specs=vmem,
        compiler_params=params(8),
        cost_estimate=cost(0, MIB),
        name="prepare",
    )(where, tokens, slot_block)


def weights_kernel(where, weight, upstream, w, up, sem):
    cols = pl.ds(pl.multiple_of(where[1] * 256, 256), 256)
    loads = [pltpu.make_async_copy(weight.at[:, cols], w, sem.at[2])]
    for k in range(2):
        rows = pl.ds(pl.multiple_of(where[2 * k] * ROWS, ROWS), ROWS)
        loads.append(pltpu.make_async_copy(upstream.at[rows, cols], up.at[k], sem.at[k]))
    for load in loads:
        load.start()
    for load in loads:
        load.wait()


def half_of_weights(where, in_weight, upstream):
    vmem = pl.BlockSpec(memory_space=pltpu.VMEM)
    hbm = pl.BlockSpec(memory_space=pl.ANY)
    return pl.pallas_call(
        weights_kernel,
        out_shape=[jax.ShapeDtypeStruct((4096, 256), BF), jax.ShapeDtypeStruct((2, ROWS, 256), BF)],
        in_specs=[pl.BlockSpec(memory_space=pltpu.SMEM), hbm, hbm],
        out_specs=[vmem, vmem],
        scratch_shapes=[pltpu.SemaphoreType.DMA((3,))],
        compiler_params=params(4),
        cost_estimate=cost(0, 5 * MIB),
        name="weights",
    )(where, in_weight, upstream)


def piece(group, m, i):
    return group[0][m * 4 + i, :ROWS] if len(group) == 1 else group[m][i, :ROWS]


def group_product(group, w, core, across, flip):
    tokens = jnp.concatenate([piece(group, j // 4, j % 4) for j in range(8)], axis=1)
    weights = []
    for j in range(8):
        row = jnp.where(core == 0, across * 1024 + j % 4 * 128, j % 4 * 1024 + across * 128) + ((j // 4) ^ flip) * 512
        weights.append(w[pl.ds(pl.multiple_of(row, 128), 128)])
    return nn(tokens, jnp.concatenate(weights, axis=0))


def forward_kernel(steps, where, before, *refs):
    count = len(steps)
    w, acc = refs[2 * count], refs[2 * count + 1]
    for half in range(2):
        core = where[1] if half == 0 else 1 - where[1]
        total = before[half] if before is not None else None
        for k, step in enumerate(steps):
            part = group_product([refs[half * count + k]], w, core, (where[6 + half] + step) & 3, where[5])
            total = part if total is None else total + part
        acc[half] = total


def forward(steps, where, groups, w, before=None):
    vmem = pl.BlockSpec(memory_space=pltpu.VMEM)
    if before is None:
        kernel = lambda where, *refs: forward_kernel(steps, where, None, *refs)
        operands = [*groups, w]
    else:
        kernel = functools.partial(forward_kernel, steps)
        operands = [before, *groups, w]
    return pl.pallas_call(
        kernel,
        out_shape=jax.ShapeDtypeStruct((2, ROWS, 256), F32),
        in_specs=[pl.BlockSpec(memory_space=pltpu.SMEM)] + [vmem] * len(operands),
        out_specs=vmem,
        compiler_params=params(8),
        cost_estimate=cost(2 * ROWS * 1024 * 256 * len(groups), 2 * MIB),
        name="forward",
    )(where, *operands)


def gradient_kernel(where, before, *refs):
    own = [refs[0:1], refs[1:2], refs[2:3], refs[3:5]]
    other = [refs[5:6], refs[6:7], refs[7:8], refs[8:10]]
    w, up, out, delta_t = refs[10:]
    core, flip = where[1], where[5]
    eye = unit(256, BF)
    for half, group in ((0, own[3]), (1, other[3])):
        last = group_product(group, w, core if half == 0 else 1 - core, (where[6 + half] + STEPS[3]) & 3, flip)
        delta = (up[half].astype(F32) * gelu_slope(before[half] + last)).astype(BF)
        delta_t[:, half * ROWS : (half + 1) * ROWS] = nt(eye, delta).astype(BF)
    delta = delta_t[...]
    for k in range(4):
        mine = (where[6] + STEPS[k]) & 3
        tokens, places = [], []
        for j in range(8):
            m, n = j % 2, j // 2
            theirs = (where[7] + STEPS[n]) & 3
            tokens.append(jnp.concatenate([piece(own[k], m, theirs), piece(other[n], m, mine)], axis=0))
            z, x = jnp.where(core == 0, mine, theirs), jnp.where(core == 0, theirs, mine)
            places.append((x * 16, z * 2 + (m ^ flip)))
        part = (nn(delta, jnp.concatenate(tokens, axis=1)) / 1536.0).astype(BF)
        for j, (quarter, row) in enumerate(places):
            out[pl.ds(quarter, 16), row] = part[:, j * 128 : (j + 1) * 128].reshape(16, 16, 128)


def gradient_pieces(where, before, own, other, w, up):
    vmem = pl.BlockSpec(memory_space=pltpu.VMEM)
    return pl.pallas_call(
        gradient_kernel,
        out_shape=jax.ShapeDtypeStruct((64, 8, 16, 128), BF),
        in_specs=[pl.BlockSpec(memory_space=pltpu.SMEM)] + [vmem] * 13,
        out_specs=vmem,
        scratch_shapes=[pltpu.VMEM((256, 2 * ROWS), BF)],
        compiler_params=params(10),
        cost_estimate=cost(3 * 768 * 4096 * 256, 12 * MIB),
        name="gradient",
    )(where, before, *own, *other, w, up)


def route_kernel(source, pieces, out):
    def some(n, c):
        for k in range(16):
            at = source[n * 16 + k]
            out[n * 16 + k] = (pieces[at].astype(F32) + pieces[at + 256].astype(F32)).astype(BF)
        return c

    lax.fori_loop(0, 16, some, 0)


def route(source, pieces):
    vmem = pl.BlockSpec(memory_space=pltpu.VMEM)
    out = pl.pallas_call(
        route_kernel,
        out_shape=jax.ShapeDtypeStruct((256, 16, 128), BF),
        in_specs=[pl.BlockSpec(memory_space=pltpu.SMEM), vmem],
        out_specs=vmem,
        compiler_params=params(16),
        cost_estimate=cost(0, 3 * MIB),
        name="route",
    )(source, pieces.reshape(512, 16, 128))
    return out.reshape(64, 4, 16, 128)


def collect(core, mine, theirs, slot, grad_t):
    for quarter in range(4):
        cols = slice(quarter * 128, (quarter + 1) * 128)
        part = slice(quarter * 16, (quarter + 1) * 16)
        grad_t[pl.ds(pl.multiple_of(core * 256, 256), 256), cols] = mine[part, slot].reshape(256, 128)
        grad_t[pl.ds(pl.multiple_of(256 - core * 256, 256), 256), cols] = theirs[part, slot].reshape(256, 128)


def hand_out(where, second, keep, send, slot, full):
    full[...] = second
    mean_square = jnp.sum(second * second, keepdims=True) * (1.0 / (BLOCK * BLOCK))
    scale = lax.rsqrt(mean_square + floor_eps)
    keep[slot] = (full[pl.ds(pl.multiple_of(where[0] * 128, 128), 128)] * scale).astype(BF)
    send[slot] = (full[pl.ds(pl.multiple_of(where[3] * 128, 128), 128)] * scale).astype(BF)


def fetch_kernel(where, slot_at, roots, statistics, pairs, statistic, sem):
    loads = [pltpu.make_async_copy(roots.at[slot_at[where[4] + k]], pairs.at[k], sem.at[k]) for k in range(4)]
    loads.append(pltpu.make_async_copy(statistics.at[slot_at[where[4]]], statistic, sem.at[4]))
    for load in loads:
        load.start()
    for load in loads:
        load.wait()


def fetch(where, slot_at, roots, statistics):
    smem = pl.BlockSpec(memory_space=pltpu.SMEM)
    vmem = pl.BlockSpec(memory_space=pltpu.VMEM)
    hbm = pl.BlockSpec(memory_space=pl.ANY)
    return pl.pallas_call(
        fetch_kernel,
        out_shape=[jax.ShapeDtypeStruct((4, 2, BLOCK, BLOCK), BF), jax.ShapeDtypeStruct((2, BLOCK, BLOCK), BF)],
        in_specs=[smem, smem, hbm, hbm],
        out_specs=[vmem, vmem],
        scratch_shapes=[pltpu.SemaphoreType.DMA((5,))],
        compiler_params=params(8),
        cost_estimate=cost(0, 9 * MIB),
        name="fetch",
    )(where, slot_at, roots, statistics)


def stored_kernel(where, mine, theirs, pairs, keep, send, grad_t, full):
    for k in range(3):
        collect(where[1], mine, theirs, k + 1, grad_t.at[k])
    firsts = [nt(pairs[k + 1, 0], grad_t[k]).astype(BF) for k in range(3)]
    seconds = [nn(firsts[k], pairs[k + 1, 1]) for k in range(3)]
    for k in range(3):
        hand_out(where, seconds[k], keep, send, k, full.at[k])


def stored_slots(where, mine, theirs, pairs):
    smem = pl.BlockSpec(memory_space=pltpu.SMEM)
    vmem = pl.BlockSpec(memory_space=pltpu.VMEM)
    return pl.pallas_call(
        stored_kernel,
        out_shape=[jax.ShapeDtypeStruct((3, 128, BLOCK), BF)] * 2,
        in_specs=[smem, vmem, vmem, vmem],
        out_specs=[vmem, vmem],
        scratch_shapes=[pltpu.VMEM((3, BLOCK, BLOCK), BF), pltpu.VMEM((3, BLOCK, BLOCK), F32)],
        compiler_params=params(20),
        cost_estimate=cost(12 * BLOCK**3, 4 * MIB),
        name="stored",
    )(where, mine, theirs, pairs)


def product(a, b):
    (c, x), (d, y) = a, b
    xy = nn(x.astype(BF), y.astype(BF))
    return c * d, xy + (c * y + d * x if c and d else d * x if d else c * y)


def square(a):
    c, x = a
    x_rounded = x.astype(BF)
    return c * c, nn(x_rounded, x_rounded) + (2.0 * c) * x


def scaled_factor(power):
    return 1.25, -0.25 * power


def inverse_roots(matrices):
    eye = unit(BLOCK, F32)
    powers = [matrix / jnp.sum(matrix * eye, keepdims=True) for matrix in matrices]
    results = [scaled_factor(power) for power in powers]
    factors = results
    for sweep in range(2):
        fourths = [square(factor) for factor in factors]
        fourths = [square(fourth) for fourth in fourths]
        powers = [product(fourth, (0.0, power))[1] for fourth, power in zip(fourths, powers)]
        factors = [scaled_factor(power) for power in powers]
        results = [product(result, factor) for result, factor in zip(results, factors)]
    return [(c * eye + x).astype(BF) for c, x in results]


def refresh_kernel(where, slot_at, mine, theirs, pairs, statistic, keep, send, grad_t, full, pair):
    collect(where[1], mine, theirs, 0, grad_t)
    g_t = grad_t[...]
    pair[...] = pairs[0]

    @pl.when(slot_at[8] > where[4] // 4)
    def _():
        eye = unit(BLOCK, F32)
        g = nt(unit(BLOCK, BF), g_t).astype(BF)
        outers = [nt(g, g), nt(g_t, g_t)]
        matrices = [decay * statistic[k].astype(F32) + outers[k] + jitter * eye for k in range(2)]
        pair[0], pair[1] = inverse_roots(matrices)

    first = nt(pair[0], g_t).astype(BF)
    hand_out(where, nn(first, pair[1]), keep, send, 0, full)


def refresh(where, slot_at, mine, theirs, pairs, statistic):
    smem = pl.BlockSpec(memory_space=pltpu.SMEM)
    vmem = pl.BlockSpec(memory_space=pltpu.VMEM)
    return pl.pallas_call(
        refresh_kernel,
        out_shape=[jax.ShapeDtypeStruct((1, 128, BLOCK), BF)] * 2,
        in_specs=[smem, smem] + [vmem] * 4,
        out_specs=[vmem, vmem],
        scratch_shapes=[
            pltpu.VMEM((BLOCK, BLOCK), BF),
            pltpu.VMEM((BLOCK, BLOCK), F32),
            pltpu.VMEM((2, BLOCK, BLOCK), BF),
        ],
        compiler_params=params(32),
        cost_estimate=cost(42 * BLOCK**3, 4 * MIB),
        name="refresh",
    )(where, slot_at, mine, theirs, pairs, statistic)


def assemble_kernel(where, slot_at, fresh_mine, mine, theirs, out):
    here = where[4]
    there = 4 - here
    out[slot_at[here]] = fresh_mine[0]
    for k in range(3):
        out[slot_at[here + k + 1]] = mine[k]
        out[slot_at[there + k + 1]] = theirs[k]


def assemble(where, slot_at, *parts):
    smem = pl.BlockSpec(memory_space=pltpu.SMEM)
    vmem = pl.BlockSpec(memory_space=pltpu.VMEM)
    return pl.pallas_call(
        assemble_kernel,
        out_shape=jax.ShapeDtypeStruct((8, 128, BLOCK), BF),
        in_specs=[smem, smem] + [vmem] * 3,
        out_specs=vmem,
        compiler_params=params(16),
        cost_estimate=cost(0, 2 * MIB),
        name="assemble",
    )(where, slot_at, *parts)


def shards(tokens, in_weight, upstream, slot_block, refreshed, statistics, roots):
    group = lax.axis_index("grp")
    core = group % 2
    chip = group // 2
    both = ("grp", "dev")
    place_z = lax.axis_index("dev") // 8
    place_x = lax.axis_index("dev") % 4
    flip = (lax.axis_index("dev") // 4) % 2 ^ chip
    where = [group, core, group + 1 - 2 * core, group + 2 - 4 * chip, 4 * chip, flip]
    where += [jnp.where(core == 0, place_z, place_x), jnp.where(core == 0, place_x, place_z)]
    where = jnp.stack(where).astype(jnp.int32)

    first = prepare(where, tokens, slot_block)
    first = lax.all_to_all(first, both, 0, 0, tiled=True, axis_index_groups=STAGE1)
    w, up = half_of_weights(where, in_weight, upstream)
    below = lax.ppermute(first, both, UP)
    above = lax.ppermute(first, both, DOWN)
    own = [first, below, above]
    shared, w = lax.optimization_barrier((first, w))
    other = [lax.ppermute(shared, "grp", CORE)]
    acc = forward(STEPS[:1], where, [own[0], other[0]], w)
    below, above, acc = lax.optimization_barrier((below, above, acc))
    own += [lax.ppermute(below[:4], both, UP), lax.ppermute(above[4:], both, DOWN)]
    other += [lax.ppermute(below, "grp", CORE), lax.ppermute(above, "grp", CORE)]
    acc = forward(STEPS[1:3], where, own[1:3] + other[1:3], w, acc)
    acc, *own[3:] = lax.optimization_barrier((acc, *own[3:]))
    other += [lax.ppermute(part, "grp", CORE) for part in own[3:]]
    all_ids = jnp.concatenate([part[:, ROWS, :8] for part in own]).astype(jnp.int32).reshape(256)
    pieces = gradient_pieces(where, acc, own, other, w, up)
    pieces = lax.all_to_all(pieces, both, 0, 0, tiled=True, axis_index_groups=SAME_CORE)
    source, slot_at = slot_order(where, all_ids, refreshed, slot_block)
    pairs, statistic = fetch(where, slot_at, roots, statistics)
    source, pairs, statistic = lax.optimization_barrier((source, pairs, statistic))
    pieces = route(source, pieces)
    mine = lax.all_to_all(pieces, both, 0, 0, tiled=True, axis_index_groups=SAME_CORE)
    theirs = lax.ppermute(mine, "grp", CORE)

    keep, send = stored_slots(where, mine, theirs, pairs)
    other_keep = lax.ppermute(send, "grp", CHIP)
    mine, theirs, keep = lax.optimization_barrier((mine, theirs, keep))
    fresh_keep, fresh_send = refresh(where, slot_at, mine, theirs, pairs, statistic)
    fresh_other = lax.ppermute(fresh_send, "grp", CHIP)
    update = assemble(where, slot_at, fresh_keep, keep, other_keep)
    return lax.dynamic_update_slice_in_dim(update, fresh_other, slot_at[4 - 4 * chip], 0)


def solution(mesh):
    return jax.shard_map(
        shards,
        mesh=mesh,
        in_specs=(
            P(None, "dev"),
            P(None, "dev"),
            P(None, "dev"),
            P("dev"),
            P(),
            P("dev", None, None, None),
            P("dev", None, None, None),
        ),
        out_specs=P("dev", "grp", None),
        check_vma=False,
    )
```

```python
import functools

import jax
import jax.numpy as jnp
from jax import lax
from jax.experimental import pallas as pl
from jax.experimental.pallas import tpu as pltpu
from jax.sharding import PartitionSpec as P

decay = 0.9
jitter = 1e-06
floor_eps = 1e-06

ROWS = 384
IDS = 16
BLOCK = 512
BF = jnp.bfloat16
F32 = jnp.float32
MIB = 1 << 20

CORE = [(0, 1), (1, 0), (2, 3), (3, 2)]
CHIP = [(0, 2), (2, 0), (1, 3), (3, 1)]
def device(chip, core, z, y_hi, x):
    return (chip * 2 + core) * 32 + z * 8 + y_hi * 4 + x


def on_rings(chip, core, y_hi, first, second):
    return device(chip, core, second, y_hi, first) if core == 0 else device(chip, core, first, y_hi, second)


STAGE1 = [
    [on_rings(m, core, m ^ flip, i, a) for m in range(2) for i in range(4)]
    for core in range(2)
    for a in range(4)
    for flip in range(2)
]
EVERYWHERE = [
    (chip, core, z, y_hi, x)
    for chip in range(2)
    for core in range(2)
    for z in range(4)
    for y_hi in range(2)
    for x in range(4)
]


def along(step):
    return [
        (
            device(chip, core, z, y_hi, x),
            device(chip, core, z, y_hi, (x + step) % 4) if core else device(chip, core, (z + step) % 4, y_hi, x),
        )
        for chip, core, z, y_hi, x in EVERYWHERE
    ]


UP, DOWN = along(1), along(-1)
STEPS = (0, -1, 1, 2)
SAME_CORE = [[chip * 64 + core * 32 + d for chip in range(2) for d in range(32)] for core in range(2)]


def params(mib):
    return pltpu.CompilerParams(vmem_limit_bytes=mib * MIB)


def cost(flops, nbytes):
    return pl.CostEstimate(flops=flops, bytes_accessed=nbytes, transcendentals=0)


def in_hbm(*arrays):
    return [pltpu.with_memory_space_constraint(array, pltpu.HBM) for array in arrays]


def nt(a, b):
    return lax.dot_general(a, b, (((1,), (1,)), ((), ())), preferred_element_type=F32)


def nn(a, b):
    return jnp.dot(a, b, preferred_element_type=F32)


def whereabouts():
    group, d = lax.axis_index("grp"), lax.axis_index("dev")
    core, chip = group & 1, group >> 1
    z, y_hi, x = d >> 3, (d >> 2) & 1, d & 3
    places = [jnp.where(core == 0, z, x), jnp.where(core == 0, x, z)]
    return [group, core, group ^ 1, group ^ 2, 4 * chip, y_hi ^ chip, *places]


def unit(n, dtype):
    row = lax.broadcasted_iota(jnp.int32, (n, n), 0)
    col = lax.broadcasted_iota(jnp.int32, (n, n), 1)
    return jnp.where(row == col, 1.0, 0.0).astype(dtype)


def gelu_slope(values):
    return (
        0.5 * (1.0 + lax.erf(values * 0.7071067811865476))
        + values * jnp.exp(-0.5 * values * values) * 0.3989422804014327
    )


def spare_position(k):
    return jnp.where(k < 3, 7 - k, jnp.where(k < 6, 6 - k, jnp.where(k == 6, 4, 0)))


def place(flag, fresh_seen, spare_seen):
    return jnp.minimum(jnp.where(flag == 1, 4 * fresh_seen, spare_position(spare_seen)), 7)


def order_kernel(ids, refreshed, slot_block, source, slot_at, table):
    where = whereabouts()

    def clear(k, c):
        table[k] = 0
        return c

    def mark(k, c):
        table[refreshed[k]] = 1
        return c

    lax.fori_loop(0, 256, clear, 0, unroll=8)
    lax.fori_loop(0, 32, mark, 0, unroll=8)

    def positions(blocks):
        flags = [table[block] for block in blocks]
        fresh_seen = jnp.int32(0)
        spare_seen = jnp.int32(0)
        found = []
        for flag in flags:
            found.append(place(flag, fresh_seen, spare_seen))
            fresh_seen += flag
            spare_seen += 1 - flag
        return found, fresh_seen

    def owner(o, c):
        z, y_hi, x = o >> 3, (o >> 2) & 1, o & 3
        across = jnp.where(where[1] == 0, z, x)
        inner = jnp.where(where[1] == 0, x, z)
        step = (across - where[6]) & 3
        group = jnp.where(step == 0, 0, jnp.where(step == 3, 1, step + 1))
        piece = group * 8 + (y_hi ^ where[5]) * 4 + inner
        blocks = [ids[piece, p] for p in range(8)]
        found, _ = positions(blocks)
        for block, position in zip(blocks, found):
            source[(position >> 2) * 128 + o * 4 + (position & 3)] = (block & 31) * 8 + (block >> 5)
        return c

    lax.fori_loop(0, 32, owner, 0)
    found, fresh_seen = positions([slot_block[p] for p in range(8)])
    for p in range(8):
        slot_at[found[p]] = p
    slot_at[8] = fresh_seen


def slot_order(ids, refreshed, slot_block):
    smem = pl.BlockSpec(memory_space=pltpu.SMEM)
    return pl.pallas_call(
        order_kernel,
        out_shape=[jax.ShapeDtypeStruct((256,), jnp.int32), jax.ShapeDtypeStruct((16,), jnp.int32)],
        in_specs=[smem] * 3,
        out_specs=[smem] * 2,
        scratch_shapes=[pltpu.SMEM((256,), jnp.int32)],
        cost_estimate=cost(0, 4096),
        name="order",
    )(ids, refreshed, slot_block)


def prepare_kernel(tokens, slot_block, out, ids, sem, id_sem):
    where = whereabouts()
    load_ids = pltpu.make_async_copy(slot_block, ids, id_sem)
    load_ids.start()
    loads = []
    for m in range(2):
        rows = pl.ds(pl.multiple_of((2 * m + where[1]) * ROWS, ROWS), ROWS)
        for i in range(4):
            k = 4 * m + i
            loads.append(pltpu.make_async_copy(tokens.at[rows], out.at[k, pl.ds(0, ROWS)], sem.at[k]))
    for load in loads:
        load.start()
    row = lax.broadcasted_iota(jnp.int32, (IDS, 128), 0)
    lane = lax.broadcasted_iota(jnp.int32, (IDS, 128), 1)
    tile = jnp.zeros((IDS, 128), jnp.int32)
    load_ids.wait()
    for p in range(8):
        tile = jnp.where((row == 0) & (lane == p), ids[p], tile)
    tile = tile.astype(F32).astype(BF)
    for k in range(8):
        out[k, ROWS:] = tile
    for load in loads:
        load.wait()


def prepare(tokens, slot_block):
    hbm = pl.BlockSpec(memory_space=pl.ANY)
    return pl.pallas_call(
        prepare_kernel,
        out_shape=jax.ShapeDtypeStruct((8, ROWS + IDS, 128), BF),
        in_specs=[hbm, hbm],
        out_specs=pl.BlockSpec(memory_space=pltpu.VMEM),
        scratch_shapes=[pltpu.SMEM((8,), jnp.int32), pltpu.SemaphoreType.DMA((8,)), pltpu.SemaphoreType.DMA],
        compiler_params=params(8),
        cost_estimate=cost(0, MIB),
        name="prepare",
    )(*in_hbm(tokens, slot_block))


def weights_kernel(weight, upstream, w, up, sem):
    where = whereabouts()
    cols = pl.ds(pl.multiple_of(where[1] * 256, 256), 256)
    loads = [pltpu.make_async_copy(weight.at[:, cols], w, sem.at[2])]
    for k in range(2):
        rows = pl.ds(pl.multiple_of(where[2 * k] * ROWS, ROWS), ROWS)
        loads.append(pltpu.make_async_copy(upstream.at[rows, cols], up.at[k], sem.at[k]))
    for load in loads:
        load.start()
    for load in loads:
        load.wait()


def half_of_weights(in_weight, upstream):
    vmem = pl.BlockSpec(memory_space=pltpu.VMEM)
    hbm = pl.BlockSpec(memory_space=pl.ANY)
    return pl.pallas_call(
        weights_kernel,
        out_shape=[jax.ShapeDtypeStruct((4096, 256), BF), jax.ShapeDtypeStruct((2, ROWS, 256), BF)],
        in_specs=[hbm, hbm],
        out_specs=[vmem, vmem],
        scratch_shapes=[pltpu.SemaphoreType.DMA((3,))],
        compiler_params=params(4),
        cost_estimate=cost(0, 5 * MIB),
        name="weights",
    )(*in_hbm(in_weight, upstream))


def piece(group, m, i):
    return group[0][m * 4 + i, :ROWS] if len(group) == 1 else group[m][i, :ROWS]


def group_product(group, w, core, across, flip):
    tokens = jnp.concatenate([piece(group, j // 4, j % 4) for j in range(8)], axis=1)
    weights = []
    for j in range(8):
        row = jnp.where(core == 0, across * 1024 + j % 4 * 128, j % 4 * 1024 + across * 128) + ((j // 4) ^ flip) * 512
        weights.append(w[pl.ds(pl.multiple_of(row, 128), 128)])
    return nn(tokens, jnp.concatenate(weights, axis=0))


def forward_kernel(steps, before, *refs):
    where = whereabouts()
    count = len(steps)
    w, acc = refs[2 * count], refs[2 * count + 1]
    for half in range(2):
        core = where[1] if half == 0 else 1 - where[1]
        total = before[half] if before is not None else None
        for k, step in enumerate(steps):
            part = group_product([refs[half * count + k]], w, core, (where[6 + half] + step) & 3, where[5])
            total = part if total is None else total + part
        acc[half] = total


def forward(steps, groups, w, before=None):
    vmem = pl.BlockSpec(memory_space=pltpu.VMEM)
    if before is None:
        kernel = functools.partial(forward_kernel, steps, None)
        operands = [*groups, w]
    else:
        kernel = functools.partial(forward_kernel, steps)
        operands = [before, *groups, w]
    return pl.pallas_call(
        kernel,
        out_shape=jax.ShapeDtypeStruct((2, ROWS, 256), F32),
        in_specs=[vmem] * len(operands),
        out_specs=vmem,
        compiler_params=params(8),
        cost_estimate=cost(2 * ROWS * 1024 * 256 * len(groups), 2 * MIB),
        name="forward",
    )(*operands)


def gradient_kernel(before, *refs):
    where = whereabouts()
    own = [refs[0:1], refs[1:2], refs[2:3], refs[3:5]]
    other = [refs[5:6], refs[6:7], refs[7:8], refs[8:10]]
    w, up, out, ids, delta_t, made, sem = refs[10:]
    core, flip = where[1], where[5]
    eye = unit(256, BF)
    for half, group in ((0, own[3]), (1, other[3])):
        last = group_product(group, w, core if half == 0 else 1 - core, (where[6 + half] + STEPS[3]) & 3, flip)
        delta = (up[half].astype(F32) * gelu_slope(before[half] + last)).astype(BF)
        delta_t[:, half * ROWS : (half + 1) * ROWS] = nt(eye, delta).astype(BF)
    for k, group in enumerate(own):
        for j in range(8):
            ref, at = (group[0], j) if len(group) == 1 else (group[j // 4], j % 4)
            rows = ref[at, ROWS:].astype(F32).astype(jnp.int32)
            ids[k * 8 + j : k * 8 + j + 1] = rows[:1]
    delta = delta_t[...]
    sends = []
    for k in range(4):
        mine = (where[6] + STEPS[k]) & 3
        tokens, places = [], []
        for j in range(8):
            m, n = j % 2, j // 2
            theirs = (where[7] + STEPS[n]) & 3
            tokens.append(jnp.concatenate([piece(own[k], m, theirs), piece(other[n], m, mine)], axis=0))
            z, x = jnp.where(core == 0, mine, theirs), jnp.where(core == 0, theirs, mine)
            places.append((x * 16, z * 2 + (m ^ flip)))
        part = (nn(delta, jnp.concatenate(tokens, axis=1)) / 1536.0).astype(BF)
        for j, (quarter, row) in enumerate(places):
            made[k, j] = part[:, j * 128 : (j + 1) * 128].reshape(16, 16, 128)
            sends.append(pltpu.make_async_copy(made.at[k, j], out.at[pl.ds(quarter, 16), row], sem.at[k, j]))
            sends[-1].start()
    for send in sends:
        send.wait()


def gradient_pieces(before, own, other, w, up):
    vmem = pl.BlockSpec(memory_space=pltpu.VMEM)
    return pl.pallas_call(
        gradient_kernel,
        out_shape=[pltpu.HBM((64, 8, 16, 128), BF), jax.ShapeDtypeStruct((32, 128), jnp.int32)],
        in_specs=[vmem] * 13,
        out_specs=[pl.BlockSpec(memory_space=pltpu.HBM), vmem],
        scratch_shapes=[
            pltpu.VMEM((256, 2 * ROWS), BF),
            pltpu.VMEM((4, 8, 16, 16, 128), BF),
            pltpu.SemaphoreType.DMA((4, 8)),
        ],
        compiler_params=params(10),
        cost_estimate=cost(3 * 768 * 4096 * 256, 12 * MIB),
        name="gradient",
    )(before, *own, *other, w, up)


def route_kernel(source, pieces, out):
    def some(n, c):
        for k in range(16):
            at = source[n * 16 + k]
            out[n * 16 + k] = (pieces[at].astype(F32) + pieces[at + 256].astype(F32)).astype(BF)
        return c

    lax.fori_loop(0, 16, some, 0)


def route(source, pieces):
    vmem = pl.BlockSpec(memory_space=pltpu.VMEM)
    out = pl.pallas_call(
        route_kernel,
        out_shape=jax.ShapeDtypeStruct((256, 16, 128), BF),
        in_specs=[pl.BlockSpec(memory_space=pltpu.SMEM), vmem],
        out_specs=vmem,
        compiler_params=params(16),
        cost_estimate=cost(0, 3 * MIB),
        name="route",
    )(source, pieces.reshape(512, 16, 128))
    return out.reshape(64, 4, 16, 128)


def collect(core, mine, theirs, slot, grad_t):
    for quarter in range(4):
        cols = slice(quarter * 128, (quarter + 1) * 128)
        part = slice(quarter * 16, (quarter + 1) * 16)
        grad_t[pl.ds(pl.multiple_of(core * 256, 256), 256), cols] = mine[part, slot].reshape(256, 128)
        grad_t[pl.ds(pl.multiple_of(256 - core * 256, 256), 256), cols] = theirs[part, slot].reshape(256, 128)


def hand_out(where, second, keep, send, slot, full):
    full[...] = second
    mean_square = jnp.sum(second * second, keepdims=True) * (1.0 / (BLOCK * BLOCK))
    scale = lax.rsqrt(mean_square + floor_eps)
    keep[slot] = (full[pl.ds(pl.multiple_of(where[0] * 128, 128), 128)] * scale).astype(BF)
    send[slot] = (full[pl.ds(pl.multiple_of(where[3] * 128, 128), 128)] * scale).astype(BF)


def fetch_kernel(slot_at, roots, statistics, pairs, statistic, sem):
    where = whereabouts()
    loads = [pltpu.make_async_copy(roots.at[slot_at[where[4] + k]], pairs.at[k], sem.at[k]) for k in range(4)]
    loads.append(pltpu.make_async_copy(statistics.at[slot_at[where[4]]], statistic, sem.at[4]))
    for load in loads:
        load.start()
    for load in loads:
        load.wait()


def fetch(slot_at, roots, statistics):
    smem = pl.BlockSpec(memory_space=pltpu.SMEM)
    vmem = pl.BlockSpec(memory_space=pltpu.VMEM)
    hbm = pl.BlockSpec(memory_space=pl.ANY)
    return pl.pallas_call(
        fetch_kernel,
        out_shape=[jax.ShapeDtypeStruct((4, 2, BLOCK, BLOCK), BF), jax.ShapeDtypeStruct((2, BLOCK, BLOCK), BF)],
        in_specs=[smem, hbm, hbm],
        out_specs=[vmem, vmem],
        scratch_shapes=[pltpu.SemaphoreType.DMA((5,))],
        compiler_params=params(8),
        cost_estimate=cost(0, 9 * MIB),
        name="fetch",
    )(slot_at, *in_hbm(roots, statistics))


def stored_kernel(mine, theirs, pairs, keep, send, grad_t, full):
    where = whereabouts()
    for k in range(3):
        collect(where[1], mine, theirs, k + 1, grad_t.at[k])
    firsts = [nt(pairs[k + 1, 0], grad_t[k]).astype(BF) for k in range(3)]
    seconds = [nn(firsts[k], pairs[k + 1, 1]) for k in range(3)]
    for k in range(3):
        hand_out(where, seconds[k], keep, send, k, full.at[k])


def stored_slots(mine, theirs, pairs):
    vmem = pl.BlockSpec(memory_space=pltpu.VMEM)
    return pl.pallas_call(
        stored_kernel,
        out_shape=[jax.ShapeDtypeStruct((3, 128, BLOCK), BF)] * 2,
        in_specs=[vmem] * 3,
        out_specs=[vmem, vmem],
        scratch_shapes=[pltpu.VMEM((3, BLOCK, BLOCK), BF), pltpu.VMEM((3, BLOCK, BLOCK), F32)],
        compiler_params=params(20),
        cost_estimate=cost(12 * BLOCK**3, 4 * MIB),
        name="stored",
    )(mine, theirs, pairs)


def product(a, b):
    (c, x), (d, y) = a, b
    xy = nn(x.astype(BF), y.astype(BF))
    return c * d, xy + (c * y + d * x if c and d else d * x if d else c * y)


def square(a):
    c, x = a
    x_rounded = x.astype(BF)
    return c * c, nn(x_rounded, x_rounded) + (2.0 * c) * x


def scaled_factor(power):
    return 1.25, -0.25 * power


def inverse_roots(matrices):
    eye = unit(BLOCK, F32)
    powers = [matrix / jnp.sum(matrix * eye, keepdims=True) for matrix in matrices]
    results = [scaled_factor(power) for power in powers]
    factors = results
    for sweep in range(2):
        fourths = [square(factor) for factor in factors]
        fourths = [square(fourth) for fourth in fourths]
        powers = [product(fourth, (0.0, power))[1] for fourth, power in zip(fourths, powers)]
        factors = [scaled_factor(power) for power in powers]
        results = [product(result, factor) for result, factor in zip(results, factors)]
    return [(c * eye + x).astype(BF) for c, x in results]


def refresh_kernel(slot_at, mine, theirs, pairs, statistic, keep, send, grad_t, full, pair):
    where = whereabouts()
    collect(where[1], mine, theirs, 0, grad_t)
    g_t = grad_t[...]
    pair[...] = pairs[0]

    @pl.when(slot_at[8] > where[4] // 4)
    def _():
        eye = unit(BLOCK, F32)
        g = nt(unit(BLOCK, BF), g_t).astype(BF)
        outers = [nt(g, g), nt(g_t, g_t)]
        matrices = [decay * statistic[k].astype(F32) + outers[k] + jitter * eye for k in range(2)]
        pair[0], pair[1] = inverse_roots(matrices)

    first = nt(pair[0], g_t).astype(BF)
    hand_out(where, nn(first, pair[1]), keep, send, 0, full)


def refresh(slot_at, mine, theirs, pairs, statistic):
    smem = pl.BlockSpec(memory_space=pltpu.SMEM)
    vmem = pl.BlockSpec(memory_space=pltpu.VMEM)
    return pl.pallas_call(
        refresh_kernel,
        out_shape=[jax.ShapeDtypeStruct((1, 128, BLOCK), BF)] * 2,
        in_specs=[smem] + [vmem] * 4,
        out_specs=[vmem, vmem],
        scratch_shapes=[
            pltpu.VMEM((BLOCK, BLOCK), BF),
            pltpu.VMEM((BLOCK, BLOCK), F32),
            pltpu.VMEM((2, BLOCK, BLOCK), BF),
        ],
        compiler_params=params(32),
        cost_estimate=cost(42 * BLOCK**3, 4 * MIB),
        name="refresh",
    )(slot_at, mine, theirs, pairs, statistic)


def assemble_kernel(slot_at, fresh_mine, mine, theirs, out):
    here = whereabouts()[4]
    there = 4 - here
    out[slot_at[here]] = fresh_mine[0]
    for k in range(3):
        out[slot_at[here + k + 1]] = mine[k]
        out[slot_at[there + k + 1]] = theirs[k]


def assemble(slot_at, *parts):
    smem = pl.BlockSpec(memory_space=pltpu.SMEM)
    vmem = pl.BlockSpec(memory_space=pltpu.VMEM)
    return pl.pallas_call(
        assemble_kernel,
        out_shape=jax.ShapeDtypeStruct((8, 128, BLOCK), BF),
        in_specs=[smem] + [vmem] * 3,
        out_specs=vmem,
        compiler_params=params(16),
        cost_estimate=cost(0, 2 * MIB),
        name="assemble",
    )(slot_at, *parts)


def shards(tokens, in_weight, upstream, slot_block, refreshed, statistics, roots):
    group = lax.axis_index("grp")
    chip = group // 2
    both = ("grp", "dev")

    first = prepare(tokens, slot_block)
    first = lax.all_to_all(first, both, 0, 0, tiled=True, axis_index_groups=STAGE1)
    w, up = half_of_weights(in_weight, upstream)
    below = lax.ppermute(first, both, UP)
    above = lax.ppermute(first, both, DOWN)
    own = [first, below, above]
    below, above, w = lax.optimization_barrier((below, above, w))
    own[1:] = [below, above]
    own += [lax.ppermute(below[:4], both, UP), lax.ppermute(above[4:], both, DOWN)]
    shared, _ = lax.optimization_barrier((first, below))
    other = [lax.ppermute(group_of, "grp", CORE) for group_of in (shared, below, above)]
    acc = forward(STEPS[:3], own[:3] + other[:3], w)
    acc, *own[3:] = lax.optimization_barrier((acc, *own[3:]))
    other += [lax.ppermute(part, "grp", CORE) for part in own[3:]]
    pieces, all_ids = gradient_pieces(acc, own, other, w, up)
    pieces = lax.all_to_all(pieces, both, 0, 0, tiled=True, axis_index_groups=SAME_CORE)
    source, slot_at = slot_order(all_ids, refreshed, slot_block)
    pairs, statistic = fetch(slot_at, roots, statistics)
    source, pairs, statistic = lax.optimization_barrier((source, pairs, statistic))
    pieces = route(source, pieces)
    mine = lax.all_to_all(pieces, both, 0, 0, tiled=True, axis_index_groups=SAME_CORE)
    theirs = lax.ppermute(mine, "grp", CORE)

    keep, send = stored_slots(mine, theirs, pairs)
    other_keep = lax.ppermute(send, "grp", CHIP)
    mine, theirs, keep = lax.optimization_barrier((mine, theirs, keep))
    fresh_keep, fresh_send = refresh(slot_at, mine, theirs, pairs, statistic)
    fresh_other = lax.ppermute(fresh_send, "grp", CHIP)
    update = assemble(slot_at, fresh_keep, keep, other_keep)
    return lax.dynamic_update_slice_in_dim(update, fresh_other, slot_at[4 - 4 * chip], 0)


def solution(mesh):
    return jax.shard_map(
        shards,
        mesh=mesh,
        in_specs=(
            P(None, "dev"),
            P(None, "dev"),
            P(None, "dev"),
            P("dev"),
            P(),
            P("dev", None, None, None),
            P("dev", None, None, None),
        ),
        out_specs=P("dev", "grp", None),
        check_vma=False,
    )
```

```python
import functools

import jax
import jax.numpy as jnp
from jax import lax
from jax.experimental import pallas as pl
from jax.experimental.pallas import tpu as pltpu
from jax.sharding import PartitionSpec as P

decay = 0.9
jitter = 1e-06
floor_eps = 1e-06

ROWS = 384
IDS = 16
BLOCK = 512
BF = jnp.bfloat16
F32 = jnp.float32
MIB = 1 << 20

CORE = [(0, 1), (1, 0), (2, 3), (3, 2)]
CHIP = [(0, 2), (2, 0), (1, 3), (3, 1)]
def device(chip, core, z, y_hi, x):
    return (chip * 2 + core) * 32 + z * 8 + y_hi * 4 + x


def on_rings(chip, core, y_hi, first, second):
    return device(chip, core, second, y_hi, first) if core == 0 else device(chip, core, first, y_hi, second)


STAGE1 = [
    [on_rings(m, core, m ^ flip, i, a) for m in range(2) for i in range(4)]
    for core in range(2)
    for a in range(4)
    for flip in range(2)
]
EVERYWHERE = [
    (chip, core, z, y_hi, x)
    for chip in range(2)
    for core in range(2)
    for z in range(4)
    for y_hi in range(2)
    for x in range(4)
]


def along(step):
    return [
        (
            device(chip, core, z, y_hi, x),
            device(chip, core, z, y_hi, (x + step) % 4) if core else device(chip, core, (z + step) % 4, y_hi, x),
        )
        for chip, core, z, y_hi, x in EVERYWHERE
    ]


UP, DOWN = along(1), along(-1)
STEPS = (0, -1, 1, 2)
SAME_CORE = [[chip * 64 + core * 32 + d for chip in range(2) for d in range(32)] for core in range(2)]


def params(mib):
    return pltpu.CompilerParams(vmem_limit_bytes=mib * MIB)


def cost(flops, nbytes):
    return pl.CostEstimate(flops=flops, bytes_accessed=nbytes, transcendentals=0)


def in_hbm(*arrays):
    return [pltpu.with_memory_space_constraint(array, pltpu.HBM) for array in arrays]


def nt(a, b):
    return lax.dot_general(a, b, (((1,), (1,)), ((), ())), preferred_element_type=F32)


def nn(a, b):
    return jnp.dot(a, b, preferred_element_type=F32)


def whereabouts():
    group, d = lax.axis_index("grp"), lax.axis_index("dev")
    core, chip = group & 1, group >> 1
    z, y_hi, x = d >> 3, (d >> 2) & 1, d & 3
    places = [jnp.where(core == 0, z, x), jnp.where(core == 0, x, z)]
    return [group, core, group ^ 1, group ^ 2, 4 * chip, y_hi ^ chip, *places]


def unit(n, dtype):
    row = lax.broadcasted_iota(jnp.int32, (n, n), 0)
    col = lax.broadcasted_iota(jnp.int32, (n, n), 1)
    return jnp.where(row == col, 1.0, 0.0).astype(dtype)


def gelu_slope(values):
    return (
        0.5 * (1.0 + lax.erf(values * 0.7071067811865476))
        + values * jnp.exp(-0.5 * values * values) * 0.3989422804014327
    )


def spare_position(k):
    return jnp.where(k < 3, 7 - k, jnp.where(k < 6, 6 - k, jnp.where(k == 6, 4, 0)))


def place(flag, fresh_seen, spare_seen):
    return jnp.minimum(jnp.where(flag == 1, 4 * fresh_seen, spare_position(spare_seen)), 7)


def order_kernel(ids, refreshed, slot_block, source, slot_at, table):
    where = whereabouts()

    def clear(k, c):
        table[k] = 0
        return c

    def mark(k, c):
        table[refreshed[k]] = 1
        return c

    lax.fori_loop(0, 256, clear, 0, unroll=8)
    lax.fori_loop(0, 32, mark, 0, unroll=8)

    def positions(blocks):
        flags = [table[block] for block in blocks]
        fresh_seen = jnp.int32(0)
        spare_seen = jnp.int32(0)
        found = []
        for flag in flags:
            found.append(place(flag, fresh_seen, spare_seen))
            fresh_seen += flag
            spare_seen += 1 - flag
        return found, fresh_seen

    def owner(o, c):
        z, y_hi, x = o >> 3, (o >> 2) & 1, o & 3
        across = jnp.where(where[1] == 0, z, x)
        inner = jnp.where(where[1] == 0, x, z)
        step = (across - where[6]) & 3
        group = jnp.where(step == 0, 0, jnp.where(step == 3, 1, step + 1))
        piece = group * 8 + (y_hi ^ where[5]) * 4 + inner
        blocks = [ids[piece, p] for p in range(8)]
        found, _ = positions(blocks)
        for block, position in zip(blocks, found):
            source[(position >> 2) * 128 + o * 4 + (position & 3)] = (block & 31) * 8 + (block >> 5)
        return c

    lax.fori_loop(0, 32, owner, 0)
    found, fresh_seen = positions([slot_block[p] for p in range(8)])
    for p in range(8):
        slot_at[found[p]] = p
    slot_at[8] = fresh_seen


def slot_order(ids, refreshed, slot_block):
    smem = pl.BlockSpec(memory_space=pltpu.SMEM)
    return pl.pallas_call(
        order_kernel,
        out_shape=[jax.ShapeDtypeStruct((256,), jnp.int32), jax.ShapeDtypeStruct((16,), jnp.int32)],
        in_specs=[smem] * 3,
        out_specs=[smem] * 2,
        scratch_shapes=[pltpu.SMEM((256,), jnp.int32)],
        cost_estimate=cost(0, 4096),
        name="order",
    )(ids, refreshed, slot_block)


def prepare_kernel(tokens, slot_block, out, ids, sem, id_sem):
    where = whereabouts()
    load_ids = pltpu.make_async_copy(slot_block, ids, id_sem)
    load_ids.start()
    loads = []
    for m in range(2):
        rows = pl.ds(pl.multiple_of((2 * m + where[1]) * ROWS, ROWS), ROWS)
        for i in range(4):
            k = 4 * m + i
            loads.append(pltpu.make_async_copy(tokens.at[rows], out.at[k, pl.ds(0, ROWS)], sem.at[k]))
    for load in loads:
        load.start()
    row = lax.broadcasted_iota(jnp.int32, (IDS, 128), 0)
    lane = lax.broadcasted_iota(jnp.int32, (IDS, 128), 1)
    tile = jnp.zeros((IDS, 128), jnp.int32)
    load_ids.wait()
    for p in range(8):
        tile = jnp.where((row == 0) & (lane == p), ids[p], tile)
    tile = tile.astype(F32).astype(BF)
    for k in range(8):
        out[k, ROWS:] = tile
    for load in loads:
        load.wait()


def prepare(tokens, slot_block):
    hbm = pl.BlockSpec(memory_space=pl.ANY)
    return pl.pallas_call(
        prepare_kernel,
        out_shape=jax.ShapeDtypeStruct((8, ROWS + IDS, 128), BF),
        in_specs=[hbm, hbm],
        out_specs=pl.BlockSpec(memory_space=pltpu.VMEM),
        scratch_shapes=[pltpu.SMEM((8,), jnp.int32), pltpu.SemaphoreType.DMA((8,)), pltpu.SemaphoreType.DMA],
        compiler_params=params(8),
        cost_estimate=cost(0, MIB),
        name="prepare",
    )(*in_hbm(tokens, slot_block))


def weights_kernel(weight, upstream, w, up, sem):
    where = whereabouts()
    cols = pl.ds(pl.multiple_of(where[1] * 256, 256), 256)
    loads = [pltpu.make_async_copy(weight.at[:, cols], w, sem.at[2])]
    for k in range(2):
        rows = pl.ds(pl.multiple_of(where[2 * k] * ROWS, ROWS), ROWS)
        loads.append(pltpu.make_async_copy(upstream.at[rows, cols], up.at[k], sem.at[k]))
    for load in loads:
        load.start()
    for load in loads:
        load.wait()


def half_of_weights(in_weight, upstream):
    vmem = pl.BlockSpec(memory_space=pltpu.VMEM)
    hbm = pl.BlockSpec(memory_space=pl.ANY)
    return pl.pallas_call(
        weights_kernel,
        out_shape=[jax.ShapeDtypeStruct((4096, 256), BF), jax.ShapeDtypeStruct((2, ROWS, 256), BF)],
        in_specs=[hbm, hbm],
        out_specs=[vmem, vmem],
        scratch_shapes=[pltpu.SemaphoreType.DMA((3,))],
        compiler_params=params(4),
        cost_estimate=cost(0, 5 * MIB),
        name="weights",
    )(*in_hbm(in_weight, upstream))


def piece(group, m, i):
    return group[0][m * 4 + i, :ROWS] if len(group) == 1 else group[m][i, :ROWS]


def group_product(group, w, core, across, flip):
    tokens = jnp.concatenate([piece(group, j // 4, j % 4) for j in range(8)], axis=1)
    weights = []
    for j in range(8):
        row = jnp.where(core == 0, across * 1024 + j % 4 * 128, j % 4 * 1024 + across * 128) + ((j // 4) ^ flip) * 512
        weights.append(w[pl.ds(pl.multiple_of(row, 128), 128)])
    return nn(tokens, jnp.concatenate(weights, axis=0))


def first_kernel(first, w, acc):
    where = whereabouts()
    acc[...] = group_product([first], w, where[1], where[6], where[5])


def first_of_own(first, w):
    vmem = pl.BlockSpec(memory_space=pltpu.VMEM)
    return pl.pallas_call(
        first_kernel,
        out_shape=jax.ShapeDtypeStruct((ROWS, 256), F32),
        in_specs=[vmem] * 2,
        out_specs=vmem,
        compiler_params=params(8),
        cost_estimate=cost(2 * ROWS * 1024 * 256, 2 * MIB),
        name="first",
    )(first, w)


def forward_kernel(before, *refs):
    where = whereabouts()
    own, other, w, acc = refs[0:2], refs[2:5], refs[5], refs[6]
    for half, groups, steps in ((0, own, STEPS[1:3]), (1, other, STEPS[:3])):
        core = where[1] if half == 0 else 1 - where[1]
        total = before[...] if half == 0 else None
        for group, step in zip(groups, steps):
            part = group_product([group], w, core, (where[6 + half] + step) & 3, where[5])
            total = part if total is None else total + part
        acc[half] = total


def forward(before, own, other, w):
    vmem = pl.BlockSpec(memory_space=pltpu.VMEM)
    return pl.pallas_call(
        forward_kernel,
        out_shape=jax.ShapeDtypeStruct((2, ROWS, 256), F32),
        in_specs=[vmem] * 7,
        out_specs=vmem,
        compiler_params=params(8),
        cost_estimate=cost(2 * ROWS * 5120 * 256, 4 * MIB),
        name="forward",
    )(before, *own, *other, w)


def slope_of(group, before, up, w, core, across, flip):
    pre = before + group_product(group, w, core, across, flip)
    delta = (up.astype(F32) * gelu_slope(pre)).astype(BF)
    return nt(unit(256, BF), delta).astype(BF)


def slope_kernel(before, low, high, w, up, out):
    where = whereabouts()
    across = (where[6] + STEPS[3]) & 3
    out[...] = slope_of([low, high], before[0], up[0], w, where[1], across, where[5])


def own_slope(before, far, w, up):
    vmem = pl.BlockSpec(memory_space=pltpu.VMEM)
    return pl.pallas_call(
        slope_kernel,
        out_shape=jax.ShapeDtypeStruct((256, ROWS), BF),
        in_specs=[vmem] * 5,
        out_specs=vmem,
        compiler_params=params(8),
        cost_estimate=cost(2 * ROWS * 1024 * 256, 2 * MIB),
        name="slope",
    )(before, *far, w, up)


def gradient_kernel(own_delta, before, *refs):
    where = whereabouts()
    own = [refs[0:1], refs[1:2], refs[2:3], refs[3:5]]
    other = [refs[5:6], refs[6:7], refs[7:8], refs[8:10]]
    w, up, out, ids_out, ids, made, sem, ids_sem = refs[10:]
    core, flip = where[1], where[5]
    for k, group in enumerate(own):
        for j in range(8):
            ref, at = (group[0], j) if len(group) == 1 else (group[j // 4], j % 4)
            rows = ref[at, ROWS:].astype(F32).astype(jnp.int32)
            ids[k * 8 + j : k * 8 + j + 1] = rows[:1]
    sends = [pltpu.make_async_copy(ids, ids_out, ids_sem)]
    sends[0].start()
    across = (where[7] + STEPS[3]) & 3
    other_delta = slope_of(other[3], before[1], up[1], w, 1 - core, across, flip)
    delta = jnp.concatenate([own_delta[...], other_delta], axis=1)
    for k in range(4):
        mine = (where[6] + STEPS[k]) & 3
        tokens, places = [], []
        for j in range(8):
            m, n = j % 2, j // 2
            theirs = (where[7] + STEPS[n]) & 3
            tokens.append(jnp.concatenate([piece(own[k], m, theirs), piece(other[n], m, mine)], axis=0))
            z, x = jnp.where(core == 0, mine, theirs), jnp.where(core == 0, theirs, mine)
            places.append((x * 16, z * 2 + (m ^ flip)))
        part = (nn(delta, jnp.concatenate(tokens, axis=1)) / 1536.0).astype(BF)
        for j, (quarter, row) in enumerate(places):
            made[k, j] = part[:, j * 128 : (j + 1) * 128].reshape(16, 16, 128)
            sends.append(pltpu.make_async_copy(made.at[k, j], out.at[pl.ds(quarter, 16), row], sem.at[k, j]))
            sends[-1].start()
    for send in sends:
        send.wait()


def gradient_pieces(own_delta, before, own, other, w, up):
    vmem = pl.BlockSpec(memory_space=pltpu.VMEM)
    return pl.pallas_call(
        gradient_kernel,
        out_shape=[pltpu.HBM((64, 8, 16, 128), BF), pltpu.HBM((32, 128), jnp.int32)],
        in_specs=[vmem] * 14,
        out_specs=[pl.BlockSpec(memory_space=pltpu.HBM)] * 2,
        scratch_shapes=[
            pltpu.VMEM((32, 128), jnp.int32),
            pltpu.VMEM((4, 8, 16, 16, 128), BF),
            pltpu.SemaphoreType.DMA((4, 8)),
            pltpu.SemaphoreType.DMA,
        ],
        compiler_params=params(10),
        cost_estimate=cost(3 * 768 * 4096 * 256, 12 * MIB),
        name="gradient",
    )(own_delta, before, *own, *other, w, up)


def route_kernel(source, pieces, out):
    def some(n, c):
        for k in range(16):
            at = source[n * 16 + k]
            out[n * 16 + k] = (pieces[at].astype(F32) + pieces[at + 256].astype(F32)).astype(BF)
        return c

    lax.fori_loop(0, 16, some, 0)


def route(source, pieces):
    vmem = pl.BlockSpec(memory_space=pltpu.VMEM)
    out = pl.pallas_call(
        route_kernel,
        out_shape=jax.ShapeDtypeStruct((256, 16, 128), BF),
        in_specs=[pl.BlockSpec(memory_space=pltpu.SMEM), vmem],
        out_specs=vmem,
        compiler_params=params(16),
        cost_estimate=cost(0, 3 * MIB),
        name="route",
    )(source, pieces.reshape(512, 16, 128))
    return out.reshape(64, 4, 16, 128)


def collect(core, mine, theirs, slot, grad_t):
    for quarter in range(4):
        cols = slice(quarter * 128, (quarter + 1) * 128)
        part = slice(quarter * 16, (quarter + 1) * 16)
        grad_t[pl.ds(pl.multiple_of(core * 256, 256), 256), cols] = mine[part, slot].reshape(256, 128)
        grad_t[pl.ds(pl.multiple_of(256 - core * 256, 256), 256), cols] = theirs[part, slot].reshape(256, 128)


def hand_out(where, second, keep, send, slot, full):
    full[...] = second
    mean_square = jnp.sum(second * second, keepdims=True) * (1.0 / (BLOCK * BLOCK))
    scale = lax.rsqrt(mean_square + floor_eps)
    keep[slot] = (full[pl.ds(pl.multiple_of(where[0] * 128, 128), 128)] * scale).astype(BF)
    send[slot] = (full[pl.ds(pl.multiple_of(where[3] * 128, 128), 128)] * scale).astype(BF)


def fetch_kernel(slot_at, roots, statistics, pairs, statistic, sem):
    where = whereabouts()
    loads = [pltpu.make_async_copy(roots.at[slot_at[where[4] + k]], pairs.at[k], sem.at[k]) for k in range(4)]
    loads.append(pltpu.make_async_copy(statistics.at[slot_at[where[4]]], statistic, sem.at[4]))
    for load in loads:
        load.start()
    for load in loads:
        load.wait()


def fetch(slot_at, roots, statistics):
    smem = pl.BlockSpec(memory_space=pltpu.SMEM)
    vmem = pl.BlockSpec(memory_space=pltpu.VMEM)
    hbm = pl.BlockSpec(memory_space=pl.ANY)
    return pl.pallas_call(
        fetch_kernel,
        out_shape=[jax.ShapeDtypeStruct((4, 2, BLOCK, BLOCK), BF), jax.ShapeDtypeStruct((2, BLOCK, BLOCK), BF)],
        in_specs=[smem, hbm, hbm],
        out_specs=[vmem, vmem],
        scratch_shapes=[pltpu.SemaphoreType.DMA((5,))],
        compiler_params=params(8),
        cost_estimate=cost(0, 9 * MIB),
        name="fetch",
    )(slot_at, *in_hbm(roots, statistics))


def stored_kernel(mine, theirs, pairs, keep, send, grad_t, full):
    where = whereabouts()
    for k in range(3):
        collect(where[1], mine, theirs, k + 1, grad_t.at[k])
    firsts = [nt(pairs[k + 1, 0], grad_t[k]).astype(BF) for k in range(3)]
    seconds = [nn(firsts[k], pairs[k + 1, 1]) for k in range(3)]
    for k in range(3):
        hand_out(where, seconds[k], keep, send, k, full.at[k])


def stored_slots(mine, theirs, pairs):
    vmem = pl.BlockSpec(memory_space=pltpu.VMEM)
    return pl.pallas_call(
        stored_kernel,
        out_shape=[jax.ShapeDtypeStruct((3, 128, BLOCK), BF)] * 2,
        in_specs=[vmem] * 3,
        out_specs=[vmem, vmem],
        scratch_shapes=[pltpu.VMEM((3, BLOCK, BLOCK), BF), pltpu.VMEM((3, BLOCK, BLOCK), F32)],
        compiler_params=params(20),
        cost_estimate=cost(12 * BLOCK**3, 4 * MIB),
        name="stored",
    )(mine, theirs, pairs)


def product(a, b):
    (c, x), (d, y) = a, b
    xy = nn(x.astype(BF), y.astype(BF))
    return c * d, xy + (c * y + d * x if c and d else d * x if d else c * y)


def square(a):
    c, x = a
    x_rounded = x.astype(BF)
    return c * c, nn(x_rounded, x_rounded) + (2.0 * c) * x


def scaled_factor(power):
    return 1.25, -0.25 * power


def inverse_roots(matrices):
    eye = unit(BLOCK, F32)
    powers = [matrix / jnp.sum(matrix * eye, keepdims=True) for matrix in matrices]
    results = [scaled_factor(power) for power in powers]
    factors = results
    for sweep in range(2):
        fourths = [square(factor) for factor in factors]
        fourths = [square(fourth) for fourth in fourths]
        powers = [product(fourth, (0.0, power))[1] for fourth, power in zip(fourths, powers)]
        factors = [scaled_factor(power) for power in powers]
        results = [product(result, factor) for result, factor in zip(results, factors)]
    return [(c * eye + x).astype(BF) for c, x in results]


def refresh_kernel(slot_at, mine, theirs, pairs, statistic, keep, send, grad_t, full, pair):
    where = whereabouts()
    collect(where[1], mine, theirs, 0, grad_t)
    g_t = grad_t[...]
    is_fresh = slot_at[8] > where[4] // 4

    @pl.when(jnp.logical_not(is_fresh))
    def _():
        pair[...] = pairs[0]

    @pl.when(is_fresh)
    def _():
        eye = unit(BLOCK, F32)
        g = nt(unit(BLOCK, BF), g_t).astype(BF)
        outers = [nt(g, g), nt(g_t, g_t)]
        matrices = [decay * statistic[k].astype(F32) + outers[k] + jitter * eye for k in range(2)]
        pair[0], pair[1] = inverse_roots(matrices)

    first = nt(pair[0], g_t).astype(BF)
    hand_out(where, nn(first, pair[1]), keep, send, 0, full)


def refresh(slot_at, mine, theirs, pairs, statistic):
    smem = pl.BlockSpec(memory_space=pltpu.SMEM)
    vmem = pl.BlockSpec(memory_space=pltpu.VMEM)
    return pl.pallas_call(
        refresh_kernel,
        out_shape=[jax.ShapeDtypeStruct((1, 128, BLOCK), BF)] * 2,
        in_specs=[smem] + [vmem] * 4,
        out_specs=[vmem, vmem],
        scratch_shapes=[
            pltpu.VMEM((BLOCK, BLOCK), BF),
            pltpu.VMEM((BLOCK, BLOCK), F32),
            pltpu.VMEM((2, BLOCK, BLOCK), BF),
        ],
        compiler_params=params(32),
        cost_estimate=cost(42 * BLOCK**3, 4 * MIB),
        name="refresh",
    )(slot_at, mine, theirs, pairs, statistic)


def assemble_kernel(slot_at, fresh_mine, mine, theirs, out):
    here = whereabouts()[4]
    there = 4 - here
    out[slot_at[here]] = fresh_mine[0]
    for k in range(3):
        out[slot_at[here + k + 1]] = mine[k]
        out[slot_at[there + k + 1]] = theirs[k]


def assemble(slot_at, *parts):
    smem = pl.BlockSpec(memory_space=pltpu.SMEM)
    vmem = pl.BlockSpec(memory_space=pltpu.VMEM)
    return pl.pallas_call(
        assemble_kernel,
        out_shape=jax.ShapeDtypeStruct((8, 128, BLOCK), BF),
        in_specs=[smem] + [vmem] * 3,
        out_specs=vmem,
        compiler_params=params(16),
        cost_estimate=cost(0, 2 * MIB),
        name="assemble",
    )(slot_at, *parts)


def shards(tokens, in_weight, upstream, slot_block, refreshed, statistics, roots):
    group = lax.axis_index("grp")
    chip = group // 2
    both = ("grp", "dev")

    first = prepare(tokens, slot_block)
    first = lax.all_to_all(first, both, 0, 0, tiled=True, axis_index_groups=STAGE1)
    w, up = half_of_weights(in_weight, upstream)
    below = lax.ppermute(first, both, UP)
    above = lax.ppermute(first, both, DOWN)
    acc = first_of_own(first, w)
    shared, acc = lax.optimization_barrier((first, acc))
    own = [first, below, above]
    own += [lax.ppermute(below[:4], both, UP), lax.ppermute(above[4:], both, DOWN)]
    other = [lax.ppermute(group_of, "grp", CORE) for group_of in (shared, below, above)]
    acc = forward(acc, own[1:3], other[:3], w)
    acc, *own[3:] = lax.optimization_barrier((acc, *own[3:]))
    other += [lax.ppermute(part, "grp", CORE) for part in own[3:]]
    own_delta = own_slope(acc, own[3:], w, up)
    pieces, all_ids = gradient_pieces(own_delta, acc, own, other, w, up)
    pieces = lax.all_to_all(pieces, both, 0, 0, tiled=True, axis_index_groups=SAME_CORE)
    source, slot_at = slot_order(all_ids, refreshed, slot_block)
    pairs, statistic = fetch(slot_at, roots, statistics)
    source, pairs, statistic = lax.optimization_barrier((source, pairs, statistic))
    pieces = route(source, pieces)
    mine = lax.all_to_all(pieces, both, 0, 0, tiled=True, axis_index_groups=SAME_CORE)
    theirs = lax.ppermute(mine, "grp", CORE)

    keep, send = stored_slots(mine, theirs, pairs)
    other_keep = lax.ppermute(send, "grp", CHIP)
    mine, theirs, keep = lax.optimization_barrier((mine, theirs, keep))
    fresh_keep, fresh_send = refresh(slot_at, mine, theirs, pairs, statistic)
    fresh_other = lax.ppermute(fresh_send, "grp", CHIP)
    update = assemble(slot_at, fresh_keep, keep, other_keep)
    return lax.dynamic_update_slice_in_dim(update, fresh_other, slot_at[4 - 4 * chip], 0)


def solution(mesh):
    return jax.shard_map(
        shards,
        mesh=mesh,
        in_specs=(
            P(None, "dev"),
            P(None, "dev"),
            P(None, "dev"),
            P("dev"),
            P(),
            P("dev", None, None, None),
            P("dev", None, None, None),
        ),
        out_specs=P("dev", "grp", None),
        check_vma=False,
    )
```

```python
import functools

import jax
import jax.numpy as jnp
from jax import lax
from jax.experimental import pallas as pl
from jax.experimental.pallas import tpu as pltpu
from jax.sharding import PartitionSpec as P

decay = 0.9
jitter = 1e-06
floor_eps = 1e-06

ROWS = 384
IDS = 16
BLOCK = 512
BF = jnp.bfloat16
F32 = jnp.float32
MIB = 1 << 20

CORE = [(0, 1), (1, 0), (2, 3), (3, 2)]
CHIP = [(0, 2), (2, 0), (1, 3), (3, 1)]
def device(chip, core, z, y_hi, x):
    return (chip * 2 + core) * 32 + z * 8 + y_hi * 4 + x


def on_rings(chip, core, y_hi, first, second):
    return device(chip, core, second, y_hi, first) if core == 0 else device(chip, core, first, y_hi, second)


STAGE1 = [
    [on_rings(m, core, m ^ flip, i, a) for m in range(2) for i in range(4)]
    for core in range(2)
    for a in range(4)
    for flip in range(2)
]
EVERYWHERE = [
    (chip, core, z, y_hi, x)
    for chip in range(2)
    for core in range(2)
    for z in range(4)
    for y_hi in range(2)
    for x in range(4)
]


def along(step):
    return [
        (
            device(chip, core, z, y_hi, x),
            device(chip, core, z, y_hi, (x + step) % 4) if core else device(chip, core, (z + step) % 4, y_hi, x),
        )
        for chip, core, z, y_hi, x in EVERYWHERE
    ]


UP, DOWN = along(1), along(-1)
STEPS = (0, -1, 1, 2)
SAME_CORE = [[chip * 64 + core * 32 + d for chip in range(2) for d in range(32)] for core in range(2)]


def params(mib):
    return pltpu.CompilerParams(vmem_limit_bytes=mib * MIB)


def cost(flops, nbytes):
    return pl.CostEstimate(flops=flops, bytes_accessed=nbytes, transcendentals=0)


def in_hbm(*arrays):
    return [pltpu.with_memory_space_constraint(array, pltpu.HBM) for array in arrays]


def nt(a, b):
    return lax.dot_general(a, b, (((1,), (1,)), ((), ())), preferred_element_type=F32)


def nn(a, b):
    return jnp.dot(a, b, preferred_element_type=F32)


def whereabouts():
    group, d = lax.axis_index("grp"), lax.axis_index("dev")
    core, chip = group & 1, group >> 1
    z, y_hi, x = d >> 3, (d >> 2) & 1, d & 3
    places = [jnp.where(core == 0, z, x), jnp.where(core == 0, x, z)]
    return [group, core, group ^ 1, group ^ 2, 4 * chip, y_hi ^ chip, *places]


def unit(n, dtype):
    row = lax.broadcasted_iota(jnp.int32, (n, n), 0)
    col = lax.broadcasted_iota(jnp.int32, (n, n), 1)
    return jnp.where(row == col, 1.0, 0.0).astype(dtype)


def gelu_slope(values):
    return (
        0.5 * (1.0 + lax.erf(values * 0.7071067811865476))
        + values * jnp.exp(-0.5 * values * values) * 0.3989422804014327
    )


def spare_position(k):
    return jnp.where(k < 3, 7 - k, jnp.where(k < 6, 6 - k, jnp.where(k == 6, 4, 0)))


def place(flag, fresh_seen, spare_seen):
    return jnp.minimum(jnp.where(flag == 1, 4 * fresh_seen, spare_position(spare_seen)), 7)


def order_kernel(ids, refreshed, slot_block, source, slot_at, table):
    where = whereabouts()

    def clear(k, c):
        table[k] = 0
        return c

    def mark(k, c):
        table[refreshed[k]] = 1
        return c

    lax.fori_loop(0, 256, clear, 0, unroll=8)
    lax.fori_loop(0, 32, mark, 0, unroll=8)

    def positions(blocks):
        flags = [table[block] for block in blocks]
        fresh_seen = jnp.int32(0)
        spare_seen = jnp.int32(0)
        found = []
        for flag in flags:
            found.append(place(flag, fresh_seen, spare_seen))
            fresh_seen += flag
            spare_seen += 1 - flag
        return found, fresh_seen

    def owner(o, c):
        z, y_hi, x = o >> 3, (o >> 2) & 1, o & 3
        across = jnp.where(where[1] == 0, z, x)
        inner = jnp.where(where[1] == 0, x, z)
        step = (across - where[6]) & 3
        group = jnp.where(step == 0, 0, jnp.where(step == 3, 1, step + 1))
        piece = group * 8 + (y_hi ^ where[5]) * 4 + inner
        blocks = [ids[piece, p] for p in range(8)]
        found, _ = positions(blocks)
        for block, position in zip(blocks, found):
            source[(position >> 2) * 128 + o * 4 + (position & 3)] = (block & 31) * 8 + (block >> 5)
        return c

    lax.fori_loop(0, 32, owner, 0)
    found, fresh_seen = positions([slot_block[p] for p in range(8)])
    for p in range(8):
        slot_at[found[p]] = p
    slot_at[8] = fresh_seen


def slot_order(ids, refreshed, slot_block):
    smem = pl.BlockSpec(memory_space=pltpu.SMEM)
    return pl.pallas_call(
        order_kernel,
        out_shape=[jax.ShapeDtypeStruct((256,), jnp.int32), jax.ShapeDtypeStruct((16,), jnp.int32)],
        in_specs=[smem] * 3,
        out_specs=[smem] * 2,
        scratch_shapes=[pltpu.SMEM((256,), jnp.int32)],
        cost_estimate=cost(0, 4096),
        name="order",
    )(ids, refreshed, slot_block)


def prepare_kernel(tokens, slot_block, out, ids, sem, id_sem):
    where = whereabouts()
    load_ids = pltpu.make_async_copy(slot_block, ids, id_sem)
    load_ids.start()
    loads = []
    for m in range(2):
        rows = pl.ds(pl.multiple_of((2 * m + where[1]) * ROWS, ROWS), ROWS)
        for i in range(4):
            k = 4 * m + i
            loads.append(pltpu.make_async_copy(tokens.at[rows], out.at[k, pl.ds(0, ROWS)], sem.at[k]))
    for load in loads:
        load.start()
    row = lax.broadcasted_iota(jnp.int32, (IDS, 128), 0)
    lane = lax.broadcasted_iota(jnp.int32, (IDS, 128), 1)
    tile = jnp.zeros((IDS, 128), jnp.int32)
    load_ids.wait()
    for p in range(8):
        tile = jnp.where((row == 0) & (lane == p), ids[p], tile)
    tile = tile.astype(F32).astype(BF)
    for k in range(8):
        out[k, ROWS:] = tile
    for load in loads:
        load.wait()


def prepare(tokens, slot_block):
    hbm = pl.BlockSpec(memory_space=pl.ANY)
    return pl.pallas_call(
        prepare_kernel,
        out_shape=jax.ShapeDtypeStruct((8, ROWS + IDS, 128), BF),
        in_specs=[hbm, hbm],
        out_specs=pl.BlockSpec(memory_space=pltpu.VMEM),
        scratch_shapes=[pltpu.SMEM((8,), jnp.int32), pltpu.SemaphoreType.DMA((8,)), pltpu.SemaphoreType.DMA],
        compiler_params=params(8),
        cost_estimate=cost(0, MIB),
        name="prepare",
    )(*in_hbm(tokens, slot_block))


def weights_kernel(weight, upstream, w, up, sem):
    where = whereabouts()
    cols = pl.ds(pl.multiple_of(where[1] * 256, 256), 256)
    loads = [pltpu.make_async_copy(weight.at[:, cols], w, sem.at[2])]
    for k in range(2):
        rows = pl.ds(pl.multiple_of(where[2 * k] * ROWS, ROWS), ROWS)
        loads.append(pltpu.make_async_copy(upstream.at[rows, cols], up.at[k], sem.at[k]))
    for load in loads:
        load.start()
    for load in loads:
        load.wait()


def half_of_weights(in_weight, upstream):
    vmem = pl.BlockSpec(memory_space=pltpu.VMEM)
    hbm = pl.BlockSpec(memory_space=pl.ANY)
    return pl.pallas_call(
        weights_kernel,
        out_shape=[jax.ShapeDtypeStruct((4096, 256), BF), jax.ShapeDtypeStruct((2, ROWS, 256), BF)],
        in_specs=[hbm, hbm],
        out_specs=[vmem, vmem],
        scratch_shapes=[pltpu.SemaphoreType.DMA((3,))],
        compiler_params=params(4),
        cost_estimate=cost(0, 5 * MIB),
        name="weights",
    )(*in_hbm(in_weight, upstream))


def piece(group, m, i):
    return group[0][m * 4 + i, :ROWS] if len(group) == 1 else group[m][i, :ROWS]


def group_product(group, w, core, across, flip):
    tokens = jnp.concatenate([piece(group, j // 4, j % 4) for j in range(8)], axis=1)
    weights = []
    for j in range(8):
        row = jnp.where(core == 0, across * 1024 + j % 4 * 128, j % 4 * 1024 + across * 128) + ((j // 4) ^ flip) * 512
        weights.append(w[pl.ds(pl.multiple_of(row, 128), 128)])
    return nn(tokens, jnp.concatenate(weights, axis=0))


def first_kernel(first, w, acc):
    where = whereabouts()
    acc[...] = group_product([first], w, where[1], where[6], where[5])


def first_of_own(first, w):
    vmem = pl.BlockSpec(memory_space=pltpu.VMEM)
    return pl.pallas_call(
        first_kernel,
        out_shape=jax.ShapeDtypeStruct((ROWS, 256), F32),
        in_specs=[vmem] * 2,
        out_specs=vmem,
        compiler_params=params(8),
        cost_estimate=cost(2 * ROWS * 1024 * 256, 2 * MIB),
        name="first",
    )(first, w)


def forward_kernel(before, *refs):
    where = whereabouts()
    own, other, w, acc = refs[0:2], refs[2:5], refs[5], refs[6]
    for half, groups, steps in ((0, own, STEPS[1:3]), (1, other, STEPS[:3])):
        core = where[1] if half == 0 else 1 - where[1]
        total = before[...] if half == 0 else None
        for group, step in zip(groups, steps):
            part = group_product([group], w, core, (where[6 + half] + step) & 3, where[5])
            total = part if total is None else total + part
        acc[half] = total


def forward(before, own, other, w):
    vmem = pl.BlockSpec(memory_space=pltpu.VMEM)
    return pl.pallas_call(
        forward_kernel,
        out_shape=jax.ShapeDtypeStruct((2, ROWS, 256), F32),
        in_specs=[vmem] * 7,
        out_specs=vmem,
        compiler_params=params(8),
        cost_estimate=cost(2 * ROWS * 5120 * 256, 4 * MIB),
        name="forward",
    )(before, *own, *other, w)


def slope_of(group, before, up, w, core, across, flip):
    pre = before + group_product(group, w, core, across, flip)
    delta = (up.astype(F32) * gelu_slope(pre)).astype(BF)
    return nt(unit(256, BF), delta).astype(BF)


def slope_kernel(before, low, high, w, up, out):
    where = whereabouts()
    across = (where[6] + STEPS[3]) & 3
    out[...] = slope_of([low, high], before[0], up[0], w, where[1], across, where[5])


def own_slope(before, far, w, up):
    vmem = pl.BlockSpec(memory_space=pltpu.VMEM)
    return pl.pallas_call(
        slope_kernel,
        out_shape=jax.ShapeDtypeStruct((256, ROWS), BF),
        in_specs=[vmem] * 5,
        out_specs=vmem,
        compiler_params=params(8),
        cost_estimate=cost(2 * ROWS * 1024 * 256, 2 * MIB),
        name="slope",
    )(before, *far, w, up)


def gradient_kernel(own_delta, before, *refs):
    where = whereabouts()
    own = [refs[0:1], refs[1:2], refs[2:3], refs[3:5]]
    other = [refs[5:6], refs[6:7], refs[7:8], refs[8:10]]
    w, up, out, ids_out, ids, made, sem, ids_sem = refs[10:]
    core, flip = where[1], where[5]
    for k, group in enumerate(own):
        for j in range(8):
            ref, at = (group[0], j) if len(group) == 1 else (group[j // 4], j % 4)
            rows = ref[at, ROWS:].astype(F32).astype(jnp.int32)
            ids[k * 8 + j : k * 8 + j + 1] = rows[:1]
    sends = [pltpu.make_async_copy(ids, ids_out, ids_sem)]
    sends[0].start()
    across = (where[7] + STEPS[3]) & 3
    other_delta = slope_of(other[3], before[1], up[1], w, 1 - core, across, flip)
    delta = jnp.concatenate([own_delta[...], other_delta], axis=1)
    for k in range(4):
        mine = (where[6] + STEPS[k]) & 3
        tokens, places = [], []
        for j in range(8):
            m, n = j % 2, j // 2
            theirs = (where[7] + STEPS[n]) & 3
            tokens.append(jnp.concatenate([piece(own[k], m, theirs), piece(other[n], m, mine)], axis=0))
            z, x = jnp.where(core == 0, mine, theirs), jnp.where(core == 0, theirs, mine)
            places.append((x * 16, z * 2 + (m ^ flip)))
        part = (nn(delta, jnp.concatenate(tokens, axis=1)) / 1536.0).astype(BF)
        for j, (quarter, row) in enumerate(places):
            made[k, j] = part[:, j * 128 : (j + 1) * 128].reshape(16, 16, 128)
            sends.append(pltpu.make_async_copy(made.at[k, j], out.at[pl.ds(quarter, 16), row], sem.at[k, j]))
            sends[-1].start()
    for send in sends:
        send.wait()


def gradient_pieces(own_delta, before, own, other, w, up):
    vmem = pl.BlockSpec(memory_space=pltpu.VMEM)
    return pl.pallas_call(
        gradient_kernel,
        out_shape=[pltpu.HBM((64, 8, 16, 128), BF), pltpu.HBM((32, 128), jnp.int32)],
        in_specs=[vmem] * 14,
        out_specs=[pl.BlockSpec(memory_space=pltpu.HBM)] * 2,
        scratch_shapes=[
            pltpu.VMEM((32, 128), jnp.int32),
            pltpu.VMEM((4, 8, 16, 16, 128), BF),
            pltpu.SemaphoreType.DMA((4, 8)),
            pltpu.SemaphoreType.DMA,
        ],
        compiler_params=params(10),
        cost_estimate=cost(3 * 768 * 4096 * 256, 12 * MIB),
        name="gradient",
    )(own_delta, before, *own, *other, w, up)


def route_kernel(source, pieces, out):
    def some(n, c):
        for k in range(16):
            at = source[n * 16 + k]
            out[n * 16 + k] = (pieces[at].astype(F32) + pieces[at + 256].astype(F32)).astype(BF)
        return c

    lax.fori_loop(0, 16, some, 0)


def route(source, pieces):
    vmem = pl.BlockSpec(memory_space=pltpu.VMEM)
    out = pl.pallas_call(
        route_kernel,
        out_shape=jax.ShapeDtypeStruct((256, 16, 128), BF),
        in_specs=[pl.BlockSpec(memory_space=pltpu.SMEM), vmem],
        out_specs=vmem,
        compiler_params=params(16),
        cost_estimate=cost(0, 3 * MIB),
        name="route",
    )(source, pieces.reshape(512, 16, 128))
    return out.reshape(64, 4, 16, 128)


def collect(core, mine, theirs, slot, grad_t):
    for quarter in range(4):
        cols = slice(quarter * 128, (quarter + 1) * 128)
        part = slice(quarter * 16, (quarter + 1) * 16)
        grad_t[pl.ds(pl.multiple_of(core * 256, 256), 256), cols] = mine[part, slot].reshape(256, 128)
        grad_t[pl.ds(pl.multiple_of(256 - core * 256, 256), 256), cols] = theirs[part, slot].reshape(256, 128)


def hand_out(where, second, keep, send, slot, full):
    full[...] = second
    mean_square = jnp.sum(second * second, keepdims=True) * (1.0 / (BLOCK * BLOCK))
    scale = lax.rsqrt(mean_square + floor_eps)
    keep[slot] = (full[pl.ds(pl.multiple_of(where[0] * 128, 128), 128)] * scale).astype(BF)
    send[slot] = (full[pl.ds(pl.multiple_of(where[3] * 128, 128), 128)] * scale).astype(BF)


def fetch_kernel(slot_at, roots, statistics, pairs, statistic, sem):
    where = whereabouts()
    loads = [pltpu.make_async_copy(roots.at[slot_at[where[4] + k]], pairs.at[k], sem.at[k]) for k in range(4)]
    loads.append(pltpu.make_async_copy(statistics.at[slot_at[where[4]]], statistic, sem.at[4]))
    for load in loads:
        load.start()
    for load in loads:
        load.wait()


def fetch(slot_at, roots, statistics):
    smem = pl.BlockSpec(memory_space=pltpu.SMEM)
    vmem = pl.BlockSpec(memory_space=pltpu.VMEM)
    hbm = pl.BlockSpec(memory_space=pl.ANY)
    return pl.pallas_call(
        fetch_kernel,
        out_shape=[jax.ShapeDtypeStruct((4, 2, BLOCK, BLOCK), BF), jax.ShapeDtypeStruct((2, BLOCK, BLOCK), BF)],
        in_specs=[smem, hbm, hbm],
        out_specs=[vmem, vmem],
        scratch_shapes=[pltpu.SemaphoreType.DMA((5,))],
        compiler_params=params(8),
        cost_estimate=cost(0, 9 * MIB),
        name="fetch",
    )(slot_at, *in_hbm(roots, statistics))


def half_block(ref, slot):
    return jnp.concatenate([ref[q * 16 : (q + 1) * 16, slot].reshape(256, 128) for q in range(4)], axis=1)


def half_kernel(mine, pairs, firsts):
    for k in range(3):
        firsts[k] = nt(pairs[k + 1, 0], half_block(mine, k + 1)).astype(BF)


def half_of_firsts(mine, pairs):
    vmem = pl.BlockSpec(memory_space=pltpu.VMEM)
    return pl.pallas_call(
        half_kernel,
        out_shape=jax.ShapeDtypeStruct((3, BLOCK, 256), BF),
        in_specs=[vmem, vmem],
        out_specs=vmem,
        compiler_params=params(12),
        cost_estimate=cost(3 * BLOCK**3, 2 * MIB),
        name="half",
    )(mine, pairs)


def stored_kernel(firsts, theirs, pairs, keep, send, full):
    where = whereabouts()
    mine = pl.ds(pl.multiple_of(where[1] * 256, 256), 256)
    rest = pl.ds(pl.multiple_of(256 - where[1] * 256, 256), 256)
    others = [nt(pairs[k + 1, 0], half_block(theirs, k + 1)).astype(BF) for k in range(3)]
    seconds = [nn(firsts[k], pairs[k + 1, 1, mine]) + nn(others[k], pairs[k + 1, 1, rest]) for k in range(3)]
    for k in range(3):
        hand_out(where, seconds[k], keep, send, k, full.at[k])


def stored_slots(firsts, theirs, pairs):
    vmem = pl.BlockSpec(memory_space=pltpu.VMEM)
    return pl.pallas_call(
        stored_kernel,
        out_shape=[jax.ShapeDtypeStruct((3, 128, BLOCK), BF)] * 2,
        in_specs=[vmem] * 3,
        out_specs=[vmem, vmem],
        scratch_shapes=[pltpu.VMEM((3, BLOCK, BLOCK), F32)],
        compiler_params=params(20),
        cost_estimate=cost(9 * BLOCK**3, 4 * MIB),
        name="stored",
    )(firsts, theirs, pairs)


def symmetric_product(x, y):
    top = nn(x[:256], y)
    corner = nn(x[256:], y[:, 256:])
    return jnp.concatenate([top, jnp.concatenate([top[:, 256:].T, corner], axis=1)], axis=0)


def product(a, b):
    (c, x), (d, y) = a, b
    xy = symmetric_product(x.astype(BF), y.astype(BF))
    return c * d, xy + (c * y + d * x if c and d else d * x if d else c * y)


def square(a):
    c, x = a
    x_rounded = x.astype(BF)
    return c * c, symmetric_product(x_rounded, x_rounded) + (2.0 * c) * x


def scaled_factor(power):
    return 1.25, -0.25 * power


def inverse_roots(matrices):
    eye = unit(BLOCK, F32)
    powers = [matrix / jnp.sum(matrix * eye, keepdims=True) for matrix in matrices]
    results = [scaled_factor(power) for power in powers]
    factors = results
    for sweep in range(2):
        fourths = [square(factor) for factor in factors]
        fourths = [square(fourth) for fourth in fourths]
        powers = [product(fourth, (0.0, power))[1] for fourth, power in zip(fourths, powers)]
        factors = [scaled_factor(power) for power in powers]
        results = [product(result, factor) for result, factor in zip(results, factors)]
    return [(c * eye + x).astype(BF) for c, x in results]


def refresh_kernel(slot_at, mine, theirs, pairs, statistic, keep, send, grad_t, full, pair):
    where = whereabouts()
    collect(where[1], mine, theirs, 0, grad_t)
    g_t = grad_t[...]
    is_fresh = slot_at[8] > where[4] // 4

    @pl.when(jnp.logical_not(is_fresh))
    def _():
        pair[...] = pairs[0]

    @pl.when(is_fresh)
    def _():
        eye = unit(BLOCK, F32)
        g = nt(unit(BLOCK, BF), g_t).astype(BF)
        outers = [nt(g, g), nt(g_t, g_t)]
        matrices = [decay * statistic[k].astype(F32) + outers[k] + jitter * eye for k in range(2)]
        pair[0], pair[1] = inverse_roots(matrices)

    first = nt(pair[0], g_t).astype(BF)
    hand_out(where, nn(first, pair[1]), keep, send, 0, full)


def refresh(slot_at, mine, theirs, pairs, statistic):
    smem = pl.BlockSpec(memory_space=pltpu.SMEM)
    vmem = pl.BlockSpec(memory_space=pltpu.VMEM)
    return pl.pallas_call(
        refresh_kernel,
        out_shape=[jax.ShapeDtypeStruct((1, 128, BLOCK), BF)] * 2,
        in_specs=[smem] + [vmem] * 4,
        out_specs=[vmem, vmem],
        scratch_shapes=[
            pltpu.VMEM((BLOCK, BLOCK), BF),
            pltpu.VMEM((BLOCK, BLOCK), F32),
            pltpu.VMEM((2, BLOCK, BLOCK), BF),
        ],
        compiler_params=params(32),
        cost_estimate=cost(42 * BLOCK**3, 4 * MIB),
        name="refresh",
    )(slot_at, mine, theirs, pairs, statistic)


def copy_all(copies):
    for copy in copies:
        copy.start()
    for copy in copies:
        copy.wait()


def assemble_kernel(slot_at, fresh, mine, theirs, out, sem):
    here = whereabouts()[4]
    copies = [pltpu.make_async_copy(fresh.at[0], out.at[slot_at[here]], sem.at[6])]
    for k in range(3):
        copies.append(pltpu.make_async_copy(mine.at[k], out.at[slot_at[here + k + 1]], sem.at[k]))
        copies.append(pltpu.make_async_copy(theirs.at[k], out.at[slot_at[4 - here + k + 1]], sem.at[k + 3]))
    for copy in copies:
        copy.start()
    for copy in copies:
        copy.wait()


def assemble(slot_at, *parts):
    hbm = pl.BlockSpec(memory_space=pl.ANY)
    return pl.pallas_call(
        assemble_kernel,
        out_shape=pltpu.HBM((8, 128, BLOCK), BF),
        in_specs=[pl.BlockSpec(memory_space=pltpu.SMEM)] + [hbm] * 3,
        out_specs=pl.BlockSpec(memory_space=pltpu.HBM),
        scratch_shapes=[pltpu.SemaphoreType.DMA((7,))],
        compiler_params=params(4),
        cost_estimate=cost(0, 2 * MIB),
        name="assemble",
    )(slot_at, *parts)


def shards(tokens, in_weight, upstream, slot_block, refreshed, statistics, roots):
    both = ("grp", "dev")

    first = prepare(tokens, slot_block)
    first = lax.all_to_all(first, both, 0, 0, tiled=True, axis_index_groups=STAGE1)
    w, up = half_of_weights(in_weight, upstream)
    below = lax.ppermute(first, both, UP)
    above = lax.ppermute(first, both, DOWN)
    acc = first_of_own(first, w)
    shared, acc = lax.optimization_barrier((first, acc))
    below, above = lax.optimization_barrier((below, above))
    own = [first, below, above]
    own += [lax.ppermute(below[:4], both, UP), lax.ppermute(above[4:], both, DOWN)]
    other = [lax.ppermute(group_of, "grp", CORE) for group_of in (shared, below, above)]
    acc = forward(acc, own[1:3], other[:3], w)
    acc, *own[3:] = lax.optimization_barrier((acc, *own[3:]))
    other += [lax.ppermute(part, "grp", CORE) for part in own[3:]]
    own_delta = own_slope(acc, own[3:], w, up)
    pieces, all_ids = gradient_pieces(own_delta, acc, own, other, w, up)
    pieces = lax.all_to_all(pieces, both, 0, 0, tiled=True, axis_index_groups=SAME_CORE)
    source, slot_at = slot_order(all_ids, refreshed, slot_block)
    pairs, statistic = fetch(slot_at, roots, statistics)
    source, pairs, statistic = lax.optimization_barrier((source, pairs, statistic))
    pieces = route(source, pieces)
    mine = lax.all_to_all(pieces, both, 0, 0, tiled=True, axis_index_groups=SAME_CORE)
    theirs = lax.ppermute(mine, "grp", CORE)

    keep, send = stored_slots(half_of_firsts(mine, pairs), theirs, pairs)
    other_keep = lax.ppermute(send, "grp", CHIP)
    mine, theirs, keep = lax.optimization_barrier((mine, theirs, keep))
    fresh_keep, fresh_send = refresh(slot_at, mine, theirs, pairs, statistic)
    fresh_other = lax.ppermute(fresh_send, "grp", CHIP)
    update = assemble(slot_at, fresh_keep, keep, other_keep)
    return lax.dynamic_update_slice_in_dim(update, fresh_other, slot_at[4 - 4 * (lax.axis_index("grp") // 2)], 0)


def solution(mesh):
    return jax.shard_map(
        shards,
        mesh=mesh,
        in_specs=(
            P(None, "dev"),
            P(None, "dev"),
            P(None, "dev"),
            P("dev"),
            P(),
            P("dev", None, None, None),
            P("dev", None, None, None),
        ),
        out_specs=P("dev", "grp", None),
        check_vma=False,
    )
```

```python
import functools

import jax
import jax.numpy as jnp
from jax import lax
from jax.experimental import pallas as pl
from jax.experimental.pallas import tpu as pltpu
from jax.sharding import PartitionSpec as P

decay = 0.9
jitter = 1e-06
floor_eps = 1e-06

ROWS = 384
IDS = 16
BLOCK = 512
BF = jnp.bfloat16
F32 = jnp.float32
MIB = 1 << 20

CORE = [(0, 1), (1, 0), (2, 3), (3, 2)]
CHIP = [(0, 2), (2, 0), (1, 3), (3, 1)]
def device(chip, core, z, y_hi, x):
    return (chip * 2 + core) * 32 + z * 8 + y_hi * 4 + x


def on_rings(chip, core, y_hi, first, second):
    return device(chip, core, second, y_hi, first) if core == 0 else device(chip, core, first, y_hi, second)


STAGE1 = [
    [on_rings(m, core, m ^ flip, i, a) for m in range(2) for i in range(4)]
    for core in range(2)
    for a in range(4)
    for flip in range(2)
]
EVERYWHERE = [
    (chip, core, z, y_hi, x)
    for chip in range(2)
    for core in range(2)
    for z in range(4)
    for y_hi in range(2)
    for x in range(4)
]


def along(step):
    return [
        (
            device(chip, core, z, y_hi, x),
            device(chip, core, z, y_hi, (x + step) % 4) if core else device(chip, core, (z + step) % 4, y_hi, x),
        )
        for chip, core, z, y_hi, x in EVERYWHERE
    ]


UP, DOWN = along(1), along(-1)
STEPS = (0, -1, 1, 2)
SAME_CORE = [[chip * 64 + core * 32 + d for chip in range(2) for d in range(32)] for core in range(2)]


def params(mib):
    return pltpu.CompilerParams(vmem_limit_bytes=mib * MIB)


def cost(flops, nbytes):
    return pl.CostEstimate(flops=flops, bytes_accessed=nbytes, transcendentals=0)


def in_hbm(*arrays):
    return [pltpu.with_memory_space_constraint(array, pltpu.HBM) for array in arrays]


def nt(a, b):
    return lax.dot_general(a, b, (((1,), (1,)), ((), ())), preferred_element_type=F32)


def nn(a, b):
    return jnp.dot(a, b, preferred_element_type=F32)


def whereabouts():
    group, d = lax.axis_index("grp"), lax.axis_index("dev")
    core, chip = group & 1, group >> 1
    z, y_hi, x = d >> 3, (d >> 2) & 1, d & 3
    places = [jnp.where(core == 0, z, x), jnp.where(core == 0, x, z)]
    return [group, core, group ^ 1, group ^ 2, 4 * chip, y_hi ^ chip, *places]


def unit(n, dtype):
    row = lax.broadcasted_iota(jnp.int32, (n, n), 0)
    col = lax.broadcasted_iota(jnp.int32, (n, n), 1)
    return jnp.where(row == col, 1.0, 0.0).astype(dtype)


def gelu_slope(values):
    return (
        0.5 * (1.0 + lax.erf(values * 0.7071067811865476))
        + values * jnp.exp(-0.5 * values * values) * 0.3989422804014327
    )


def spare_position(k):
    return jnp.where(k < 3, 7 - k, jnp.where(k < 6, 6 - k, jnp.where(k == 6, 4, 0)))


def place(flag, fresh_seen, spare_seen):
    return jnp.minimum(jnp.where(flag == 1, 4 * fresh_seen, spare_position(spare_seen)), 7)


def order_kernel(ids, refreshed, slot_block, source, slot_at, table):
    where = whereabouts()

    def clear(k, c):
        table[k] = 0
        return c

    def mark(k, c):
        table[refreshed[k]] = 1
        return c

    lax.fori_loop(0, 256, clear, 0, unroll=8)
    lax.fori_loop(0, 32, mark, 0, unroll=8)

    def positions(blocks):
        flags = [table[block] for block in blocks]
        fresh_seen = jnp.int32(0)
        spare_seen = jnp.int32(0)
        found = []
        for flag in flags:
            found.append(place(flag, fresh_seen, spare_seen))
            fresh_seen += flag
            spare_seen += 1 - flag
        return found, fresh_seen

    def owner(o, c):
        z, y_hi, x = o >> 3, (o >> 2) & 1, o & 3
        across = jnp.where(where[1] == 0, z, x)
        inner = jnp.where(where[1] == 0, x, z)
        step = (across - where[6]) & 3
        group = jnp.where(step == 0, 0, jnp.where(step == 3, 1, step + 1))
        piece = group * 8 + (y_hi ^ where[5]) * 4 + inner
        blocks = [ids[piece, p] for p in range(8)]
        found, _ = positions(blocks)
        for block, position in zip(blocks, found):
            source[(position >> 2) * 128 + o * 4 + (position & 3)] = (block & 31) * 8 + (block >> 5)
        return c

    lax.fori_loop(0, 32, owner, 0)
    found, fresh_seen = positions([slot_block[p] for p in range(8)])
    for p in range(8):
        slot_at[found[p]] = p
    slot_at[8] = fresh_seen


def slot_order(ids, refreshed, slot_block):
    smem = pl.BlockSpec(memory_space=pltpu.SMEM)
    return pl.pallas_call(
        order_kernel,
        out_shape=[jax.ShapeDtypeStruct((256,), jnp.int32), jax.ShapeDtypeStruct((16,), jnp.int32)],
        in_specs=[smem] * 3,
        out_specs=[smem] * 2,
        scratch_shapes=[pltpu.SMEM((256,), jnp.int32)],
        cost_estimate=cost(0, 4096),
        name="order",
    )(ids, refreshed, slot_block)


def prepare_kernel(tokens, slot_block, out, ids, sem, id_sem):
    where = whereabouts()
    load_ids = pltpu.make_async_copy(slot_block, ids, id_sem)
    load_ids.start()
    loads = []
    for m in range(2):
        rows = pl.ds(pl.multiple_of((2 * m + where[1]) * ROWS, ROWS), ROWS)
        for i in range(4):
            k = 4 * m + i
            loads.append(pltpu.make_async_copy(tokens.at[rows], out.at[k, pl.ds(0, ROWS)], sem.at[k]))
    for load in loads:
        load.start()
    row = lax.broadcasted_iota(jnp.int32, (IDS, 128), 0)
    lane = lax.broadcasted_iota(jnp.int32, (IDS, 128), 1)
    tile = jnp.zeros((IDS, 128), jnp.int32)
    load_ids.wait()
    for p in range(8):
        tile = jnp.where((row == 0) & (lane == p), ids[p], tile)
    tile = tile.astype(F32).astype(BF)
    for k in range(8):
        out[k, ROWS:] = tile
    for load in loads:
        load.wait()


def prepare(tokens, slot_block):
    hbm = pl.BlockSpec(memory_space=pl.ANY)
    return pl.pallas_call(
        prepare_kernel,
        out_shape=jax.ShapeDtypeStruct((8, ROWS + IDS, 128), BF),
        in_specs=[hbm, hbm],
        out_specs=pl.BlockSpec(memory_space=pltpu.VMEM),
        scratch_shapes=[pltpu.SMEM((8,), jnp.int32), pltpu.SemaphoreType.DMA((8,)), pltpu.SemaphoreType.DMA],
        compiler_params=params(8),
        cost_estimate=cost(0, MIB),
        name="prepare",
    )(*in_hbm(tokens, slot_block))


def weights_kernel(weight, upstream, w, up, sem):
    where = whereabouts()
    cols = pl.ds(pl.multiple_of(where[1] * 256, 256), 256)
    loads = [pltpu.make_async_copy(weight.at[:, cols], w, sem.at[2])]
    for k in range(2):
        rows = pl.ds(pl.multiple_of(where[2 * k] * ROWS, ROWS), ROWS)
        loads.append(pltpu.make_async_copy(upstream.at[rows, cols], up.at[k], sem.at[k]))
    for load in loads:
        load.start()
    for load in loads:
        load.wait()


def half_of_weights(in_weight, upstream):
    vmem = pl.BlockSpec(memory_space=pltpu.VMEM)
    hbm = pl.BlockSpec(memory_space=pl.ANY)
    return pl.pallas_call(
        weights_kernel,
        out_shape=[jax.ShapeDtypeStruct((4096, 256), BF), jax.ShapeDtypeStruct((2, ROWS, 256), BF)],
        in_specs=[hbm, hbm],
        out_specs=[vmem, vmem],
        scratch_shapes=[pltpu.SemaphoreType.DMA((3,))],
        compiler_params=params(4),
        cost_estimate=cost(0, 5 * MIB),
        name="weights",
    )(*in_hbm(in_weight, upstream))


def piece(group, m, i):
    return group[0][m * 4 + i, :ROWS] if len(group) == 1 else group[m][i, :ROWS]


def group_product(group, w, core, across, flip):
    tokens = jnp.concatenate([piece(group, j // 4, j % 4) for j in range(8)], axis=1)
    weights = []
    for j in range(8):
        row = jnp.where(core == 0, across * 1024 + j % 4 * 128, j % 4 * 1024 + across * 128) + ((j // 4) ^ flip) * 512
        weights.append(w[pl.ds(pl.multiple_of(row, 128), 128)])
    return nn(tokens, jnp.concatenate(weights, axis=0))


def first_kernel(first, w, acc):
    where = whereabouts()
    acc[...] = group_product([first], w, where[1], where[6], where[5])


def first_of_own(first, w):
    vmem = pl.BlockSpec(memory_space=pltpu.VMEM)
    return pl.pallas_call(
        first_kernel,
        out_shape=jax.ShapeDtypeStruct((ROWS, 256), F32),
        in_specs=[vmem] * 2,
        out_specs=vmem,
        compiler_params=params(8),
        cost_estimate=cost(2 * ROWS * 1024 * 256, 2 * MIB),
        name="first",
    )(first, w)


def own_kernel(before, below, above, w, acc):
    where = whereabouts()
    total = before[...]
    for ref, step in ((below, STEPS[1]), (above, STEPS[2])):
        total = total + group_product([ref], w, where[1], (where[6] + step) & 3, where[5])
    acc[...] = total


def more_of_own(before, below, above, w):
    vmem = pl.BlockSpec(memory_space=pltpu.VMEM)
    return pl.pallas_call(
        own_kernel,
        out_shape=jax.ShapeDtypeStruct((ROWS, 256), F32),
        in_specs=[vmem] * 4,
        out_specs=vmem,
        compiler_params=params(8),
        cost_estimate=cost(2 * ROWS * 2048 * 256, 2 * MIB),
        name="own",
    )(before, below, above, w)


def other_kernel(*refs):
    where = whereabouts()
    w, acc = refs[5:]
    total = None
    for group, step in zip([refs[0:1], refs[1:3], refs[3:5]], STEPS):
        part = group_product(group, w, 1 - where[1], (where[7] + step) & 3, where[5])
        total = part if total is None else total + part
    acc[...] = total


def forward_of_other(other, w):
    vmem = pl.BlockSpec(memory_space=pltpu.VMEM)
    return pl.pallas_call(
        other_kernel,
        out_shape=jax.ShapeDtypeStruct((ROWS, 256), F32),
        in_specs=[vmem] * 6,
        out_specs=vmem,
        compiler_params=params(8),
        cost_estimate=cost(2 * ROWS * 3072 * 256, 2 * MIB),
        name="other",
    )(*other, w)


def slope_of(group, before, up, w, core, across, flip):
    pre = before + group_product(group, w, core, across, flip)
    delta = (up.astype(F32) * gelu_slope(pre)).astype(BF)
    return nt(unit(256, BF), delta).astype(BF)


def slope_kernel(before, low, high, w, up, out):
    where = whereabouts()
    across = (where[6] + STEPS[3]) & 3
    out[...] = slope_of([low, high], before[...], up[0], w, where[1], across, where[5])


def own_slope(before, far, w, up):
    vmem = pl.BlockSpec(memory_space=pltpu.VMEM)
    return pl.pallas_call(
        slope_kernel,
        out_shape=jax.ShapeDtypeStruct((256, ROWS), BF),
        in_specs=[vmem] * 5,
        out_specs=vmem,
        compiler_params=params(8),
        cost_estimate=cost(2 * ROWS * 1024 * 256, 2 * MIB),
        name="slope",
    )(before, *far, w, up)


def gradient_kernel(own_delta, before, *refs):
    where = whereabouts()
    own = [refs[0:1], refs[1:2], refs[2:3], refs[3:5]]
    other = [refs[5:6], refs[6:8], refs[8:10], refs[10:12]]
    w, up, out, ids_out, ids, made, sem, ids_sem = refs[12:]
    core, flip = where[1], where[5]
    for k, group in enumerate(own):
        for j in range(8):
            ref, at = (group[0], j) if len(group) == 1 else (group[j // 4], j % 4)
            rows = ref[at, ROWS:].astype(F32).astype(jnp.int32)
            ids[k * 8 + j : k * 8 + j + 1] = rows[:1]
    sends = [pltpu.make_async_copy(ids, ids_out, ids_sem)]
    sends[0].start()
    across = (where[7] + STEPS[3]) & 3
    other_delta = slope_of(other[3], before[...], up[1], w, 1 - core, across, flip)
    delta = jnp.concatenate([own_delta[...], other_delta], axis=1)
    for k in range(4):
        mine = (where[6] + STEPS[k]) & 3
        tokens, places = [], []
        for j in range(8):
            m, n = j % 2, j // 2
            theirs = (where[7] + STEPS[n]) & 3
            tokens.append(jnp.concatenate([piece(own[k], m, theirs), piece(other[n], m, mine)], axis=0))
            z, x = jnp.where(core == 0, mine, theirs), jnp.where(core == 0, theirs, mine)
            places.append((x * 16, z * 2 + (m ^ flip)))
        part = (nn(delta, jnp.concatenate(tokens, axis=1)) / 1536.0).astype(BF)
        for j, (quarter, row) in enumerate(places):
            made[k, j] = part[:, j * 128 : (j + 1) * 128].reshape(16, 16, 128)
            sends.append(pltpu.make_async_copy(made.at[k, j], out.at[pl.ds(quarter, 16), row], sem.at[k, j]))
            sends[-1].start()
    for send in sends:
        send.wait()


def gradient_pieces(own_delta, before, own, other, w, up):
    vmem = pl.BlockSpec(memory_space=pltpu.VMEM)
    return pl.pallas_call(
        gradient_kernel,
        out_shape=[pltpu.HBM((64, 8, 16, 128), BF), pltpu.HBM((32, 128), jnp.int32)],
        in_specs=[vmem] * 16,
        out_specs=[pl.BlockSpec(memory_space=pltpu.HBM)] * 2,
        scratch_shapes=[
            pltpu.VMEM((32, 128), jnp.int32),
            pltpu.VMEM((4, 8, 16, 16, 128), BF),
            pltpu.SemaphoreType.DMA((4, 8)),
            pltpu.SemaphoreType.DMA,
        ],
        compiler_params=params(10),
        cost_estimate=cost(3 * 768 * 4096 * 256, 12 * MIB),
        name="gradient",
    )(own_delta, before, *own, *other, w, up)


def route_kernel(source, pieces, out):
    def some(n, c):
        for k in range(16):
            at = source[n * 16 + k]
            out[n * 16 + k] = (pieces[at].astype(F32) + pieces[at + 256].astype(F32)).astype(BF)
        return c

    lax.fori_loop(0, 16, some, 0)


def route(source, pieces):
    vmem = pl.BlockSpec(memory_space=pltpu.VMEM)
    out = pl.pallas_call(
        route_kernel,
        out_shape=jax.ShapeDtypeStruct((256, 16, 128), BF),
        in_specs=[pl.BlockSpec(memory_space=pltpu.SMEM), vmem],
        out_specs=vmem,
        compiler_params=params(16),
        cost_estimate=cost(0, 3 * MIB),
        name="route",
    )(source, pieces.reshape(512, 16, 128))
    return out.reshape(64, 4, 16, 128)


def collect(core, mine, theirs, slot, grad_t):
    for quarter in range(4):
        cols = slice(quarter * 128, (quarter + 1) * 128)
        part = slice(quarter * 16, (quarter + 1) * 16)
        grad_t[pl.ds(pl.multiple_of(core * 256, 256), 256), cols] = mine[part, slot].reshape(256, 128)
        grad_t[pl.ds(pl.multiple_of(256 - core * 256, 256), 256), cols] = theirs[part, slot].reshape(256, 128)


def hand_out(where, second, keep, send, slot, full):
    full[...] = second
    mean_square = jnp.sum(second * second, keepdims=True) * (1.0 / (BLOCK * BLOCK))
    scale = lax.rsqrt(mean_square + floor_eps)
    keep[slot] = (full[pl.ds(pl.multiple_of(where[0] * 128, 128), 128)] * scale).astype(BF)
    send[slot] = (full[pl.ds(pl.multiple_of(where[3] * 128, 128), 128)] * scale).astype(BF)


def fetch_kernel(slot_at, roots, statistics, pairs, statistic, sem):
    where = whereabouts()
    loads = [pltpu.make_async_copy(roots.at[slot_at[where[4] + k]], pairs.at[k], sem.at[k]) for k in range(4)]
    loads.append(pltpu.make_async_copy(statistics.at[slot_at[where[4]]], statistic, sem.at[4]))
    for load in loads:
        load.start()
    for load in loads:
        load.wait()


def fetch(slot_at, roots, statistics):
    smem = pl.BlockSpec(memory_space=pltpu.SMEM)
    vmem = pl.BlockSpec(memory_space=pltpu.VMEM)
    hbm = pl.BlockSpec(memory_space=pl.ANY)
    return pl.pallas_call(
        fetch_kernel,
        out_shape=[jax.ShapeDtypeStruct((4, 2, BLOCK, BLOCK), BF), jax.ShapeDtypeStruct((2, BLOCK, BLOCK), BF)],
        in_specs=[smem, hbm, hbm],
        out_specs=[vmem, vmem],
        scratch_shapes=[pltpu.SemaphoreType.DMA((5,))],
        compiler_params=params(8),
        cost_estimate=cost(0, 9 * MIB),
        name="fetch",
    )(slot_at, *in_hbm(roots, statistics))


def half_block(ref, slot):
    return jnp.concatenate([ref[q * 16 : (q + 1) * 16, slot].reshape(256, 128) for q in range(4)], axis=1)


def half_kernel(mine, pairs, firsts):
    for k in range(3):
        firsts[k] = nt(pairs[k + 1, 0], half_block(mine, k + 1)).astype(BF)


def half_of_firsts(mine, pairs):
    vmem = pl.BlockSpec(memory_space=pltpu.VMEM)
    return pl.pallas_call(
        half_kernel,
        out_shape=jax.ShapeDtypeStruct((3, BLOCK, 256), BF),
        in_specs=[vmem, vmem],
        out_specs=vmem,
        compiler_params=params(12),
        cost_estimate=cost(3 * BLOCK**3, 2 * MIB),
        name="half",
    )(mine, pairs)


def stored_kernel(firsts, theirs, pairs, keep, send, full):
    where = whereabouts()
    mine = pl.ds(pl.multiple_of(where[1] * 256, 256), 256)
    rest = pl.ds(pl.multiple_of(256 - where[1] * 256, 256), 256)
    others = [nt(pairs[k + 1, 0], half_block(theirs, k + 1)).astype(BF) for k in range(3)]
    seconds = [nn(firsts[k], pairs[k + 1, 1, mine]) + nn(others[k], pairs[k + 1, 1, rest]) for k in range(3)]
    for k in range(3):
        hand_out(where, seconds[k], keep, send, k, full.at[k])


def stored_slots(firsts, theirs, pairs):
    vmem = pl.BlockSpec(memory_space=pltpu.VMEM)
    return pl.pallas_call(
        stored_kernel,
        out_shape=[jax.ShapeDtypeStruct((3, 128, BLOCK), BF)] * 2,
        in_specs=[vmem] * 3,
        out_specs=[vmem, vmem],
        scratch_shapes=[pltpu.VMEM((3, BLOCK, BLOCK), F32)],
        compiler_params=params(20),
        cost_estimate=cost(9 * BLOCK**3, 4 * MIB),
        name="stored",
    )(firsts, theirs, pairs)


def symmetric_product(x, y):
    top = nn(x[:256], y)
    corner = nn(x[256:], y[:, 256:])
    return jnp.concatenate([top, jnp.concatenate([top[:, 256:].T, corner], axis=1)], axis=0)


def product(a, b):
    (c, x), (d, y) = a, b
    xy = symmetric_product(x.astype(BF), y.astype(BF))
    return c * d, xy + (c * y + d * x if c and d else d * x if d else c * y)


def square(a):
    c, x = a
    x_rounded = x.astype(BF)
    return c * c, symmetric_product(x_rounded, x_rounded) + (2.0 * c) * x


def scaled_factor(power):
    return 1.25, -0.25 * power


def inverse_roots(matrices):
    eye = unit(BLOCK, F32)
    powers = [matrix / jnp.sum(matrix * eye, keepdims=True) for matrix in matrices]
    results = [scaled_factor(power) for power in powers]
    factors = results
    for sweep in range(2):
        fourths = [square(factor) for factor in factors]
        fourths = [square(fourth) for fourth in fourths]
        powers = [product(fourth, (0.0, power))[1] for fourth, power in zip(fourths, powers)]
        factors = [scaled_factor(power) for power in powers]
        results = [product(result, factor) for result, factor in zip(results, factors)]
    return [(c * eye + x).astype(BF) for c, x in results]


def refresh_kernel(slot_at, mine, theirs, pairs, statistic, keep, send, grad_t, full, pair):
    where = whereabouts()
    collect(where[1], mine, theirs, 0, grad_t)
    g_t = grad_t[...]
    is_fresh = slot_at[8] > where[4] // 4

    @pl.when(jnp.logical_not(is_fresh))
    def _():
        pair[...] = pairs[0]

    @pl.when(is_fresh)
    def _():
        eye = unit(BLOCK, F32)
        g = nt(unit(BLOCK, BF), g_t).astype(BF)
        outers = [nt(g, g), nt(g_t, g_t)]
        matrices = [decay * statistic[k].astype(F32) + outers[k] + jitter * eye for k in range(2)]
        pair[0], pair[1] = inverse_roots(matrices)

    first = nt(pair[0], g_t).astype(BF)
    hand_out(where, nn(first, pair[1]), keep, send, 0, full)


def refresh(slot_at, mine, theirs, pairs, statistic):
    smem = pl.BlockSpec(memory_space=pltpu.SMEM)
    vmem = pl.BlockSpec(memory_space=pltpu.VMEM)
    return pl.pallas_call(
        refresh_kernel,
        out_shape=[jax.ShapeDtypeStruct((1, 128, BLOCK), BF)] * 2,
        in_specs=[smem] + [vmem] * 4,
        out_specs=[vmem, vmem],
        scratch_shapes=[
            pltpu.VMEM((BLOCK, BLOCK), BF),
            pltpu.VMEM((BLOCK, BLOCK), F32),
            pltpu.VMEM((2, BLOCK, BLOCK), BF),
        ],
        compiler_params=params(32),
        cost_estimate=cost(42 * BLOCK**3, 4 * MIB),
        name="refresh",
    )(slot_at, mine, theirs, pairs, statistic)


def copy_all(copies):
    for copy in copies:
        copy.start()
    for copy in copies:
        copy.wait()


def assemble_kernel(slot_at, fresh, mine, theirs, out, sem):
    here = whereabouts()[4]
    copies = [pltpu.make_async_copy(fresh.at[0], out.at[slot_at[here]], sem.at[6])]
    for k in range(3):
        copies.append(pltpu.make_async_copy(mine.at[k], out.at[slot_at[here + k + 1]], sem.at[k]))
        copies.append(pltpu.make_async_copy(theirs.at[k], out.at[slot_at[4 - here + k + 1]], sem.at[k + 3]))
    for copy in copies:
        copy.start()
    for copy in copies:
        copy.wait()


def assemble(slot_at, *parts):
    hbm = pl.BlockSpec(memory_space=pl.ANY)
    return pl.pallas_call(
        assemble_kernel,
        out_shape=pltpu.HBM((8, 128, BLOCK), BF),
        in_specs=[pl.BlockSpec(memory_space=pltpu.SMEM)] + [hbm] * 3,
        out_specs=pl.BlockSpec(memory_space=pltpu.HBM),
        scratch_shapes=[pltpu.SemaphoreType.DMA((7,))],
        compiler_params=params(4),
        cost_estimate=cost(0, 2 * MIB),
        name="assemble",
    )(slot_at, *parts)


def shards(tokens, in_weight, upstream, slot_block, refreshed, statistics, roots):
    both = ("grp", "dev")

    first = prepare(tokens, slot_block)
    first = lax.all_to_all(first, both, 0, 0, tiled=True, axis_index_groups=STAGE1)
    w, up = half_of_weights(in_weight, upstream)
    below = lax.ppermute(first, both, UP)
    above = lax.ppermute(first, both, DOWN)
    acc = first_of_own(first, w)
    shared, acc = lax.optimization_barrier((first, acc))
    below, above = lax.optimization_barrier((below, above))
    own = [first, below, above]
    halves = [below[:4], below[4:], above[:4], above[4:]]
    own += [lax.ppermute(halves[0], both, UP), lax.ppermute(halves[3], both, DOWN)]
    other = [lax.ppermute(part, "grp", CORE) for part in (shared, *halves)]
    acc = more_of_own(acc, below, above, w)
    acc, own[3:], other[1:3] = lax.optimization_barrier((acc, own[3:], other[1:3]))
    other_acc = forward_of_other(other[:5], w)
    other += [lax.ppermute(part, "grp", CORE) for part in own[3:]]
    own_delta = own_slope(acc, own[3:], w, up)
    pieces, all_ids = gradient_pieces(own_delta, other_acc, own, other, w, up)
    pieces = lax.all_to_all(pieces, both, 0, 0, tiled=True, axis_index_groups=SAME_CORE)
    source, slot_at = slot_order(all_ids, refreshed, slot_block)
    pairs, statistic = fetch(slot_at, roots, statistics)
    source, pairs, statistic = lax.optimization_barrier((source, pairs, statistic))
    pieces = route(source, pieces)
    mine = lax.all_to_all(pieces, both, 0, 0, tiled=True, axis_index_groups=SAME_CORE)
    theirs = lax.ppermute(mine, "grp", CORE)

    keep, send = stored_slots(half_of_firsts(mine, pairs), theirs, pairs)
    other_keep = lax.ppermute(send, "grp", CHIP)
    mine, theirs, keep = lax.optimization_barrier((mine, theirs, keep))
    fresh_keep, fresh_send = refresh(slot_at, mine, theirs, pairs, statistic)
    fresh_other = lax.ppermute(fresh_send, "grp", CHIP)
    update = assemble(slot_at, fresh_keep, keep, other_keep)
    return lax.dynamic_update_slice_in_dim(update, fresh_other, slot_at[4 - 4 * (lax.axis_index("grp") // 2)], 0)


def solution(mesh):
    return jax.shard_map(
        shards,
        mesh=mesh,
        in_specs=(
            P(None, "dev"),
            P(None, "dev"),
            P(None, "dev"),
            P("dev"),
            P(),
            P("dev", None, None, None),
            P("dev", None, None, None),
        ),
        out_specs=P("dev", "grp", None),
        check_vma=False,
    )
```

```python
import functools

import jax
import jax.numpy as jnp
from jax import lax
from jax.experimental import pallas as pl
from jax.experimental.pallas import tpu as pltpu
from jax.sharding import PartitionSpec as P

decay = 0.9
jitter = 1e-06
floor_eps = 1e-06

ROWS = 384
IDS = 16
BLOCK = 512
BF = jnp.bfloat16
F32 = jnp.float32
MIB = 1 << 20

CORE = [(0, 1), (1, 0), (2, 3), (3, 2)]
CHIP = [(0, 2), (2, 0), (1, 3), (3, 1)]
def device(chip, core, z, y_hi, x):
    return (chip * 2 + core) * 32 + z * 8 + y_hi * 4 + x


def on_rings(chip, core, y_hi, first, second):
    return device(chip, core, second, y_hi, first) if core == 0 else device(chip, core, first, y_hi, second)


STAGE1 = [
    [on_rings(m, core, m ^ flip, i, a) for m in range(2) for i in range(4)]
    for core in range(2)
    for a in range(4)
    for flip in range(2)
]
EVERYWHERE = [
    (chip, core, z, y_hi, x)
    for chip in range(2)
    for core in range(2)
    for z in range(4)
    for y_hi in range(2)
    for x in range(4)
]


def along(step):
    return [
        (
            device(chip, core, z, y_hi, x),
            device(chip, core, z, y_hi, (x + step) % 4) if core else device(chip, core, (z + step) % 4, y_hi, x),
        )
        for chip, core, z, y_hi, x in EVERYWHERE
    ]


UP, DOWN = along(1), along(-1)
STEPS = (0, -1, 1, 2)
SAME_CORE = [[chip * 64 + core * 32 + d for chip in range(2) for d in range(32)] for core in range(2)]


def params(mib):
    return pltpu.CompilerParams(vmem_limit_bytes=mib * MIB)


def cost(flops, nbytes):
    return pl.CostEstimate(flops=flops, bytes_accessed=nbytes, transcendentals=0)


def in_hbm(*arrays):
    return [pltpu.with_memory_space_constraint(array, pltpu.HBM) for array in arrays]


def nt(a, b):
    return lax.dot_general(a, b, (((1,), (1,)), ((), ())), preferred_element_type=F32)


def nn(a, b):
    return jnp.dot(a, b, preferred_element_type=F32)


def whereabouts():
    group, d = lax.axis_index("grp"), lax.axis_index("dev")
    core, chip = group & 1, group >> 1
    z, y_hi, x = d >> 3, (d >> 2) & 1, d & 3
    places = [jnp.where(core == 0, z, x), jnp.where(core == 0, x, z)]
    return [group, core, group ^ 1, group ^ 2, 4 * chip, y_hi ^ chip, *places]


def unit(n, dtype):
    row = lax.broadcasted_iota(jnp.int32, (n, n), 0)
    col = lax.broadcasted_iota(jnp.int32, (n, n), 1)
    return jnp.where(row == col, 1.0, 0.0).astype(dtype)


def gelu_slope(values):
    return (
        0.5 * (1.0 + lax.erf(values * 0.7071067811865476))
        + values * jnp.exp(-0.5 * values * values) * 0.3989422804014327
    )


def spare_position(k):
    return jnp.where(k < 3, 7 - k, jnp.where(k < 6, 6 - k, jnp.where(k == 6, 4, 0)))


def place(flag, fresh_seen, spare_seen):
    return jnp.minimum(jnp.where(flag == 1, 4 * fresh_seen, spare_position(spare_seen)), 7)


def order_kernel(ids, refreshed, slot_block, source, slot_at, table):
    where = whereabouts()

    def clear(k, c):
        table[k] = 0
        return c

    def mark(k, c):
        table[refreshed[k]] = 1
        return c

    lax.fori_loop(0, 256, clear, 0, unroll=8)
    lax.fori_loop(0, 32, mark, 0, unroll=8)

    def positions(blocks):
        flags = [table[block] for block in blocks]
        fresh_seen = jnp.int32(0)
        spare_seen = jnp.int32(0)
        found = []
        for flag in flags:
            found.append(place(flag, fresh_seen, spare_seen))
            fresh_seen += flag
            spare_seen += 1 - flag
        return found, fresh_seen

    def owner(o, c):
        z, y_hi, x = o >> 3, (o >> 2) & 1, o & 3
        across = jnp.where(where[1] == 0, z, x)
        inner = jnp.where(where[1] == 0, x, z)
        step = (across - where[6]) & 3
        group = jnp.where(step == 0, 0, jnp.where(step == 3, 1, step + 1))
        piece = group * 8 + (y_hi ^ where[5]) * 4 + inner
        blocks = [ids[piece, p] for p in range(8)]
        found, _ = positions(blocks)
        for block, position in zip(blocks, found):
            source[(position >> 2) * 128 + o * 4 + (position & 3)] = (block & 31) * 8 + (block >> 5)
        return c

    lax.fori_loop(0, 32, owner, 0)
    found, fresh_seen = positions([slot_block[p] for p in range(8)])
    for p in range(8):
        slot_at[found[p]] = p
    slot_at[8] = fresh_seen


def slot_order(ids, refreshed, slot_block):
    smem = pl.BlockSpec(memory_space=pltpu.SMEM)
    return pl.pallas_call(
        order_kernel,
        out_shape=[jax.ShapeDtypeStruct((256,), jnp.int32), jax.ShapeDtypeStruct((16,), jnp.int32)],
        in_specs=[smem] * 3,
        out_specs=[smem] * 2,
        scratch_shapes=[pltpu.SMEM((256,), jnp.int32)],
        cost_estimate=cost(0, 4096),
        name="order",
    )(ids, refreshed, slot_block)


def prepare_kernel(tokens, slot_block, out, ids, sem, id_sem):
    where = whereabouts()
    load_ids = pltpu.make_async_copy(slot_block, ids, id_sem)
    load_ids.start()
    loads = []
    for m in range(2):
        rows = pl.ds(pl.multiple_of((2 * m + where[1]) * ROWS, ROWS), ROWS)
        for i in range(4):
            k = 4 * m + i
            loads.append(pltpu.make_async_copy(tokens.at[rows], out.at[k, pl.ds(0, ROWS)], sem.at[k]))
    for load in loads:
        load.start()
    row = lax.broadcasted_iota(jnp.int32, (IDS, 128), 0)
    lane = lax.broadcasted_iota(jnp.int32, (IDS, 128), 1)
    tile = jnp.zeros((IDS, 128), jnp.int32)
    load_ids.wait()
    for p in range(8):
        tile = jnp.where((row == 0) & (lane == p), ids[p], tile)
    tile = tile.astype(F32).astype(BF)
    for k in range(8):
        out[k, ROWS:] = tile
    for load in loads:
        load.wait()


def prepare(tokens, slot_block):
    hbm = pl.BlockSpec(memory_space=pl.ANY)
    return pl.pallas_call(
        prepare_kernel,
        out_shape=jax.ShapeDtypeStruct((8, ROWS + IDS, 128), BF),
        in_specs=[hbm, hbm],
        out_specs=pl.BlockSpec(memory_space=pltpu.VMEM),
        scratch_shapes=[pltpu.SMEM((8,), jnp.int32), pltpu.SemaphoreType.DMA((8,)), pltpu.SemaphoreType.DMA],
        compiler_params=params(8),
        cost_estimate=cost(0, MIB),
        name="prepare",
    )(*in_hbm(tokens, slot_block))


def weights_kernel(weight, upstream, w, up, sem):
    where = whereabouts()
    cols = pl.ds(pl.multiple_of(where[1] * 256, 256), 256)
    loads = [pltpu.make_async_copy(weight.at[:, cols], w, sem.at[2])]
    for k in range(2):
        rows = pl.ds(pl.multiple_of(where[2 * k] * ROWS, ROWS), ROWS)
        loads.append(pltpu.make_async_copy(upstream.at[rows, cols], up.at[k], sem.at[k]))
    for load in loads:
        load.start()
    for load in loads:
        load.wait()


def half_of_weights(in_weight, upstream):
    vmem = pl.BlockSpec(memory_space=pltpu.VMEM)
    hbm = pl.BlockSpec(memory_space=pl.ANY)
    return pl.pallas_call(
        weights_kernel,
        out_shape=[jax.ShapeDtypeStruct((4096, 256), BF), jax.ShapeDtypeStruct((2, ROWS, 256), BF)],
        in_specs=[hbm, hbm],
        out_specs=[vmem, vmem],
        scratch_shapes=[pltpu.SemaphoreType.DMA((3,))],
        compiler_params=params(4),
        cost_estimate=cost(0, 5 * MIB),
        name="weights",
    )(*in_hbm(in_weight, upstream))


def piece(group, m, i):
    return group[0][m * 4 + i, :ROWS] if len(group) == 1 else group[m][i, :ROWS]


def group_product(group, w, core, across, flip):
    tokens = jnp.concatenate([piece(group, j // 4, j % 4) for j in range(8)], axis=1)
    weights = []
    for j in range(8):
        row = jnp.where(core == 0, across * 1024 + j % 4 * 128, j % 4 * 1024 + across * 128) + ((j // 4) ^ flip) * 512
        weights.append(w[pl.ds(pl.multiple_of(row, 128), 128)])
    return nn(tokens, jnp.concatenate(weights, axis=0))


def first_kernel(first, w, acc):
    where = whereabouts()
    acc[...] = group_product([first], w, where[1], where[6], where[5])


def first_of_own(first, w):
    vmem = pl.BlockSpec(memory_space=pltpu.VMEM)
    return pl.pallas_call(
        first_kernel,
        out_shape=jax.ShapeDtypeStruct((ROWS, 256), F32),
        in_specs=[vmem] * 2,
        out_specs=vmem,
        compiler_params=params(8),
        cost_estimate=cost(2 * ROWS * 1024 * 256, 2 * MIB),
        name="first",
    )(first, w)


def own_kernel(before, below, above, w, acc):
    where = whereabouts()
    total = before[...]
    for ref, step in ((below, STEPS[1]), (above, STEPS[2])):
        total = total + group_product([ref], w, where[1], (where[6] + step) & 3, where[5])
    acc[...] = total


def more_of_own(before, below, above, w):
    vmem = pl.BlockSpec(memory_space=pltpu.VMEM)
    return pl.pallas_call(
        own_kernel,
        out_shape=jax.ShapeDtypeStruct((ROWS, 256), F32),
        in_specs=[vmem] * 4,
        out_specs=vmem,
        compiler_params=params(8),
        cost_estimate=cost(2 * ROWS * 2048 * 256, 2 * MIB),
        name="own",
    )(before, below, above, w)


def other_kernel(*refs):
    where = whereabouts()
    w, acc = refs[5:]
    total = None
    for group, step in zip([refs[0:1], refs[1:3], refs[3:5]], STEPS):
        part = group_product(group, w, 1 - where[1], (where[7] + step) & 3, where[5])
        total = part if total is None else total + part
    acc[...] = total


def forward_of_other(other, w):
    vmem = pl.BlockSpec(memory_space=pltpu.VMEM)
    return pl.pallas_call(
        other_kernel,
        out_shape=jax.ShapeDtypeStruct((ROWS, 256), F32),
        in_specs=[vmem] * 6,
        out_specs=vmem,
        compiler_params=params(8),
        cost_estimate=cost(2 * ROWS * 3072 * 256, 2 * MIB),
        name="other",
    )(*other, w)


def slope_of(group, before, up, w, core, across, flip):
    pre = before + group_product(group, w, core, across, flip)
    delta = (up.astype(F32) * gelu_slope(pre)).astype(BF)
    return nt(unit(256, BF), delta).astype(BF)


def slope_kernel(before, low, high, w, up, out):
    where = whereabouts()
    across = (where[6] + STEPS[3]) & 3
    out[...] = slope_of([low, high], before[...], up[0], w, where[1], across, where[5])


def own_slope(before, far, w, up):
    vmem = pl.BlockSpec(memory_space=pltpu.VMEM)
    return pl.pallas_call(
        slope_kernel,
        out_shape=jax.ShapeDtypeStruct((256, ROWS), BF),
        in_specs=[vmem] * 5,
        out_specs=vmem,
        compiler_params=params(8),
        cost_estimate=cost(2 * ROWS * 1024 * 256, 2 * MIB),
        name="slope",
    )(before, *far, w, up)


def gradient_kernel(own_delta, before, *refs):
    where = whereabouts()
    own = [refs[0:1], refs[1:2], refs[2:3], refs[3:5]]
    other = [refs[5:6], refs[6:8], refs[8:10], refs[10:12]]
    w, up, out, ids_out, ids, made, sem, ids_sem = refs[12:]
    core, flip = where[1], where[5]
    for k, group in enumerate(own):
        for j in range(8):
            ref, at = (group[0], j) if len(group) == 1 else (group[j // 4], j % 4)
            rows = ref[at, ROWS:].astype(F32).astype(jnp.int32)
            ids[k * 8 + j : k * 8 + j + 1] = rows[:1]
    sends = [pltpu.make_async_copy(ids, ids_out, ids_sem)]
    sends[0].start()
    across = (where[7] + STEPS[3]) & 3
    other_delta = slope_of(other[3], before[...], up[1], w, 1 - core, across, flip)
    delta = jnp.concatenate([own_delta[...], other_delta], axis=1)
    for k in range(4):
        mine = (where[6] + STEPS[k]) & 3
        tokens, places = [], []
        for j in range(8):
            m, n = j % 2, j // 2
            theirs = (where[7] + STEPS[n]) & 3
            tokens.append(jnp.concatenate([piece(own[k], m, theirs), piece(other[n], m, mine)], axis=0))
            z, x = jnp.where(core == 0, mine, theirs), jnp.where(core == 0, theirs, mine)
            places.append((x * 16, z * 2 + (m ^ flip)))
        part = (nn(delta, jnp.concatenate(tokens, axis=1)) / 1536.0).astype(BF)
        for j, (quarter, row) in enumerate(places):
            made[k, j] = part[:, j * 128 : (j + 1) * 128].reshape(16, 16, 128)
            sends.append(pltpu.make_async_copy(made.at[k, j], out.at[pl.ds(quarter, 16), row], sem.at[k, j]))
            sends[-1].start()
    for send in sends:
        send.wait()


def gradient_pieces(own_delta, before, own, other, w, up):
    vmem = pl.BlockSpec(memory_space=pltpu.VMEM)
    return pl.pallas_call(
        gradient_kernel,
        out_shape=[pltpu.HBM((64, 8, 16, 128), BF), pltpu.HBM((32, 128), jnp.int32)],
        in_specs=[vmem] * 16,
        out_specs=[pl.BlockSpec(memory_space=pltpu.HBM)] * 2,
        scratch_shapes=[
            pltpu.VMEM((32, 128), jnp.int32),
            pltpu.VMEM((4, 8, 16, 16, 128), BF),
            pltpu.SemaphoreType.DMA((4, 8)),
            pltpu.SemaphoreType.DMA,
        ],
        compiler_params=params(10),
        cost_estimate=cost(3 * 768 * 4096 * 256, 12 * MIB),
        name="gradient",
    )(own_delta, before, *own, *other, w, up)


def route_kernel(source, pieces, out):
    def some(n, c):
        for k in range(16):
            at = source[n * 16 + k]
            out[n * 16 + k] = (pieces[at].astype(F32) + pieces[at + 256].astype(F32)).astype(BF)
        return c

    lax.fori_loop(0, 16, some, 0)


def route(source, pieces):
    vmem = pl.BlockSpec(memory_space=pltpu.VMEM)
    out = pl.pallas_call(
        route_kernel,
        out_shape=jax.ShapeDtypeStruct((256, 16, 128), BF),
        in_specs=[pl.BlockSpec(memory_space=pltpu.SMEM), vmem],
        out_specs=vmem,
        compiler_params=params(16),
        cost_estimate=cost(0, 3 * MIB),
        name="route",
    )(source, pieces.reshape(512, 16, 128))
    return out.reshape(64, 4, 16, 128)


def collect(core, mine, theirs, slot, grad_t):
    for quarter in range(4):
        cols = slice(quarter * 128, (quarter + 1) * 128)
        part = slice(quarter * 16, (quarter + 1) * 16)
        grad_t[pl.ds(pl.multiple_of(core * 256, 256), 256), cols] = mine[part, slot].reshape(256, 128)
        grad_t[pl.ds(pl.multiple_of(256 - core * 256, 256), 256), cols] = theirs[part, slot].reshape(256, 128)


def hand_out(where, second, keep, send, slot, full):
    full[...] = second
    mean_square = jnp.sum(second * second, keepdims=True) * (1.0 / (BLOCK * BLOCK))
    scale = lax.rsqrt(mean_square + floor_eps)
    keep[slot] = (full[pl.ds(pl.multiple_of(where[0] * 128, 128), 128)] * scale).astype(BF)
    send[slot] = (full[pl.ds(pl.multiple_of(where[3] * 128, 128), 128)] * scale).astype(BF)


def fetch_kernel(slot_at, roots, statistics, pairs, statistic, sem):
    where = whereabouts()
    loads = [pltpu.make_async_copy(roots.at[slot_at[where[4] + k]], pairs.at[k], sem.at[k]) for k in range(4)]
    loads.append(pltpu.make_async_copy(statistics.at[slot_at[where[4]]], statistic, sem.at[4]))
    for load in loads:
        load.start()
    for load in loads:
        load.wait()


def fetch(slot_at, roots, statistics):
    smem = pl.BlockSpec(memory_space=pltpu.SMEM)
    vmem = pl.BlockSpec(memory_space=pltpu.VMEM)
    hbm = pl.BlockSpec(memory_space=pl.ANY)
    return pl.pallas_call(
        fetch_kernel,
        out_shape=[jax.ShapeDtypeStruct((4, 2, BLOCK, BLOCK), BF), jax.ShapeDtypeStruct((2, BLOCK, BLOCK), BF)],
        in_specs=[smem, hbm, hbm],
        out_specs=[vmem, vmem],
        scratch_shapes=[pltpu.SemaphoreType.DMA((5,))],
        compiler_params=params(8),
        cost_estimate=cost(0, 9 * MIB),
        name="fetch",
    )(slot_at, *in_hbm(roots, statistics))


def half_block(ref, slot):
    return jnp.concatenate([ref[q * 16 : (q + 1) * 16, slot].reshape(256, 128) for q in range(4)], axis=1)


def half_kernel(mine, pairs, firsts):
    for k in range(3):
        firsts[k] = nt(pairs[k + 1, 0], half_block(mine, k + 1)).astype(BF)


def half_of_firsts(mine, pairs):
    vmem = pl.BlockSpec(memory_space=pltpu.VMEM)
    return pl.pallas_call(
        half_kernel,
        out_shape=jax.ShapeDtypeStruct((3, BLOCK, 256), BF),
        in_specs=[vmem, vmem],
        out_specs=vmem,
        compiler_params=params(12),
        cost_estimate=cost(3 * BLOCK**3, 2 * MIB),
        name="half",
    )(mine, pairs)


def stored_kernel(firsts, theirs, pairs, keep, send, full):
    where = whereabouts()
    mine = pl.ds(pl.multiple_of(where[1] * 256, 256), 256)
    rest = pl.ds(pl.multiple_of(256 - where[1] * 256, 256), 256)
    others = [nt(pairs[k + 1, 0], half_block(theirs, k + 1)).astype(BF) for k in range(3)]
    seconds = [nn(firsts[k], pairs[k + 1, 1, mine]) + nn(others[k], pairs[k + 1, 1, rest]) for k in range(3)]
    for k in range(3):
        hand_out(where, seconds[k], keep, send, k, full.at[k])


def stored_slots(firsts, theirs, pairs):
    vmem = pl.BlockSpec(memory_space=pltpu.VMEM)
    return pl.pallas_call(
        stored_kernel,
        out_shape=[jax.ShapeDtypeStruct((3, 128, BLOCK), BF)] * 2,
        in_specs=[vmem] * 3,
        out_specs=[vmem, vmem],
        scratch_shapes=[pltpu.VMEM((3, BLOCK, BLOCK), F32)],
        compiler_params=params(20),
        cost_estimate=cost(9 * BLOCK**3, 4 * MIB),
        name="stored",
    )(firsts, theirs, pairs)


def symmetric_product(x, y):
    top = nn(x[:256], y)
    corner = nn(x[256:], y[:, 256:])
    return jnp.concatenate([top, jnp.concatenate([top[:, 256:].T, corner], axis=1)], axis=0)


def product(a, b):
    (c, x), (d, y) = a, b
    xy = symmetric_product(x.astype(BF), y.astype(BF))
    return c * d, xy + (c * y + d * x if c and d else d * x if d else c * y)


def square(a):
    c, x = a
    x_rounded = x.astype(BF)
    return c * c, symmetric_product(x_rounded, x_rounded) + (2.0 * c) * x


def scaled_factor(power):
    return 1.25, -0.25 * power


def inverse_roots(matrices):
    eye = unit(BLOCK, F32)
    powers = [matrix / jnp.sum(matrix * eye, keepdims=True) for matrix in matrices]
    results = [scaled_factor(power) for power in powers]
    factors = results
    for sweep in range(2):
        fourths = [square(factor) for factor in factors]
        fourths = [square(fourth) for fourth in fourths]
        powers = [product(fourth, (0.0, power))[1] for fourth, power in zip(fourths, powers)]
        factors = [scaled_factor(power) for power in powers]
        results = [product(result, factor) for result, factor in zip(results, factors)]
    return [(c * eye + x).astype(BF) for c, x in results]


def refresh_kernel(slot_at, mine, theirs, pairs, statistic, keep, send, grad_t, full, pair):
    where = whereabouts()
    collect(where[1], mine, theirs, 0, grad_t)
    g_t = grad_t[...]
    is_fresh = slot_at[8] > where[4] // 4

    @pl.when(jnp.logical_not(is_fresh))
    def _():
        pair[...] = pairs[0]

    @pl.when(is_fresh)
    def _():
        eye = unit(BLOCK, F32)
        g = nt(unit(BLOCK, BF), g_t).astype(BF)
        outers = [nt(g, g), nt(g_t, g_t)]
        matrices = [decay * statistic[k].astype(F32) + outers[k] + jitter * eye for k in range(2)]
        pair[0], pair[1] = inverse_roots(matrices)

    first = nt(pair[0], g_t).astype(BF)
    hand_out(where, nn(first, pair[1]), keep, send, 0, full)


def refresh(slot_at, mine, theirs, pairs, statistic):
    smem = pl.BlockSpec(memory_space=pltpu.SMEM)
    vmem = pl.BlockSpec(memory_space=pltpu.VMEM)
    return pl.pallas_call(
        refresh_kernel,
        out_shape=[jax.ShapeDtypeStruct((1, 128, BLOCK), BF)] * 2,
        in_specs=[smem] + [vmem] * 4,
        out_specs=[vmem, vmem],
        scratch_shapes=[
            pltpu.VMEM((BLOCK, BLOCK), BF),
            pltpu.VMEM((BLOCK, BLOCK), F32),
            pltpu.VMEM((2, BLOCK, BLOCK), BF),
        ],
        compiler_params=params(32),
        cost_estimate=cost(42 * BLOCK**3, 4 * MIB),
        name="refresh",
    )(slot_at, mine, theirs, pairs, statistic)


def copy_all(copies):
    for copy in copies:
        copy.start()
    for copy in copies:
        copy.wait()


def assemble_kernel(slot_at, fresh, mine, theirs, out, sem):
    here = whereabouts()[4]
    copies = [pltpu.make_async_copy(fresh.at[0], out.at[slot_at[here]], sem.at[6])]
    for k in range(3):
        copies.append(pltpu.make_async_copy(mine.at[k], out.at[slot_at[here + k + 1]], sem.at[k]))
        copies.append(pltpu.make_async_copy(theirs.at[k], out.at[slot_at[4 - here + k + 1]], sem.at[k + 3]))
    for copy in copies:
        copy.start()
    for copy in copies:
        copy.wait()


def assemble(slot_at, *parts):
    hbm = pl.BlockSpec(memory_space=pl.ANY)
    return pl.pallas_call(
        assemble_kernel,
        out_shape=pltpu.HBM((8, 128, BLOCK), BF),
        in_specs=[pl.BlockSpec(memory_space=pltpu.SMEM)] + [hbm] * 3,
        out_specs=pl.BlockSpec(memory_space=pltpu.HBM),
        scratch_shapes=[pltpu.SemaphoreType.DMA((7,))],
        compiler_params=params(4),
        cost_estimate=cost(0, 2 * MIB),
        name="assemble",
    )(slot_at, *parts)


def shards(tokens, in_weight, upstream, slot_block, refreshed, statistics, roots):
    both = ("grp", "dev")

    first = prepare(tokens, slot_block)
    first = lax.all_to_all(first, both, 0, 0, tiled=True, axis_index_groups=STAGE1)
    w, up = half_of_weights(in_weight, upstream)
    below = lax.ppermute(first, both, UP)
    above = lax.ppermute(first, both, DOWN)
    acc = first_of_own(first, w)
    shared, acc = lax.optimization_barrier((first, acc))
    below, above = lax.optimization_barrier((below, above))
    own = [first, below, above]
    halves = [below[:4], below[4:], above[:4], above[4:]]
    own += [lax.ppermute(halves[0], both, UP), lax.ppermute(halves[3], both, DOWN)]
    acc = more_of_own(acc, below, above, w)
    halves[2:], acc = lax.optimization_barrier((halves[2:], acc))
    other = [lax.ppermute(part, "grp", CORE) for part in (shared, *halves)]
    acc, own[3:], other[1:3] = lax.optimization_barrier((acc, own[3:], other[1:3]))
    other_acc = forward_of_other(other[:5], w)
    other += [lax.ppermute(part, "grp", CORE) for part in own[3:]]
    own_delta = own_slope(acc, own[3:], w, up)
    pieces, all_ids = gradient_pieces(own_delta, other_acc, own, other, w, up)
    pieces = lax.all_to_all(pieces, both, 0, 0, tiled=True, axis_index_groups=SAME_CORE)
    source, slot_at = slot_order(all_ids, refreshed, slot_block)
    pairs, statistic = fetch(slot_at, roots, statistics)
    source, pairs, statistic = lax.optimization_barrier((source, pairs, statistic))
    pieces = route(source, pieces)
    mine = lax.all_to_all(pieces, both, 0, 0, tiled=True, axis_index_groups=SAME_CORE)
    theirs = lax.ppermute(mine, "grp", CORE)

    keep, send = stored_slots(half_of_firsts(mine, pairs), theirs, pairs)
    other_keep = lax.ppermute(send, "grp", CHIP)
    mine, theirs, keep = lax.optimization_barrier((mine, theirs, keep))
    fresh_keep, fresh_send = refresh(slot_at, mine, theirs, pairs, statistic)
    fresh_other = lax.ppermute(fresh_send, "grp", CHIP)
    update = assemble(slot_at, fresh_keep, keep, other_keep)
    return lax.dynamic_update_slice_in_dim(update, fresh_other, slot_at[4 - 4 * (lax.axis_index("grp") // 2)], 0)


def solution(mesh):
    return jax.shard_map(
        shards,
        mesh=mesh,
        in_specs=(
            P(None, "dev"),
            P(None, "dev"),
            P(None, "dev"),
            P("dev"),
            P(),
            P("dev", None, None, None),
            P("dev", None, None, None),
        ),
        out_specs=P("dev", "grp", None),
        check_vma=False,
    )
```

```python
import functools

import jax
import jax.numpy as jnp
from jax import lax
from jax.experimental import pallas as pl
from jax.experimental.pallas import tpu as pltpu
from jax.sharding import PartitionSpec as P

decay = 0.9
jitter = 1e-06
floor_eps = 1e-06

ROWS = 384
IDS = 16
BLOCK = 512
BF = jnp.bfloat16
F32 = jnp.float32
MIB = 1 << 20

CORE = [(0, 1), (1, 0), (2, 3), (3, 2)]
CHIP = [(0, 2), (2, 0), (1, 3), (3, 1)]
def device(chip, core, z, y_hi, x):
    return (chip * 2 + core) * 32 + z * 8 + y_hi * 4 + x


def on_rings(chip, core, y_hi, first, second):
    return device(chip, core, second, y_hi, first) if core == 0 else device(chip, core, first, y_hi, second)


STAGE1 = [
    [on_rings(m, core, m ^ flip, i, a) for m in range(2) for i in range(4)]
    for core in range(2)
    for a in range(4)
    for flip in range(2)
]
EVERYWHERE = [
    (chip, core, z, y_hi, x)
    for chip in range(2)
    for core in range(2)
    for z in range(4)
    for y_hi in range(2)
    for x in range(4)
]


def along(step):
    return [
        (
            device(chip, core, z, y_hi, x),
            device(chip, core, z, y_hi, (x + step) % 4) if core else device(chip, core, (z + step) % 4, y_hi, x),
        )
        for chip, core, z, y_hi, x in EVERYWHERE
    ]


UP, DOWN = along(1), along(-1)
STEPS = (0, -1, 1, 2)
SAME_CORE = [[chip * 64 + core * 32 + d for chip in range(2) for d in range(32)] for core in range(2)]


def params(mib):
    return pltpu.CompilerParams(vmem_limit_bytes=mib * MIB)


def cost(flops, nbytes):
    return pl.CostEstimate(flops=flops, bytes_accessed=nbytes, transcendentals=0)


def in_hbm(*arrays):
    return [pltpu.with_memory_space_constraint(array, pltpu.HBM) for array in arrays]


def nt(a, b):
    return lax.dot_general(a, b, (((1,), (1,)), ((), ())), preferred_element_type=F32)


def nn(a, b):
    return jnp.dot(a, b, preferred_element_type=F32)


def whereabouts():
    group, d = lax.axis_index("grp"), lax.axis_index("dev")
    core, chip = group & 1, group >> 1
    z, y_hi, x = d >> 3, (d >> 2) & 1, d & 3
    places = [jnp.where(core == 0, z, x), jnp.where(core == 0, x, z)]
    return [group, core, group ^ 1, group ^ 2, 4 * chip, y_hi ^ chip, *places]


def unit(n, dtype):
    row = lax.broadcasted_iota(jnp.int32, (n, n), 0)
    col = lax.broadcasted_iota(jnp.int32, (n, n), 1)
    return jnp.where(row == col, 1.0, 0.0).astype(dtype)


def gelu_slope(values):
    return (
        0.5 * (1.0 + lax.erf(values * 0.7071067811865476))
        + values * jnp.exp(-0.5 * values * values) * 0.3989422804014327
    )


def spare_position(k):
    return jnp.where(k < 3, 7 - k, jnp.where(k < 6, 6 - k, jnp.where(k == 6, 4, 0)))


def place(flag, fresh_seen, spare_seen):
    return jnp.minimum(jnp.where(flag == 1, 4 * fresh_seen, spare_position(spare_seen)), 7)


def order_kernel(ids, refreshed, slot_block, source, slot_at, table):
    where = whereabouts()

    def clear(k, c):
        table[k] = 0
        return c

    def mark(k, c):
        table[refreshed[k]] = 1
        return c

    lax.fori_loop(0, 256, clear, 0, unroll=8)
    lax.fori_loop(0, 32, mark, 0, unroll=8)

    def positions(blocks):
        flags = [table[block] for block in blocks]
        fresh_seen = jnp.int32(0)
        spare_seen = jnp.int32(0)
        found = []
        for flag in flags:
            found.append(place(flag, fresh_seen, spare_seen))
            fresh_seen += flag
            spare_seen += 1 - flag
        return found, fresh_seen

    def owner(o, c):
        z, y_hi, x = o >> 3, (o >> 2) & 1, o & 3
        across = jnp.where(where[1] == 0, z, x)
        inner = jnp.where(where[1] == 0, x, z)
        step = (across - where[6]) & 3
        group = jnp.where(step == 0, 0, jnp.where(step == 3, 1, step + 1))
        piece = group * 8 + (y_hi ^ where[5]) * 4 + inner
        blocks = [ids[piece, p] for p in range(8)]
        found, _ = positions(blocks)
        for block, position in zip(blocks, found):
            source[(position >> 2) * 128 + o * 4 + (position & 3)] = (block & 31) * 8 + (block >> 5)
        return c

    lax.fori_loop(0, 32, owner, 0)
    found, fresh_seen = positions([slot_block[p] for p in range(8)])
    for p in range(8):
        slot_at[found[p]] = p
    slot_at[8] = fresh_seen


def slot_order(ids, refreshed, slot_block):
    smem = pl.BlockSpec(memory_space=pltpu.SMEM)
    return pl.pallas_call(
        order_kernel,
        out_shape=[jax.ShapeDtypeStruct((256,), jnp.int32), jax.ShapeDtypeStruct((16,), jnp.int32)],
        in_specs=[smem] * 3,
        out_specs=[smem] * 2,
        scratch_shapes=[pltpu.SMEM((256,), jnp.int32)],
        cost_estimate=cost(0, 4096),
        name="order",
    )(ids, refreshed, slot_block)


def prepare_kernel(tokens, slot_block, out, ids, sem, id_sem):
    where = whereabouts()
    load_ids = pltpu.make_async_copy(slot_block, ids, id_sem)
    load_ids.start()
    loads = []
    for m in range(2):
        rows = pl.ds(pl.multiple_of((2 * m + where[1]) * ROWS, ROWS), ROWS)
        for i in range(4):
            k = 4 * m + i
            loads.append(pltpu.make_async_copy(tokens.at[rows], out.at[k, pl.ds(0, ROWS)], sem.at[k]))
    for load in loads:
        load.start()
    row = lax.broadcasted_iota(jnp.int32, (IDS, 128), 0)
    lane = lax.broadcasted_iota(jnp.int32, (IDS, 128), 1)
    tile = jnp.zeros((IDS, 128), jnp.int32)
    load_ids.wait()
    for p in range(8):
        tile = jnp.where((row == 0) & (lane == p), ids[p], tile)
    tile = tile.astype(F32).astype(BF)
    for k in range(8):
        out[k, ROWS:] = tile
    for load in loads:
        load.wait()


def prepare(tokens, slot_block):
    hbm = pl.BlockSpec(memory_space=pl.ANY)
    return pl.pallas_call(
        prepare_kernel,
        out_shape=jax.ShapeDtypeStruct((8, ROWS + IDS, 128), BF),
        in_specs=[hbm, hbm],
        out_specs=pl.BlockSpec(memory_space=pltpu.VMEM),
        scratch_shapes=[pltpu.SMEM((8,), jnp.int32), pltpu.SemaphoreType.DMA((8,)), pltpu.SemaphoreType.DMA],
        compiler_params=params(8),
        cost_estimate=cost(0, MIB),
        name="prepare",
    )(*in_hbm(tokens, slot_block))


def weights_kernel(weight, upstream, w, up, sem):
    where = whereabouts()
    cols = pl.ds(pl.multiple_of(where[1] * 256, 256), 256)
    loads = [pltpu.make_async_copy(weight.at[:, cols], w, sem.at[2])]
    for k in range(2):
        rows = pl.ds(pl.multiple_of(where[2 * k] * ROWS, ROWS), ROWS)
        loads.append(pltpu.make_async_copy(upstream.at[rows, cols], up.at[k], sem.at[k]))
    for load in loads:
        load.start()
    for load in loads:
        load.wait()


def half_of_weights(in_weight, upstream):
    vmem = pl.BlockSpec(memory_space=pltpu.VMEM)
    hbm = pl.BlockSpec(memory_space=pl.ANY)
    return pl.pallas_call(
        weights_kernel,
        out_shape=[jax.ShapeDtypeStruct((4096, 256), BF), jax.ShapeDtypeStruct((2, ROWS, 256), BF)],
        in_specs=[hbm, hbm],
        out_specs=[vmem, vmem],
        scratch_shapes=[pltpu.SemaphoreType.DMA((3,))],
        compiler_params=params(4),
        cost_estimate=cost(0, 5 * MIB),
        name="weights",
    )(*in_hbm(in_weight, upstream))


def piece(group, m, i):
    return group[0][m * 4 + i, :ROWS] if len(group) == 1 else group[m][i, :ROWS]


def group_product(group, w, core, across, flip):
    tokens = jnp.concatenate([piece(group, j // 4, j % 4) for j in range(8)], axis=1)
    weights = []
    for j in range(8):
        row = jnp.where(core == 0, across * 1024 + j % 4 * 128, j % 4 * 1024 + across * 128) + ((j // 4) ^ flip) * 512
        weights.append(w[pl.ds(pl.multiple_of(row, 128), 128)])
    return nn(tokens, jnp.concatenate(weights, axis=0))


def first_kernel(first, w, acc):
    where = whereabouts()
    acc[...] = group_product([first], w, where[1], where[6], where[5])


def first_of_own(first, w):
    vmem = pl.BlockSpec(memory_space=pltpu.VMEM)
    return pl.pallas_call(
        first_kernel,
        out_shape=jax.ShapeDtypeStruct((ROWS, 256), F32),
        in_specs=[vmem] * 2,
        out_specs=vmem,
        compiler_params=params(8),
        cost_estimate=cost(2 * ROWS * 1024 * 256, 2 * MIB),
        name="first",
    )(first, w)


def own_kernel(before, below, above, w, acc):
    where = whereabouts()
    total = before[...]
    for ref, step in ((below, STEPS[1]), (above, STEPS[2])):
        total = total + group_product([ref], w, where[1], (where[6] + step) & 3, where[5])
    acc[...] = total


def more_of_own(before, below, above, w):
    vmem = pl.BlockSpec(memory_space=pltpu.VMEM)
    return pl.pallas_call(
        own_kernel,
        out_shape=jax.ShapeDtypeStruct((ROWS, 256), F32),
        in_specs=[vmem] * 4,
        out_specs=vmem,
        compiler_params=params(8),
        cost_estimate=cost(2 * ROWS * 2048 * 256, 2 * MIB),
        name="own",
    )(before, below, above, w)


def other_kernel(*refs):
    where = whereabouts()
    w, acc = refs[5:]
    total = None
    for group, step in zip([refs[0:1], refs[1:3], refs[3:5]], STEPS):
        part = group_product(group, w, 1 - where[1], (where[7] + step) & 3, where[5])
        total = part if total is None else total + part
    acc[...] = total


def forward_of_other(other, w):
    vmem = pl.BlockSpec(memory_space=pltpu.VMEM)
    return pl.pallas_call(
        other_kernel,
        out_shape=jax.ShapeDtypeStruct((ROWS, 256), F32),
        in_specs=[vmem] * 6,
        out_specs=vmem,
        compiler_params=params(8),
        cost_estimate=cost(2 * ROWS * 3072 * 256, 2 * MIB),
        name="other",
    )(*other, w)


def slope_of(group, before, up, w, core, across, flip):
    pre = before + group_product(group, w, core, across, flip)
    delta = (up.astype(F32) * gelu_slope(pre)).astype(BF)
    return nt(unit(256, BF), delta).astype(BF)


def slope_kernel(before, low, high, w, up, out):
    where = whereabouts()
    across = (where[6] + STEPS[3]) & 3
    out[...] = slope_of([low, high], before[...], up[0], w, where[1], across, where[5])


def own_slope(before, far, w, up):
    vmem = pl.BlockSpec(memory_space=pltpu.VMEM)
    return pl.pallas_call(
        slope_kernel,
        out_shape=jax.ShapeDtypeStruct((256, ROWS), BF),
        in_specs=[vmem] * 5,
        out_specs=vmem,
        compiler_params=params(8),
        cost_estimate=cost(2 * ROWS * 1024 * 256, 2 * MIB),
        name="slope",
    )(before, *far, w, up)


def gradient_kernel(own_delta, before, *refs):
    where = whereabouts()
    own = [refs[0:1], refs[1:2], refs[2:3], refs[3:5]]
    other = [refs[5:6], refs[6:8], refs[8:10], refs[10:12]]
    w, up, out, ids_out, ids, made, sem, ids_sem = refs[12:]
    core, flip = where[1], where[5]
    for k, group in enumerate(own):
        for j in range(8):
            ref, at = (group[0], j) if len(group) == 1 else (group[j // 4], j % 4)
            rows = ref[at, ROWS:].astype(F32).astype(jnp.int32)
            ids[k * 8 + j : k * 8 + j + 1] = rows[:1]
    sends = [pltpu.make_async_copy(ids, ids_out, ids_sem)]
    sends[0].start()
    across = (where[7] + STEPS[3]) & 3
    other_delta = slope_of(other[3], before[...], up[1], w, 1 - core, across, flip)
    delta = jnp.concatenate([own_delta[...], other_delta], axis=1)
    for k in range(4):
        mine = (where[6] + STEPS[k]) & 3
        tokens, places = [], []
        for j in range(8):
            m, n = j % 2, j // 2
            theirs = (where[7] + STEPS[n]) & 3
            tokens.append(jnp.concatenate([piece(own[k], m, theirs), piece(other[n], m, mine)], axis=0))
            z, x = jnp.where(core == 0, mine, theirs), jnp.where(core == 0, theirs, mine)
            places.append((x * 16, z * 2 + (m ^ flip)))
        part = (nn(delta, jnp.concatenate(tokens, axis=1)) / 1536.0).astype(BF)
        for j, (quarter, row) in enumerate(places):
            made[k, j] = part[:, j * 128 : (j + 1) * 128].reshape(16, 16, 128)
            sends.append(pltpu.make_async_copy(made.at[k, j], out.at[pl.ds(quarter, 16), row], sem.at[k, j]))
            sends[-1].start()
    for send in sends:
        send.wait()


def gradient_pieces(own_delta, before, own, other, w, up):
    vmem = pl.BlockSpec(memory_space=pltpu.VMEM)
    return pl.pallas_call(
        gradient_kernel,
        out_shape=[pltpu.HBM((64, 8, 16, 128), BF), pltpu.HBM((32, 128), jnp.int32)],
        in_specs=[vmem] * 16,
        out_specs=[pl.BlockSpec(memory_space=pltpu.HBM)] * 2,
        scratch_shapes=[
            pltpu.VMEM((32, 128), jnp.int32),
            pltpu.VMEM((4, 8, 16, 16, 128), BF),
            pltpu.SemaphoreType.DMA((4, 8)),
            pltpu.SemaphoreType.DMA,
        ],
        compiler_params=params(10),
        cost_estimate=cost(3 * 768 * 4096 * 256, 12 * MIB),
        name="gradient",
    )(own_delta, before, *own, *other, w, up)


def route_kernel(source, pieces, out):
    def some(n, c):
        for k in range(16):
            at = source[n * 16 + k]
            out[n * 16 + k] = (pieces[at].astype(F32) + pieces[at + 256].astype(F32)).astype(BF)
        return c

    lax.fori_loop(0, 16, some, 0)


def route(source, pieces):
    vmem = pl.BlockSpec(memory_space=pltpu.VMEM)
    out = pl.pallas_call(
        route_kernel,
        out_shape=jax.ShapeDtypeStruct((256, 16, 128), BF),
        in_specs=[pl.BlockSpec(memory_space=pltpu.SMEM), vmem],
        out_specs=vmem,
        compiler_params=params(16),
        cost_estimate=cost(0, 3 * MIB),
        name="route",
    )(source, pieces.reshape(512, 16, 128))
    return out.reshape(64, 4, 16, 128)


def collect(core, mine, theirs, slot, grad_t):
    for quarter in range(4):
        cols = slice(quarter * 128, (quarter + 1) * 128)
        part = slice(quarter * 16, (quarter + 1) * 16)
        grad_t[pl.ds(pl.multiple_of(core * 256, 256), 256), cols] = mine[part, slot].reshape(256, 128)
        grad_t[pl.ds(pl.multiple_of(256 - core * 256, 256), 256), cols] = theirs[part, slot].reshape(256, 128)


def hand_out(where, second, keep, send, slot, full):
    full[...] = second
    mean_square = jnp.sum(second * second, keepdims=True) * (1.0 / (BLOCK * BLOCK))
    scale = lax.rsqrt(mean_square + floor_eps)
    keep[slot] = (full[pl.ds(pl.multiple_of(where[0] * 128, 128), 128)] * scale).astype(BF)
    send[slot] = (full[pl.ds(pl.multiple_of(where[3] * 128, 128), 128)] * scale).astype(BF)


def fetch_kernel(slot_at, roots, statistics, pairs, statistic, sem):
    where = whereabouts()
    loads = [pltpu.make_async_copy(roots.at[slot_at[where[4] + k]], pairs.at[k], sem.at[k]) for k in range(4)]
    loads.append(pltpu.make_async_copy(statistics.at[slot_at[where[4]]], statistic, sem.at[4]))
    for load in loads:
        load.start()
    for load in loads:
        load.wait()


def fetch(slot_at, roots, statistics):
    smem = pl.BlockSpec(memory_space=pltpu.SMEM)
    vmem = pl.BlockSpec(memory_space=pltpu.VMEM)
    hbm = pl.BlockSpec(memory_space=pl.ANY)
    return pl.pallas_call(
        fetch_kernel,
        out_shape=[jax.ShapeDtypeStruct((4, 2, BLOCK, BLOCK), BF), jax.ShapeDtypeStruct((2, BLOCK, BLOCK), BF)],
        in_specs=[smem, hbm, hbm],
        out_specs=[vmem, vmem],
        scratch_shapes=[pltpu.SemaphoreType.DMA((5,))],
        compiler_params=params(8),
        cost_estimate=cost(0, 9 * MIB),
        name="fetch",
    )(slot_at, *in_hbm(roots, statistics))


def half_block(ref, slot):
    return jnp.concatenate([ref[q * 16 : (q + 1) * 16, slot].reshape(256, 128) for q in range(4)], axis=1)


def half_kernel(mine, pairs, firsts):
    for k in range(3):
        firsts[k] = nt(pairs[k + 1, 0], half_block(mine, k + 1)).astype(BF)


def half_of_firsts(mine, pairs):
    vmem = pl.BlockSpec(memory_space=pltpu.VMEM)
    return pl.pallas_call(
        half_kernel,
        out_shape=jax.ShapeDtypeStruct((3, BLOCK, 256), BF),
        in_specs=[vmem, vmem],
        out_specs=vmem,
        compiler_params=params(12),
        cost_estimate=cost(3 * BLOCK**3, 2 * MIB),
        name="half",
    )(mine, pairs)


def stored_kernel(firsts, theirs, pairs, keep, send, full):
    where = whereabouts()
    mine = pl.ds(pl.multiple_of(where[1] * 256, 256), 256)
    rest = pl.ds(pl.multiple_of(256 - where[1] * 256, 256), 256)
    others = [nt(pairs[k + 1, 0], half_block(theirs, k + 1)).astype(BF) for k in range(3)]
    seconds = [nn(firsts[k], pairs[k + 1, 1, mine]) + nn(others[k], pairs[k + 1, 1, rest]) for k in range(3)]
    for k in range(3):
        hand_out(where, seconds[k], keep, send, k, full.at[k])


def stored_slots(firsts, theirs, pairs):
    vmem = pl.BlockSpec(memory_space=pltpu.VMEM)
    return pl.pallas_call(
        stored_kernel,
        out_shape=[jax.ShapeDtypeStruct((3, 128, BLOCK), BF)] * 2,
        in_specs=[vmem] * 3,
        out_specs=[vmem, vmem],
        scratch_shapes=[pltpu.VMEM((3, BLOCK, BLOCK), F32)],
        compiler_params=params(20),
        cost_estimate=cost(9 * BLOCK**3, 4 * MIB),
        name="stored",
    )(firsts, theirs, pairs)


def symmetric_product(x, y):
    top = nn(x[:256], y)
    corner = nn(x[256:], y[:, 256:])
    return jnp.concatenate([top, jnp.concatenate([top[:, 256:].T, corner], axis=1)], axis=0)


def product(a, b):
    (c, x), (d, y) = a, b
    xy = symmetric_product(x.astype(BF), y.astype(BF))
    return c * d, xy + (c * y + d * x if c and d else d * x if d else c * y)


def square(a):
    c, x = a
    x_rounded = x.astype(BF)
    return c * c, symmetric_product(x_rounded, x_rounded) + (2.0 * c) * x


def scaled_factor(power):
    return 1.25, -0.25 * power


def inverse_roots(matrices):
    eye = unit(BLOCK, F32)
    powers = [matrix / jnp.sum(matrix * eye, keepdims=True) for matrix in matrices]
    results = [scaled_factor(power) for power in powers]
    factors = results
    for sweep in range(2):
        fourths = [square(factor) for factor in factors]
        fourths = [square(fourth) for fourth in fourths]
        powers = [product(fourth, (0.0, power))[1] for fourth, power in zip(fourths, powers)]
        factors = [scaled_factor(power) for power in powers]
        results = [product(result, factor) for result, factor in zip(results, factors)]
    return [(c * eye + x).astype(BF) for c, x in results]


def refresh_kernel(slot_at, mine, theirs, pairs, statistic, stored, keep, send, out, grad_t, full, pair, sem):
    where = whereabouts()
    copies = [
        pltpu.make_async_copy(stored.at[k], out.at[slot_at[where[4] + k + 1]], sem.at[k]) for k in range(3)
    ]
    for copy in copies:
        copy.start()
    collect(where[1], mine, theirs, 0, grad_t)
    g_t = grad_t[...]
    is_fresh = slot_at[8] > where[4] // 4

    @pl.when(jnp.logical_not(is_fresh))
    def _():
        pair[...] = pairs[0]

    @pl.when(is_fresh)
    def _():
        eye = unit(BLOCK, F32)
        g = nt(unit(BLOCK, BF), g_t).astype(BF)
        outers = [nt(g, g), nt(g_t, g_t)]
        matrices = [decay * statistic[k].astype(F32) + outers[k] + jitter * eye for k in range(2)]
        pair[0], pair[1] = inverse_roots(matrices)

    first = nt(pair[0], g_t).astype(BF)
    hand_out(where, nn(first, pair[1]), keep, send, 0, full)
    for copy in copies:
        copy.wait()


def refresh(slot_at, mine, theirs, pairs, statistic, stored):
    smem = pl.BlockSpec(memory_space=pltpu.SMEM)
    vmem = pl.BlockSpec(memory_space=pltpu.VMEM)
    return pl.pallas_call(
        refresh_kernel,
        out_shape=[jax.ShapeDtypeStruct((1, 128, BLOCK), BF)] * 2 + [pltpu.HBM((8, 128, BLOCK), BF)],
        in_specs=[smem] + [vmem] * 5,
        out_specs=[vmem, vmem, pl.BlockSpec(memory_space=pltpu.HBM)],
        scratch_shapes=[
            pltpu.VMEM((BLOCK, BLOCK), BF),
            pltpu.VMEM((BLOCK, BLOCK), F32),
            pltpu.VMEM((2, BLOCK, BLOCK), BF),
            pltpu.SemaphoreType.DMA((3,)),
        ],
        compiler_params=params(32),
        cost_estimate=cost(42 * BLOCK**3, 4 * MIB),
        name="refresh",
    )(slot_at, mine, theirs, pairs, statistic, stored)


def copy_all(copies):
    for copy in copies:
        copy.start()
    for copy in copies:
        copy.wait()


def assemble_kernel(slot_at, before, fresh, theirs, out, sem):
    here = whereabouts()[4]
    copies = [pltpu.make_async_copy(fresh.at[0], out.at[slot_at[here]], sem.at[3])]
    for k in range(3):
        copies.append(pltpu.make_async_copy(theirs.at[k], out.at[slot_at[4 - here + k + 1]], sem.at[k]))
    for copy in copies:
        copy.start()
    for copy in copies:
        copy.wait()


def assemble(slot_at, *parts):
    hbm = pl.BlockSpec(memory_space=pl.ANY)
    return pl.pallas_call(
        assemble_kernel,
        out_shape=pltpu.HBM((8, 128, BLOCK), BF),
        in_specs=[pl.BlockSpec(memory_space=pltpu.SMEM)] + [hbm] * 3,
        out_specs=pl.BlockSpec(memory_space=pltpu.HBM),
        scratch_shapes=[pltpu.SemaphoreType.DMA((4,))],
        input_output_aliases={1: 0},
        compiler_params=params(4),
        cost_estimate=cost(0, 2 * MIB),
        name="assemble",
    )(slot_at, *parts)


def shards(tokens, in_weight, upstream, slot_block, refreshed, statistics, roots):
    both = ("grp", "dev")

    first = prepare(tokens, slot_block)
    first = lax.all_to_all(first, both, 0, 0, tiled=True, axis_index_groups=STAGE1)
    w, up = half_of_weights(in_weight, upstream)
    below = lax.ppermute(first, both, UP)
    above = lax.ppermute(first, both, DOWN)
    acc = first_of_own(first, w)
    shared, acc = lax.optimization_barrier((first, acc))
    own = [first, below, above]
    halves = [below[:4], below[4:], above[:4], above[4:]]
    own += [lax.ppermute(halves[0], both, UP), lax.ppermute(halves[3], both, DOWN)]
    acc = more_of_own(acc, below, above, w)
    halves[2:], acc = lax.optimization_barrier((halves[2:], acc))
    other = [lax.ppermute(part, "grp", CORE) for part in (shared, *halves)]
    acc, own[3:], other[1:3] = lax.optimization_barrier((acc, own[3:], other[1:3]))
    other_acc = forward_of_other(other[:5], w)
    other += [lax.ppermute(part, "grp", CORE) for part in own[3:]]
    own_delta = own_slope(acc, own[3:], w, up)
    pieces, all_ids = gradient_pieces(own_delta, other_acc, own, other, w, up)
    pieces = lax.all_to_all(pieces, both, 0, 0, tiled=True, axis_index_groups=SAME_CORE)
    source, slot_at = slot_order(all_ids, refreshed, slot_block)
    pairs, statistic = fetch(slot_at, roots, statistics)
    source, pairs, statistic = lax.optimization_barrier((source, pairs, statistic))
    pieces = route(source, pieces)
    mine = lax.all_to_all(pieces, both, 0, 0, tiled=True, axis_index_groups=SAME_CORE)
    theirs = lax.ppermute(mine, "grp", CORE)

    keep, send = stored_slots(half_of_firsts(mine, pairs), theirs, pairs)
    other_keep = lax.ppermute(send, "grp", CHIP)
    mine, theirs, keep = lax.optimization_barrier((mine, theirs, keep))
    fresh_keep, fresh_send, update = refresh(slot_at, mine, theirs, pairs, statistic, keep)
    fresh_other = lax.ppermute(fresh_send, "grp", CHIP)
    update = assemble(slot_at, update, fresh_keep, other_keep)
    return lax.dynamic_update_slice_in_dim(update, fresh_other, slot_at[4 - 4 * (lax.axis_index("grp") // 2)], 0)


def solution(mesh):
    return jax.shard_map(
        shards,
        mesh=mesh,
        in_specs=(
            P(None, "dev"),
            P(None, "dev"),
            P(None, "dev"),
            P("dev"),
            P(),
            P("dev", None, None, None),
            P("dev", None, None, None),
        ),
        out_specs=P("dev", "grp", None),
        check_vma=False,
    )
```
